32 devices in a mesh: lon: 16 (over z, x, core), lat: 2 (over y).
Axes of the slice: x: 2, y: 2, z: 4, core: 2. Of those that a mesh axis runs over, the one named last changes fastest.
Arguments:
- states: bfloat16 [8, 256, 128, 128], P(None, 'lon', 'lat'), may hold values from -6 to 6
- targets: bfloat16 [8, 256, 128, 128], P(None, 'lon', 'lat'), may hold values from -6 to 6
- sea_temp: bfloat16 [8, 256, 128], P(None, 'lon', 'lat'), may hold values from -6 to 6
- ocean: int32 [8, 256, 128], P(None, 'lon', 'lat'), may hold values from 0 to 1
- valid: int32 [8, 256, 128], P(None, 'lon', 'lat'), may hold values from 0 to 1
- order: int32 [8], replicated, may hold values from 0 to 7, each once
- w_enc: float32 [2, 9, 128, 256], replicated, may hold values from -0.1875 to 0.1875
- w_mid: float32 [2, 256, 256], replicated, may hold values from -0.375 to 0.375
- w_dec: float32 [2, 256, 128], replicated, may hold values from -0.375 to 0.375
- biases: float32 [2, 896], replicated, may hold values from -3 to 3
- mom_enc: float32 [2, 9, 128, 256], replicated, may hold values from -0.625 to 0.625
- mom_mid: float32 [2, 256, 256], replicated, may hold values from -0.625 to 0.625
- mom_dec: float32 [2, 256, 128], replicated, may hold values from -0.625 to 0.625
- mom_bias: float32 [2, 896], replicated, may hold values from -0.625 to 0.625
- avg_enc: float32 [2, 9, 128, 256], replicated, may hold values from -0.1875 to 0.1875
- avg_mid: float32 [2, 256, 256], replicated, may hold values from -0.375 to 0.375
- avg_dec: float32 [2, 256, 128], replicated, may hold values from -0.375 to 0.375
- avg_bias: float32 [2, 896], replicated, may hold values from -3 to 3
Outputs:
- loss_sum: float32 [], replicated
- weight_sum: float32 [], replicated
- new_enc: float32 [2, 9, 128, 256], replicated
- new_mid: float32 [2, 256, 256], replicated
- new_dec: float32 [2, 256, 128], replicated
- new_bias: float32 [2, 896], replicated
- next_mom_enc: float32 [2, 9, 128, 256], replicated
- next_mom_mid: float32 [2, 256, 256], replicated
- next_mom_dec: float32 [2, 256, 128], replicated
- next_mom_bias: float32 [2, 896], replicated
- next_avg_enc: float32 [2, 9, 128, 256], replicated
- next_avg_mid: float32 [2, 256, 256], replicated
- next_avg_dec: float32 [2, 256, 128], replicated
- next_avg_bias: float32 [2, 896], replicated
- copy_enc: bfloat16 [2, 9, 128, 256], replicated
- copy_mid: bfloat16 [2, 256, 256], replicated
- copy_dec: bfloat16 [2, 256, 128], replicated
- copy_bias: bfloat16 [2, 896], replicated
The draws below stay inside these ranges and needn't reach their ends.
Inputs may be any that keep to these rules, and one draw needn't show every extreme that they name: order names every snapshot once.
All inputs are finite; a program needn't handle non-finite values.
Results may differ from the reference program's by a relative error of at most 0.0024.
The reference program's roundings to bfloat16 on the way count: a program that leaves them out, or rounds other values in their place, can miss the bound.
Values may be sent and summed in bfloat16 or wider, within the bound.
No kernel may reach another device: no remote copies, remote signals or barrier semaphores. Data moves between devices by JAX's collectives and lax.ppermute only.
A program may use at most 448 MiB of HBM per device.

```python
import math
import jax
import jax.numpy as jnp
from jax import lax

NLON = 256
NLAT = 128
HID = 256
MW = 86
NDEG = 86
LAYERS = 2
POOL = 8
C = 128


def draw_ocean(key, part):
    key = jax.random.fold_in(key, 11)
    first, second = jax.random.split(key)
    levels = jax.random.randint(first, (POOL, NLON // 8, NLAT // 16), 1, 11)
    levels = jnp.repeat(jnp.repeat(levels, 8, axis=1), 16, axis=2)
    rolls = jax.random.randint(second, (POOL, NLON, NLAT), 0, 10)
    return (rolls < levels).astype(jnp.int32)


def draw_valid(key, part):
    key = jax.random.fold_in(key, 23)
    rolls = jax.random.randint(key, (POOL, NLON, NLAT), 0, 10)
    rising = 2 + 8 * jnp.arange(NLAT) // NLAT
    return (rolls < rising[None, None, :]).astype(jnp.int32)


def block_scale(own_key, extent, shards, least, top_value):
    def one(position, blocks):
        steps = jax.random.uniform(jax.random.fold_in(jax.random.fold_in(own_key, 6), position), (blocks,), jnp.float32, least / len(shards), top_value / len(shards))
        return jnp.repeat(jnp.exp(steps), extent[position] // blocks).reshape((-1,) + (1,) * (len(extent) - position - 1))

    level = one(*shards[0])
    for cut in shards[1:]:
        level = level * one(*cut)
    return level


def gaussian(own_key, dims, width, bound, cuts=(), dtype=jnp.bfloat16):
    values = width * jax.random.normal(own_key, dims, jnp.float32)
    if cuts:
        values = values * block_scale(own_key, dims, cuts, -0.22, 0.18)
    return jnp.clip(values, -bound, bound).astype(dtype)


def setup_inputs(seed: int = 0) -> dict:
    key_list = jax.random.split(jax.random.key(seed), 19)
    states = gaussian(key_list[0], (POOL, NLON, NLAT, C), 1.0, 6.0, ((1, 16), (2, 2)))
    targets = gaussian(key_list[1], (POOL, NLON, NLAT, C), 1.0, 6.0, ((1, 16), (2, 2)))
    sea_temp = gaussian(key_list[2], (POOL, NLON, NLAT), 1.0, 6.0, ((1, 16), (2, 2)))
    ocean = draw_ocean(jax.random.fold_in(key_list[18], 71), 0)
    valid = draw_valid(jax.random.fold_in(key_list[18], 71), 0)
    order = jax.random.permutation(key_list[5], POOL).astype(jnp.int32)
    w_enc = gaussian(key_list[6], (LAYERS, 9, C, HID), (9 * C) ** -0.5, 0.1875, (), jnp.float32)
    w_mid = gaussian(key_list[7], (LAYERS, HID, HID), HID ** -0.5, 0.375, (), jnp.float32)
    w_dec = gaussian(key_list[8], (LAYERS, HID, C), HID ** -0.5, 0.375, (), jnp.float32)
    biases = gaussian(key_list[9], (LAYERS, 3 * HID + C), 0.5, 3.0, (), jnp.float32)
    mom_enc = gaussian(key_list[10], (LAYERS, 9, C, HID), (50 / (POOL * NLON * NLAT) ** 0.5), 0.625, (), jnp.float32)
    mom_mid = gaussian(key_list[11], (LAYERS, HID, HID), (50 / (POOL * NLON * NLAT) ** 0.5), 0.625, (), jnp.float32)
    mom_dec = gaussian(key_list[12], (LAYERS, HID, C), (50 / (POOL * NLON * NLAT) ** 0.5), 0.625, (), jnp.float32)
    mom_bias = gaussian(key_list[13], (LAYERS, 3 * HID + C), (50 / (POOL * NLON * NLAT) ** 0.5), 0.625, (), jnp.float32)
    avg_enc = gaussian(key_list[14], (LAYERS, 9, C, HID), (9 * C) ** -0.5, 0.1875, (), jnp.float32)
    avg_mid = gaussian(key_list[15], (LAYERS, HID, HID), HID ** -0.5, 0.375, (), jnp.float32)
    avg_dec = gaussian(key_list[16], (LAYERS, HID, C), HID ** -0.5, 0.375, (), jnp.float32)
    avg_bias = gaussian(key_list[17], (LAYERS, 3 * HID + C), 0.5, 3.0, (), jnp.float32)
    return {"states": states, "targets": targets, "sea_temp": sea_temp, "ocean": ocean, "valid": valid, "order": order, "w_enc": w_enc, "w_mid": w_mid, "w_dec": w_dec, "biases": biases, "mom_enc": mom_enc, "mom_mid": mom_mid, "mom_dec": mom_dec, "mom_bias": mom_bias, "avg_enc": avg_enc, "avg_mid": avg_mid, "avg_dec": avg_dec, "avg_bias": avg_bias}


@jax.custom_vjp
def low(v):
    return lax.optimization_barrier(v.astype(jnp.bfloat16)).astype(jnp.float32)

@jax.custom_vjp
def low_back(v):
    return v

def low_keep(v):
    return (low(v), None)

def low_pass(kept, grad):
    return (grad,)

def back_keep(v):
    return (v, None)

def back_low(kept, grad):
    return (low(grad),)
low.defvjp(low_keep, low_pass)
low_back.defvjp(back_keep, back_low)
HIGH = lax.Precision.HIGHEST
MOMENTUM = 0.9
AVERAGE = 0.99
RATE_BASE = 0.0006

def tables(nlon, nlat):
    coeffs = jnp.arange(2 * MW)
    wave = jnp.where(coeffs < MW, coeffs, coeffs - MW + 1).astype(jnp.float32)
    places = jnp.arange(nlon).astype(jnp.float32)
    angle = 2.0 * math.pi * wave[:, None] * places[None, :] / nlon
    fourier = jnp.where((coeffs < MW)[:, None], jnp.cos(angle), jnp.sin(angle)) * math.sqrt(2.0 / nlon)
    phase = ((jnp.arange(nlat).astype(jnp.float32) + 0.5) / nlat - 0.5) * math.pi
    sine = jnp.sin(phase)
    quad = jnp.cos(phase) * math.pi / nlat
    polys = [jnp.ones_like(sine), sine]
    for degree in range(1, NDEG - 1):
        polys.append(((2 * degree + 1) * sine * polys[-1] - degree * polys[-2]) / (degree + 1))
    stacked = jnp.stack(polys[:NDEG])
    degrees = jnp.arange(NDEG).astype(jnp.float32)
    legendre = jnp.sqrt((2 * degrees + 1) / 2)[:, None] * jnp.sqrt(quad)[None, :] * stacked
    damping = 1.5 * (1.0 - 2.0 * degrees * (degrees + 1) / (NDEG * (NDEG + 1)))
    filters = damping[None, :] * (1.0 - 0.5 * wave / MW)[:, None]
    return (fourier, legendre, filters)

def spectral(field, tabs):
    fourier, legendre, filters = tabs
    coeff = jnp.einsum('kx,xjc->kjc', fourier, field, precision=HIGH)
    spec = jnp.einsum('nj,kjc->knc', legendre, coeff, precision=HIGH) * filters[:, :, None]
    back = jnp.einsum('nj,knc->kjc', legendre, spec, precision=HIGH)
    return jnp.einsum('kx,kjc->xjc', fourier, back, precision=HIGH)

def neighbours(field):
    wrapped = jnp.concatenate([field[-1:], field, field[:1]], axis=0)
    padded = jnp.pad(wrapped, ((0, 0), (1, 1), (0, 0)))
    parts = [padded[row_off:row_off + NLON, col_off:col_off + NLAT] for row_off in range(3) for col_off in range(3)]
    return jnp.stack(parts, axis=2).reshape(NLON * NLAT, 9 * field.shape[-1])

def snapshot_loss(params, state, target, sea, weight, tabs):
    w_enc, w_mid, w_dec, biases = params
    for layer_id in range(LAYERS):
        vec = biases[layer_id]
        moved = state + spectral(state, tabs)
        patches = neighbours(low(moved))
        pre1 = jnp.dot(patches, low(w_enc[layer_id]).reshape(9 * C, HID), precision=HIGH)
        pre1 = low_back(pre1 + sea.reshape(-1, 1) * vec[HID:2 * HID] + vec[:HID])
        active1 = low(jax.nn.gelu(pre1, approximate=True))
        pre2 = low_back(jnp.dot(active1, low(w_mid[layer_id]), precision=HIGH) + vec[2 * HID:3 * HID])
        active2 = low(jax.nn.gelu(pre2, approximate=True))
        output = low_back(jnp.dot(active2, low(w_dec[layer_id]), precision=HIGH) + vec[3 * HID:])
        state = moved + output.reshape(NLON, NLAT, C)
    diff = state - target
    return jnp.sum(weight[:, :, None] * diff * diff)

def reference(states, targets, sea_temp, ocean, valid, order, w_enc, w_mid, w_dec, biases, mom_enc, mom_mid, mom_dec, mom_bias, avg_enc, avg_mid, avg_dec, avg_bias):
    tabs = tables(NLON, NLAT)
    phase = ((jnp.arange(NLAT).astype(jnp.float32) + 0.5) / NLAT - 0.5) * math.pi
    area = jnp.cos(phase)
    params = (w_enc, w_mid, w_dec, biases)

    def step(carry, pick):
        grads, loss, total = carry
        state = lax.dynamic_index_in_dim(states, pick, 0, keepdims=False).astype(jnp.float32)
        target = lax.dynamic_index_in_dim(targets, pick, 0, keepdims=False).astype(jnp.float32)
        sea = lax.dynamic_index_in_dim(ocean, pick, 0, keepdims=False).astype(jnp.float32) * lax.dynamic_index_in_dim(sea_temp, pick, 0, keepdims=False).astype(jnp.float32)
        weight = lax.dynamic_index_in_dim(valid, pick, 0, keepdims=False).astype(jnp.float32) * area[None, :]
        value, back = jax.vjp(lambda given: snapshot_loss(given, state, target, sea, weight, tabs), params)
        found = back(jnp.ones_like(value))[0]
        grads = jax.tree.map(lambda a, b: a + b, grads, found)
        return ((grads, loss + value, total + jnp.sum(weight)), None)
    zeros = jax.tree.map(jnp.zeros_like, params)
    start = (zeros, jnp.zeros((), jnp.float32), jnp.zeros((), jnp.float32))
    (grads, loss, total), _ = lax.scan(step, start, order)
    rate = RATE_BASE * math.sqrt(POOL * NLON * NLAT)
    news, moms, avgs, copies = ([], [], [], [])
    for weight_now, grad, mom, avg in zip(params, grads, (mom_enc, mom_mid, mom_dec, mom_bias), (avg_enc, avg_mid, avg_dec, avg_bias)):
        scaled = grad / total
        mom_new = MOMENTUM * mom + scaled
        fresh = weight_now - rate * (scaled + MOMENTUM * mom_new)
        news.append(fresh)
        moms.append(mom_new)
        avgs.append(AVERAGE * avg + (1.0 - AVERAGE) * fresh)
        copies.append(fresh.astype(jnp.bfloat16))
    return (loss, total, news[0], news[1], news[2], news[3], moms[0], moms[1], moms[2], moms[3], avgs[0], avgs[1], avgs[2], avgs[3], copies[0], copies[1], copies[2], copies[3])
```

```python
import functools
import math

import jax
import jax.numpy as jnp
import numpy as np
from jax import lax
from jax.experimental import pallas as pl
from jax.experimental.pallas import tpu as pltpu
from jax.sharding import PartitionSpec as P

MW = 86
NDEG = 86
MB = 4


HIGH = lax.Precision.HIGHEST
MOMENTUM = 0.9
AVERAGE = 0.99
RATE_BASE = 0.0006

F32 = jnp.float32
BF16 = jnp.bfloat16
CHUNK = 4
VMEM = 56 * 1024 * 1024
GELU_A = math.sqrt(2.0 / math.pi)
GELU_B = 0.044715


def split_table(table):
    table = np.asarray(table, np.float32)
    high = table.astype(BF16)
    low = (table - high.astype(np.float32)).astype(BF16)
    return np.concatenate([high, low], axis=0)


def host_tables(nlon, nlat, deg):
    kept = np.arange(2 * MW)
    wave = np.where(kept < MW, kept, kept - MW + 1).astype(np.float64)
    angle = 2.0 * np.pi * wave[:, None] * np.arange(nlon)[None, :] / nlon
    fourier = np.where((kept < MW)[:, None], np.cos(angle), np.sin(angle)) * np.sqrt(2.0 / nlon)
    zonal = (fourier * (1.0 - 0.5 * wave / MW)[:, None]).T @ fourier
    phase = ((np.arange(nlat) + 0.5) / nlat - 0.5) * np.pi
    sine, area = np.sin(phase), np.cos(phase)
    polys = [np.ones_like(sine), sine]
    for n in range(1, NDEG - 1):
        polys.append(((2 * n + 1) * sine * polys[-1] - n * polys[-2]) / (n + 1))
    degrees = np.arange(NDEG)
    legendre = np.sqrt((2 * degrees + 1) / 2)[:, None] * np.sqrt(area * np.pi / nlat)[None, :]
    legendre = legendre * np.stack(polys)
    damping = 1.5 * (1.0 - 2.0 * degrees * (degrees + 1) / (NDEG * (NDEG + 1)))
    forward = np.zeros((deg, nlat))
    forward[:NDEG] = legendre
    inverse = np.zeros((nlat, -(-deg // 32) * 32))
    inverse[:, :NDEG] = (legendre * damping[:, None]).T
    return split_table(zonal), split_table(forward), split_table(inverse), area


def mm(a, b):
    return jnp.dot(a, b, preferred_element_type=F32)


def mm_rows(a, b):
    return lax.dot_general(a, b, (((0,), (0,)), ((), ())), preferred_element_type=F32)


def whole(shape):
    return pl.BlockSpec(shape, lambda *_: (0,) * len(shape))


def params():
    return pltpu.CompilerParams(vmem_limit_bytes=VMEM)


def legendre_kernel(x_ref, l_ref, o_ref, tmp):
    lon_t = x_ref.shape[2]
    deg = l_ref.shape[0] // 2
    chans = x_ref.shape[-1]
    for base in range(0, lon_t, 4):
        cols = [
            jnp.concatenate([x_ref[h, 0, base + i] for h in range(x_ref.shape[0])], axis=0)
            for i in range(4)
        ]
        r = mm(l_ref[...], jnp.concatenate(cols, axis=1))
        r = r[:deg] + r[deg:]
        for i in range(4):
            tmp[:, base + i, :] = r[:, i * chans : (i + 1) * chans]
    o_ref[...] = tmp[...].astype(BF16).reshape(o_ref.shape)


def legendre_call(fields, table):
    hemis, snaps, lon_t, lat_t, chans = fields.shape
    deg = table.shape[0] // 2
    parts = 8
    return pl.pallas_call(
        legendre_kernel,
        grid=(snaps,),
        in_specs=[
            pl.BlockSpec((hemis, 1, lon_t, lat_t, chans), lambda s: (0, s, 0, 0, 0)),
            whole(table.shape),
        ],
        out_specs=pl.BlockSpec((parts, deg // parts, lon_t, chans), lambda s: (s, 0, 0, 0)),
        out_shape=jax.ShapeDtypeStruct((snaps * parts, deg // parts, lon_t, chans), BF16),
        scratch_shapes=[pltpu.VMEM((deg, lon_t, chans), F32)],
        compiler_params=params(),
        name="legendre",
    )(fields, table)


def zonal_kernel(x_ref, a_ref, o_ref):
    groups, rows, lon_t, chans = x_ref.shape
    nlon = groups * lon_t
    for base in range(0, rows, 4):
        count = min(4, rows - base)
        cols = [x_ref[:, base + i].reshape(nlon, chans) for i in range(count)]
        r = mm(a_ref[...], jnp.concatenate(cols, axis=1))
        r = (r[:nlon] + r[nlon:]).astype(BF16)
        for i in range(count):
            o_ref[:, base + i] = r[:, i * chans : (i + 1) * chans].reshape(groups, lon_t, chans)


def zonal_call(fields, table):
    return pl.pallas_call(
        zonal_kernel,
        in_specs=[pl.BlockSpec(memory_space=pltpu.VMEM)] * 2,
        out_specs=pl.BlockSpec(memory_space=pltpu.VMEM),
        out_shape=jax.ShapeDtypeStruct(fields.shape, BF16),
        compiler_params=params(),
        name="zonal",
    )(fields, table)


def synthesis_kernel(halo, x_ref, l_ref, o_ref, tmp):
    parts, rows, lon_t, chans = x_ref.shape
    deg = parts * rows
    nlat = l_ref.shape[0] // 2
    half = nlat // 2
    tmp[:deg] = x_ref[...].reshape(deg, lon_t, chans).astype(F32)
    tmp[deg:] = jnp.zeros((tmp.shape[0] - deg, lon_t, chans), F32)
    for base in range(0, lon_t, 4):
        cols = jnp.concatenate([tmp[:, base + i, :] for i in range(4)], axis=1).astype(BF16)
        r = mm(l_ref[...], cols)
        r = r[:nlat] + r[nlat:]
        for i in range(4):
            one = r[:, i * chans : (i + 1) * chans]
            o_ref[0, 0, base + i] = one[:half].astype(BF16)
            o_ref[1, 0, base + i] = one[half:].astype(BF16)
            if halo:
                tmp[0, base + i : base + i + 1, :] = one[half : half + 1]
                tmp[1, base + i : base + i + 1, :] = one[half - 1 : half]
    if halo:
        rest = jnp.zeros((half - lon_t, chans), BF16)
        for h in range(2):
            o_ref[h, 0, lon_t, :lon_t] = tmp[h].astype(BF16)
            o_ref[h, 0, lon_t, lon_t:] = rest


def synthesis_call(coeffs, table, snaps, halo):
    total, rows, lon_t, chans = coeffs.shape
    parts = total // snaps
    nlat = table.shape[0] // 2
    slabs = lon_t + 1 if halo else lon_t
    return pl.pallas_call(
        functools.partial(synthesis_kernel, halo),
        grid=(snaps,),
        in_specs=[
            pl.BlockSpec((parts, rows, lon_t, chans), lambda s: (s, 0, 0, 0)),
            whole(table.shape),
        ],
        out_specs=pl.BlockSpec((2, 1, slabs, nlat // 2, chans), lambda s: (0, s, 0, 0, 0)),
        out_shape=jax.ShapeDtypeStruct((2, snaps, slabs, nlat // 2, chans), BF16),
        scratch_shapes=[pltpu.VMEM((table.shape[1], lon_t, chans), F32)],
        compiler_params=params(),
        name="synthesis",
    )(coeffs, table)


def spectral_fast(low, tabs, halo):
    zonal, forward, inverse = tabs
    snaps, lon_t, lat_t, chans = low.shape
    mine = snaps // 2
    cols = lax.all_to_all(low, "lat", split_axis=0, concat_axis=0, tiled=True)
    spec = legendre_call(cols.reshape(2, mine, lon_t, lat_t, chans), forward)
    spec = lax.all_to_all(spec, "lon", split_axis=0, concat_axis=0, tiled=True)
    spec = zonal_call(spec, zonal)
    spec = lax.all_to_all(spec, "lon", split_axis=0, concat_axis=0, tiled=True)
    back = synthesis_call(spec, inverse, mine, halo)
    back = lax.all_to_all(back, "lat", split_axis=0, concat_axis=0, tiled=True)
    return back.reshape((snaps,) + back.shape[2:])


def gelu_of(x):
    t = jnp.tanh(x * (GELU_A + (GELU_A * GELU_B) * (x * x)))
    return 0.5 * x * (1.0 + t)


def gelu_and_slope(x):
    sq = x * x
    t = jnp.tanh(x * (GELU_A + (GELU_A * GELU_B) * sq))
    cdf = 0.5 + 0.5 * t
    slope = cdf + (0.5 * x) * (1.0 - t * t) * (GELU_A + (3.0 * GELU_A * GELU_B) * sq)
    return x * cdf, slope


def fill_patches(patches, moved, halo_row, lon_lo, lon_hi, masks):
    lon_t, lat_t, chans = moved.shape
    slabs = [lon_lo[:lat_t].astype(F32)] + [moved[i] for i in range(lon_t)] + [lon_hi[:lat_t].astype(F32)]
    ends = [lon_lo[lat_t : lat_t + 1].astype(F32)]
    ends += [halo_row[i : i + 1] for i in range(lon_t)]
    ends += [lon_hi[lat_t : lat_t + 1].astype(F32)]
    place = lax.broadcasted_iota(jnp.int32, (lat_t, chans), 0)
    for i in range(lon_t + 2):
        low_row, high_row = ends[i] * masks[0:1], ends[i] * masks[1:2]
        down = jnp.where(place == 0, low_row, pltpu.roll(slabs[i], 1, 0)).astype(BF16)
        up = jnp.where(place == lat_t - 1, high_row, pltpu.roll(slabs[i], lat_t - 1, 0)).astype(BF16)
        mid = slabs[i].astype(BF16)
        for a in range(3):
            x = i - a
            if 0 <= x < lon_t:
                for b, piece in enumerate((down, mid, up)):
                    k = 3 * a + b
                    patches[x * lat_t : (x + 1) * lat_t, k * chans : (k + 1) * chans] = piece


def assemble(patches, state_ref, s_ref, row_ref, lo_ref, hi_ref, extra_ref, masks_ref, moved):
    lon_t, lat_t, chans = moved.shape
    moved[...] = state_ref[0].astype(F32) + s_ref[0, :lon_t].astype(F32)
    halo_row = row_ref[0].astype(F32) + s_ref[0, lon_t, :lon_t].astype(F32)
    fill_patches(patches, moved, halo_row, lo_ref[0], hi_ref[0], masks_ref[...])
    patches[:, 9 * chans :] = extra_ref[0]


def forward_kernel(
    state_ref, s_ref, row_ref, lo_ref, hi_ref, extra_ref, masks_ref, w1_ref, mid_ref, dec_ref, bias_ref,
    state_out, low_out, pre1_out, pre2_out, patches, moved,
):
    lon_t, lat_t, chans = moved.shape
    hid = mid_ref.shape[0]
    assemble(patches, state_ref, s_ref, row_ref, lo_ref, hi_ref, extra_ref, masks_ref, moved)
    step = 4
    for x in range(0, lon_t, step):
        rows = slice(x * lat_t, (x + step) * lat_t)
        pre1 = mm(patches[rows], w1_ref[...])
        pre1_out[0, rows] = pre1
        active1 = gelu_of(pre1).astype(BF16)
        pre2 = mm(active1, mid_ref[...]) + bias_ref[0:1, :hid]
        pre2_out[0, rows] = pre2
        active2 = gelu_of(pre2).astype(BF16)
        out = mm(active2, dec_ref[...]) + bias_ref[1:2, :chans]
        fresh = moved[x : x + step] + out.reshape(step, lat_t, chans)
        state_out[0, x : x + step] = fresh
        low_out[0, x : x + step] = fresh.astype(BF16)


def grad_layout(chans, hid):
    return (9 * chans, 9 * chans + hid, 9 * chans + hid + chans, 9 * chans + hid + chans + 8)


def add_grads(first, patches, active1, active2, g_out, g_pre2, g_pre1, acc_enc, acc_mid, acc_dec):
    enc = mm_rows(patches[...], g_pre1[...])
    mid = mm_rows(active1[...], g_pre2[...])
    dec = mm_rows(g_out[...], active2[...])

    @pl.when(first)
    def _():
        acc_enc[...] = enc
        acc_mid[...] = mid
        acc_dec[...] = dec

    @pl.when(jnp.logical_not(first))
    def _():
        acc_enc[...] += enc
        acc_mid[...] += mid
        acc_dec[...] += dec


def pack_grads(out, chans, hid, acc_enc, acc_mid, acc_dec, vec2, tail):
    one, two, three, _ = grad_layout(chans, hid)
    out[:one] = acc_enc[:one]
    out[one:two] = acc_mid[...]
    out[two:three] = acc_dec[...]
    out[three : three + 1] = acc_enc[one + 3 : one + 4]
    out[three + 1 : three + 2] = acc_enc[one : one + 1]
    out[three + 2 : three + 3] = vec2
    out[three + 3 : three + 4] = tail
    out[three + 4 :] = jnp.zeros((4, hid), F32)


def turn_kernel(
    state_ref, s_ref, row_ref, lo_ref, hi_ref, extra_ref, masks_ref, w1_ref, mid_ref, dec_ref, bias_ref,
    target_ref, area_ref, w1t_ref, midt_ref, dect_ref,
    gm_out, edge_out, rows_out, grads_out,
    patches, moved, active1, active2, slope1, slope2, g_out, g_pre2, g_pre1, spread, acc_enc, acc_mid, acc_dec, vecs,
):
    lon_t, lat_t, chans = moved.shape
    hid = mid_ref.shape[0]
    first = pl.program_id(0) == 0
    assemble(patches, state_ref, s_ref, row_ref, lo_ref, hi_ref, extra_ref, masks_ref, moved)
    spread[...] = jnp.zeros_like(spread)

    @pl.when(first)
    def _():
        vecs[...] = jnp.zeros_like(vecs)

    step = 4
    for x in range(0, lon_t, step):
        rows = slice(x * lat_t, (x + step) * lat_t)
        pre1 = mm(patches[rows], w1_ref[...])
        a1, d1 = gelu_and_slope(pre1)
        active1[rows] = a1.astype(BF16)
        slope1[rows] = d1
        pre2 = mm(active1[rows], mid_ref[...]) + bias_ref[0:1, :hid]
        a2, d2 = gelu_and_slope(pre2)
        active2[rows] = a2.astype(BF16)
        slope2[rows] = d2
        out = mm(active2[rows], dec_ref[...]) + bias_ref[1:2, :chans]
        fresh = moved[x : x + step] + out.reshape(step, lat_t, chans)
        diff = fresh - target_ref[0, x : x + step].astype(F32)
        valid = jnp.broadcast_to(extra_ref[0, rows, 6:7].astype(F32), (step * lat_t, chans))
        weighted = valid.reshape(step, lat_t, chans) * area_ref[...][None] * diff
        vecs[1:2, :chans] += jnp.sum((weighted * diff).reshape(step * lat_t, chans), 0, keepdims=True)
        grad = 2.0 * weighted
        moved[x : x + step] = grad
        low = grad.reshape(step * lat_t, chans).astype(BF16)
        g_out[rows] = low
        vecs[2:3, :chans] += jnp.sum(low.astype(F32), 0, keepdims=True)
        gp2 = (mm(low, dect_ref[...]) * slope2[rows]).astype(BF16)
        g_pre2[rows] = gp2
        vecs[0:1] += jnp.sum(gp2.astype(F32), 0, keepdims=True)
        gp1 = (mm(gp2, midt_ref[...]) * slope1[rows]).astype(BF16)
        g_pre1[rows] = gp1
        taps = mm(gp1, w1t_ref[...])
        for a in range(3):
            for b in range(3):
                k = 3 * a + b
                spread[b, x + a : x + a + step] += taps[:, k * chans : (k + 1) * chans].reshape(
                    step, lat_t, chans
                )
    place = lax.broadcasted_iota(jnp.int32, (lat_t, chans), 0)
    masks = masks_ref[...]
    for i in range(lon_t + 2):
        down, here, up = spread[0, i], spread[1, i], spread[2, i]
        got = here + jnp.where(place == lat_t - 1, 0.0, pltpu.roll(down, lat_t - 1, 0))
        got = got + jnp.where(place == 0, 0.0, pltpu.roll(up, 1, 0))
        rows_out[0, i : i + 1] = down[0:1] * masks[0:1] + up[lat_t - 1 : lat_t] * masks[1:2]
        if i == 0:
            edge_out[0, 0] = got
        elif i == lon_t + 1:
            edge_out[0, 1] = got
        else:
            gm_out[0, i - 1] = got + moved[i - 1]
    add_grads(first, patches, active1, active2, g_out, g_pre2, g_pre1, acc_enc, acc_mid, acc_dec)

    @pl.when(pl.program_id(0) == pl.num_programs(0) - 1)
    def _():
        tail = jnp.concatenate([vecs[2:3, :chans], vecs[1:2, :chans]], axis=1)
        pack_grads(grads_out, chans, hid, acc_enc, acc_mid, acc_dec, vecs[0:1], tail)


def bottom_kernel(
    state_ref, s_ref, row_ref, lo_ref, hi_ref, extra_ref, masks_ref, pre1_ref, pre2_ref, gm_ref, gs_ref,
    midt_ref, dect_ref, grads_out,
    patches, moved, active1, active2, g_out, g_pre2, g_pre1, acc_enc, acc_mid, acc_dec, vecs,
):
    lon_t, lat_t, chans = moved.shape
    hid = midt_ref.shape[0]
    first = pl.program_id(0) == 0
    assemble(patches, state_ref, s_ref, row_ref, lo_ref, hi_ref, extra_ref, masks_ref, moved)

    @pl.when(first)
    def _():
        vecs[...] = jnp.zeros_like(vecs)

    step = 4
    for x in range(0, lon_t, step):
        rows = slice(x * lat_t, (x + step) * lat_t)
        a1, d1 = gelu_and_slope(pre1_ref[0, rows])
        active1[rows] = a1.astype(BF16)
        a2, d2 = gelu_and_slope(pre2_ref[0, rows])
        active2[rows] = a2.astype(BF16)
        grad = gm_ref[0, x : x + step] + gs_ref[0, x : x + step].astype(F32)
        low = grad.reshape(step * lat_t, chans).astype(BF16)
        g_out[rows] = low
        vecs[2:3, :chans] += jnp.sum(low.astype(F32), 0, keepdims=True)
        gp2 = (mm(low, dect_ref[...]) * d2).astype(BF16)
        g_pre2[rows] = gp2
        vecs[0:1] += jnp.sum(gp2.astype(F32), 0, keepdims=True)
        g_pre1[rows] = (mm(gp2, midt_ref[...]) * d1).astype(BF16)
    add_grads(first, patches, active1, active2, g_out, g_pre2, g_pre1, acc_enc, acc_mid, acc_dec)

    @pl.when(pl.program_id(0) == pl.num_programs(0) - 1)
    def _():
        tail = jnp.concatenate([vecs[2:3, :chans], jnp.zeros((1, chans), F32)], axis=1)
        pack_grads(grads_out, chans, hid, acc_enc, acc_mid, acc_dec, vecs[0:1], tail)


def per_snap(shape):
    return pl.BlockSpec((1,) + shape, lambda s: (s,) + (0,) * len(shape))


def field_specs(lon_t, lat_t, chans, edge):
    return [
        per_snap((lon_t, lat_t, chans)),
        per_snap((lon_t + 1, lat_t, chans)),
        per_snap((lon_t, chans)),
        per_snap((edge, chans)),
        per_snap((edge, chans)),
        per_snap((lon_t * lat_t, chans)),
        whole((2, chans)),
    ]


def cost(flops):
    return pl.CostEstimate(flops=int(flops), bytes_accessed=30_000_000, transcendentals=0)


def forward_call(field, masks, weights):
    state, s_ext, row, lo, hi, extra = field
    snaps, lon_t, lat_t, chans = state.shape
    hid = weights["mid"].shape[0]
    cells = lon_t * lat_t
    ws = [weights[k] for k in ("w1", "mid", "dec", "bias")]
    return pl.pallas_call(
        forward_kernel,
        grid=(snaps,),
        in_specs=field_specs(lon_t, lat_t, chans, lo.shape[1]) + [whole(w.shape) for w in ws],
        out_specs=[
            per_snap((lon_t, lat_t, chans)),
            per_snap((lon_t, lat_t, chans)),
            per_snap((cells, hid)),
            per_snap((cells, hid)),
        ],
        out_shape=[
            jax.ShapeDtypeStruct((snaps, lon_t, lat_t, chans), F32),
            jax.ShapeDtypeStruct((snaps, lon_t, lat_t, chans), BF16),
            jax.ShapeDtypeStruct((snaps, cells, hid), F32),
            jax.ShapeDtypeStruct((snaps, cells, hid), F32),
        ],
        scratch_shapes=[
            pltpu.VMEM((cells, 10 * chans), BF16),
            pltpu.VMEM((lon_t, lat_t, chans), F32),
        ],
        compiler_params=params(),
        cost_estimate=cost(snaps * cells * 2 * hid * (10 * chans + hid + chans)),
        name="forward",
    )(state, s_ext, row, lo, hi, extra, masks, *ws)


def acc_scratch(chans, hid):
    return [
        pltpu.VMEM((10 * chans, hid), F32),
        pltpu.VMEM((hid, hid), F32),
        pltpu.VMEM((chans, hid), F32),
        pltpu.VMEM((8, hid), F32),
    ]


def turn_call(field, masks, weights, target, area):
    state, s_ext, row, lo, hi, extra = field
    snaps, lon_t, lat_t, chans = state.shape
    hid = weights["mid"].shape[0]
    cells = lon_t * lat_t
    ws = [weights[k] for k in ("w1", "mid", "dec", "bias")]
    wt = [weights[k] for k in ("w1t", "midt", "dect")]
    grad_rows = grad_layout(chans, hid)[-1]
    return pl.pallas_call(
        turn_kernel,
        grid=(snaps,),
        in_specs=field_specs(lon_t, lat_t, chans, lo.shape[1])
        + [whole(w.shape) for w in ws]
        + [per_snap((lon_t, lat_t, chans)), whole(area.shape)]
        + [whole(w.shape) for w in wt],
        out_specs=[
            per_snap((lon_t, lat_t, chans)),
            per_snap((2, lat_t, chans)),
            per_snap((lon_t + 2, chans)),
            whole((grad_rows, hid)),
        ],
        out_shape=[
            jax.ShapeDtypeStruct((snaps, lon_t, lat_t, chans), F32),
            jax.ShapeDtypeStruct((snaps, 2, lat_t, chans), F32),
            jax.ShapeDtypeStruct((snaps, lon_t + 2, chans), F32),
            jax.ShapeDtypeStruct((grad_rows, hid), F32),
        ],
        scratch_shapes=[
            pltpu.VMEM((cells, 10 * chans), BF16),
            pltpu.VMEM((lon_t, lat_t, chans), F32),
            pltpu.VMEM((cells, hid), BF16),
            pltpu.VMEM((cells, hid), BF16),
            pltpu.VMEM((cells, hid), F32),
            pltpu.VMEM((cells, hid), F32),
            pltpu.VMEM((cells, chans), BF16),
            pltpu.VMEM((cells, hid), BF16),
            pltpu.VMEM((cells, hid), BF16),
            pltpu.VMEM((3, lon_t + 2, lat_t, chans), F32),
        ]
        + acc_scratch(chans, hid),
        compiler_params=params(),
        cost_estimate=cost(snaps * cells * 6 * hid * (10 * chans + hid + chans)),
        name="turn",
    )(state, s_ext, row, lo, hi, extra, masks, *ws, target, area, *wt)


def bottom_call(field, masks, weights, pre1, pre2, gm, gs):
    state, s_ext, row, lo, hi, extra = field
    snaps, lon_t, lat_t, chans = state.shape
    hid = weights["mid"].shape[0]
    cells = lon_t * lat_t
    wt = [weights[k] for k in ("midt", "dect")]
    grad_rows = grad_layout(chans, hid)[-1]
    return pl.pallas_call(
        bottom_kernel,
        grid=(snaps,),
        in_specs=field_specs(lon_t, lat_t, chans, lo.shape[1])
        + [per_snap((cells, hid)), per_snap((cells, hid))]
        + [per_snap((lon_t, lat_t, chans)), per_snap((lon_t, lat_t, chans))]
        + [whole(w.shape) for w in wt],
        out_specs=whole((grad_rows, hid)),
        out_shape=jax.ShapeDtypeStruct((grad_rows, hid), F32),
        scratch_shapes=[
            pltpu.VMEM((cells, 10 * chans), BF16),
            pltpu.VMEM((lon_t, lat_t, chans), F32),
            pltpu.VMEM((cells, hid), BF16),
            pltpu.VMEM((cells, hid), BF16),
            pltpu.VMEM((cells, chans), BF16),
            pltpu.VMEM((cells, hid), BF16),
            pltpu.VMEM((cells, hid), BF16),
        ]
        + acc_scratch(chans, hid),
        compiler_params=params(),
        cost_estimate=cost(snaps * cells * 3 * hid * (10 * chans + hid + chans)),
        name="bottom",
    )(state, s_ext, row, lo, hi, extra, masks, pre1, pre2, gm, gs, *wt)


def three_parts(vec):
    high = lax.reduce_precision(vec, 8, 7)
    rest = vec - high
    mid = lax.reduce_precision(rest, 8, 7)
    low = lax.reduce_precision(rest - mid, 8, 7)
    return jnp.stack([high, mid, low], axis=-2)


def layer_weights(enc, mid, dec, vec):
    taps, chans, hid = enc.shape
    parts = jnp.concatenate([three_parts(vec[hid : 2 * hid]), three_parts(vec[:hid])], axis=0)
    parts = jnp.pad(parts, ((0, chans - 6), (0, 0)))
    w1 = jnp.concatenate([enc.reshape(taps * chans, hid), parts], axis=0).astype(BF16)
    pad = jnp.zeros((hid - chans,), F32)
    bias = jnp.stack([vec[2 * hid : 3 * hid], jnp.concatenate([vec[3 * hid :], pad])])
    return {
        "w1": w1,
        "mid": mid.astype(BF16),
        "dec": dec.astype(BF16),
        "bias": bias,
        "w1t": jnp.transpose(enc, (2, 0, 1)).reshape(hid, taps * chans).astype(BF16),
        "midt": mid.T.astype(BF16),
        "dect": dec.T.astype(BF16),
    }


def reduce_all(part):
    count = lax.axis_size("lon") * lax.axis_size("lat")
    rows, wide = part.shape
    each = -(-rows // (8 * count)) * 8
    cut = jnp.pad(part, ((0, each * count - rows), (0, 0))).reshape(count, each, wide)
    got = lax.all_to_all(cut, ("lon", "lat"), split_axis=0, concat_axis=0, tiled=True)
    mine = jnp.sum(got, axis=0, keepdims=True)
    spread = jnp.broadcast_to(mine, (count, each, wide))
    full = lax.all_to_all(spread, ("lon", "lat"), split_axis=0, concat_axis=0, tiled=True)
    return full.reshape(count * each, wide)[:rows]


def fast_grads(states, targets, sea_temp, ocean, valid, w_enc, w_mid, w_dec, biases):
    pool, lon_t, lat_t, chans = states.shape
    hid = w_mid.shape[1]
    lon_n, lat_n = lax.axis_size("lon"), lax.axis_size("lat")
    nlon, nlat = lon_t * lon_n, lat_t * lat_n
    zonal, forward, inverse, area_all = host_tables(nlon, nlat, 88)
    tabs = (jnp.asarray(zonal), jnp.asarray(forward), jnp.asarray(inverse))
    where = lax.axis_index("lat")
    side = jnp.stack([where == 1, where == 0]).astype(F32)
    masks = jnp.broadcast_to(side[:, None], (2, chans))
    area = lax.dynamic_slice_in_dim(jnp.asarray(area_all, F32), where * lat_t, lat_t)
    area_wide = jnp.broadcast_to(area[:, None], (lat_t, chans))
    sea = ocean.astype(F32) * sea_temp.astype(F32)
    weight_sum = jnp.sum(valid.astype(F32) * area)

    cells = lon_t * lat_t
    lane = jnp.arange(chans)
    wide_sea = sea.reshape(pool, cells, 1).astype(BF16)
    wide_valid = valid.reshape(pool, cells, 1).astype(BF16)
    extra = jnp.where(lane < 3, wide_sea, jnp.where(lane < 6, jnp.ones((), BF16), wide_valid))
    extra = jnp.where(lane < 7, extra, jnp.zeros((), BF16))

    layers = [layer_weights(w_enc[i], w_mid[i], w_dec[i], biases[i]) for i in range(2)]
    up = [(i, (i + 1) % lon_n) for i in range(lon_n)]
    down = [(t, s) for s, t in up]
    swap = [(0, 1), (1, 0)]

    def inner_row(field):
        return jnp.where(where == 0, field[:, :, -1], field[:, :, 0])

    def lon_edges(state, s_ext, row):
        def edge(i):
            body = (state[:, i].astype(F32) + s_ext[:, i].astype(F32)).astype(BF16)
            corner = (row[:, i].astype(F32) + s_ext[:, lon_t, i].astype(F32)).astype(BF16)
            return jnp.concatenate([body, corner[:, None]], axis=1)

        lo = lax.ppermute(edge(lon_t - 1), "lon", up)
        hi = lax.ppermute(edge(0), "lon", down)
        return lo, hi

    rows0 = lax.ppermute(inner_row(states), "lat", swap)
    totals = [[], []]
    starts = range(0, pool, CHUNK)
    for start in starts:
        cut = slice(start, start + CHUNK)
        state, row = states[cut], rows0[cut]
        s_ext = spectral_fast(state, tabs, True)
        lo, hi = lon_edges(state, s_ext, row)
        field0 = (state, s_ext, row, lo, hi, extra[cut])
        fresh, low, pre1, pre2 = forward_call(field0, masks, layers[0])
        row1 = lax.ppermute(inner_row(fresh), "lat", swap)
        s_ext = spectral_fast(low, tabs, True)
        lo, hi = lon_edges(fresh, s_ext, row1)
        field1 = (fresh, s_ext, row1, lo, hi, extra[cut])
        gm, edges, rows, found = turn_call(field1, masks, layers[1], targets[cut], area_wide)
        totals[1].append(found)
        rows = lax.ppermute(rows, "lat", swap)
        place = jnp.arange(lat_t)[:, None]
        inner = jnp.where(where == 0, place == lat_t - 1, place == 0)
        to_lo = edges[:, 0] + jnp.where(inner, rows[:, 0][:, None], 0.0)
        to_hi = edges[:, 1] + jnp.where(inner, rows[:, lon_t + 1][:, None], 0.0)
        from_hi = lax.ppermute(to_lo, "lon", down)
        from_lo = lax.ppermute(to_hi, "lon", up)
        lon_place = jnp.arange(lon_t)[:, None, None]
        gm = gm + jnp.where(inner, rows[:, 1 : lon_t + 1][:, :, None], 0.0)
        gm = gm + jnp.where(lon_place == 0, from_lo[:, None], 0.0)
        gm = gm + jnp.where(lon_place == lon_t - 1, from_hi[:, None], 0.0)
        gs = spectral_fast(gm.astype(BF16), tabs, False)
        totals[0].append(bottom_call(field0, masks, layers[0], pre1, pre2, gm, gs))

    one, two, three, _ = grad_layout(chans, hid)
    sums = []
    for layer_id in range(2):
        part = sum(totals[layer_id][1:], totals[layer_id][0])
        if layer_id == 0:
            part = part.at[three + 4, 0].set(weight_sum)
        sums.append(reduce_all(part))
    g_enc = jnp.stack([s[:one] for s in sums])
    g_mid = jnp.stack([s[one:two] for s in sums])
    g_dec = jnp.stack([s[two:three].T for s in sums])
    g_vec = jnp.stack(
        [jnp.concatenate([s[three : three + 3].reshape(-1), s[three + 3, :chans]]) for s in sums]
    )
    loss = jnp.sum(sums[1][three + 3, chans : 2 * chans])
    total = sums[0][three + 4, 0]
    return g_enc, g_mid, g_dec, g_vec, loss, total


def fits(states, w_mid, lon_n, lat_n):
    pool, lon_t, lat_t, chans = states.shape
    return (
        lat_n == 2
        and lon_n == 16
        and lon_t == 16
        and lat_t % 16 == 0
        and lat_t >= lon_t
        and pool % CHUNK == 0
        and chans == 128
        and w_mid.shape[1] == 2 * chans
        and w_mid.shape[0] == 2
    )


def with_halo(block, sides, width, periodic):
    for axis, dim in sides:
        count = lax.axis_size(axis)
        forward = [(i, i + 1) for i in range(count - 1)]
        if periodic:
            forward.append((count - 1, 0))
        backward = [(target, source) for source, target in forward]
        low = lax.ppermute(
            lax.slice_in_dim(block, block.shape[dim] - width, None, axis=dim), axis, forward
        )
        high = lax.ppermute(lax.slice_in_dim(block, 0, width, axis=dim), axis, backward)
        block = jnp.concatenate([low, block, high], axis=dim)
    return block


def tables(nlon, nlat, groups):
    coeffs = jnp.arange(2 * MW)
    wave = jnp.where(coeffs < MW, coeffs, coeffs - MW + 1).astype(jnp.float32)
    places = jnp.arange(nlon).astype(jnp.float32)
    angle = 2.0 * math.pi * wave[:, None] * places[None, :] / nlon
    fourier = jnp.where((coeffs < MW)[:, None], jnp.cos(angle), jnp.sin(angle)) * math.sqrt(
        2.0 / nlon
    )
    phase = ((jnp.arange(nlat).astype(jnp.float32) + 0.5) / nlat - 0.5) * math.pi
    sine = jnp.sin(phase)
    quad = jnp.cos(phase) * math.pi / nlat
    polys = [jnp.ones_like(sine), sine]
    for degree in range(1, NDEG - 1):
        polys.append(((2 * degree + 1) * sine * polys[-1] - degree * polys[-2]) / (degree + 1))
    stacked = jnp.stack(polys[:NDEG])
    degrees = jnp.arange(NDEG).astype(jnp.float32)
    legendre = jnp.sqrt((2 * degrees + 1) / 2)[:, None] * jnp.sqrt(quad)[None, :] * stacked
    damping = 1.5 * (1.0 - 2.0 * degrees * (degrees + 1) / (NDEG * (NDEG + 1)))
    filters = damping[None, :] * (1.0 - 0.5 * wave / MW)[:, None]
    kept = 2 * MW
    slots = (kept + groups - 1) // groups * groups
    fourier = jnp.pad(fourier, ((0, slots - kept), (0, 0)))
    filters = jnp.pad(filters, ((0, slots - kept), (0, 0)))
    return (fourier, legendre, filters)


def spectral(values, tabs):
    fourier, legendre, filters = tabs
    cycles = lax.all_to_all(
        values.astype(jnp.bfloat16), "lon", split_axis=3, concat_axis=1, tiled=True
    ).astype(values.dtype)
    coeff = jnp.einsum("kx,sxjc->skjc", fourier, cycles, precision=HIGH)
    block = fourier.shape[0] // lax.axis_size("lat")
    where = lax.axis_index("lat")
    block_filter = lax.dynamic_slice_in_dim(filters, where * block, block, 0)
    columns = lax.all_to_all(
        coeff.astype(jnp.bfloat16), "lat", split_axis=1, concat_axis=2, tiled=True
    ).astype(coeff.dtype)
    spec = (
        jnp.einsum("nj,skjc->sknc", legendre, columns, precision=HIGH)
        * block_filter[None, :, :, None]
    )
    back = jnp.einsum("nj,sknc->skjc", legendre, spec, precision=HIGH)
    coeff_back = lax.all_to_all(
        back.astype(jnp.bfloat16), "lat", split_axis=2, concat_axis=1, tiled=True
    ).astype(back.dtype)
    grid = jnp.einsum("kx,skjc->sxjc", fourier, coeff_back, precision=HIGH)
    return lax.all_to_all(
        grid.astype(jnp.bfloat16), "lon", split_axis=1, concat_axis=3, tiled=True
    ).astype(grid.dtype)


def extend(field):
    wider = with_halo(field, (("lon", 1),), 1, True)
    return with_halo(wider, (("lat", 2),), 1, False)


def neighbours(padded, flipped, lon_t, lat_t):
    parts = []
    for row_off in range(3):
        for col_off in range(3):
            first = 2 - row_off if flipped else row_off
            second = 2 - col_off if flipped else col_off
            parts.append(padded[:, first : first + lon_t, second : second + lat_t])
    stacked = jnp.stack(parts, axis=3)
    return stacked.reshape(-1, 9 * padded.shape[-1])


def gelu_fn(value):
    return jax.nn.gelu(value, approximate=True)


def gelu_back(value, grad):
    return jax.vjp(gelu_fn, value)[1](grad)[0]


def layer_forward(state, sea, enc, mid, dec, vec, tabs):
    hid = mid.shape[0]
    lon_t, lat_t = (state.shape[1], state.shape[2])
    moved = state + spectral(state, tabs)
    patches = neighbours(extend(moved.astype(jnp.bfloat16)), False, lon_t, lat_t)
    pre1 = jnp.dot(patches, enc, preferred_element_type=jnp.float32)
    pre1 = pre1 + sea.reshape(-1, 1) * vec[hid : 2 * hid] + vec[:hid]
    active1 = gelu_fn(pre1).astype(jnp.bfloat16)
    pre2 = jnp.dot(active1, mid, preferred_element_type=jnp.float32) + vec[2 * hid : 3 * hid]
    active2 = gelu_fn(pre2).astype(jnp.bfloat16)
    output = jnp.dot(active2, dec, preferred_element_type=jnp.float32) + vec[3 * hid :]
    return (moved + output.reshape(state.shape), (patches, pre1, active1, pre2, active2))


def layer_backward(grad_state, sea, enc, mid, dec, saved, tabs):
    patches, pre1, active1, pre2, active2 = saved
    hid = mid.shape[0]
    shape = grad_state.shape
    chans = shape[-1]
    g_out = grad_state.reshape(-1, chans).astype(jnp.bfloat16)
    g_dec = jnp.einsum("rh,rc->hc", active2, g_out, preferred_element_type=jnp.float32)
    g_act2 = jnp.einsum("rc,hc->rh", g_out, dec, preferred_element_type=jnp.float32)
    g_pre2 = gelu_back(pre2, g_act2).astype(jnp.bfloat16)
    g_mid = jnp.einsum("rh,rg->hg", active1, g_pre2, preferred_element_type=jnp.float32)
    g_act1 = jnp.einsum("rg,hg->rh", g_pre2, mid, preferred_element_type=jnp.float32)
    g_pre1 = gelu_back(pre1, g_act1).astype(jnp.bfloat16)
    g_enc = jnp.einsum("rk,rh->kh", patches, g_pre1, preferred_element_type=jnp.float32)
    wide1 = g_pre1.astype(jnp.float32)
    g_vec = jnp.concatenate(
        [
            jnp.sum(wide1, 0),
            jnp.sum(sea.reshape(-1, 1) * wide1, 0),
            jnp.sum(g_pre2.astype(jnp.float32), 0),
            jnp.sum(g_out.astype(jnp.float32), 0),
        ]
    )
    spread = extend(g_pre1.reshape(shape[0], shape[1], shape[2], hid))
    gathered = neighbours(spread, True, shape[1], shape[2]).reshape(-1, 9, hid)
    g_input = jnp.einsum(
        "rkh,kch->rc", gathered, enc.reshape(9, chans, hid), preferred_element_type=jnp.float32
    )
    grad_moved = grad_state + g_input.reshape(shape)
    return (grad_moved + spectral(grad_moved, tabs), (g_enc, g_mid, g_dec, g_vec))


def general_grads(states, targets, sea_temp, ocean, valid, order, w_enc, w_mid, w_dec, biases):
    pool, lon_t, lat_t, chans = states.shape
    layers, hid = (w_mid.shape[0], w_mid.shape[1])
    nlon = lon_t * lax.axis_size("lon")
    nlat = lat_t * lax.axis_size("lat")
    tabs = tables(nlon, nlat, lax.axis_size("lat"))
    lat_glob = (lax.axis_index("lat") * lat_t + jnp.arange(lat_t)).astype(jnp.float32)
    area = jnp.cos(((lat_glob + 0.5) / nlat - 0.5) * math.pi)
    enc_low = w_enc.astype(jnp.bfloat16).reshape(layers, 9 * chans, hid)
    mid_low = w_mid.astype(jnp.bfloat16)
    dec_low = w_dec.astype(jnp.bfloat16)
    snaps = pool // MB
    sums = [
        jnp.zeros((layers, 9 * chans, hid), jnp.float32),
        jnp.zeros_like(w_mid),
        jnp.zeros_like(w_dec),
        jnp.zeros_like(biases),
    ]
    loss = jnp.zeros((), jnp.float32)
    total = jnp.zeros((), jnp.float32)
    for batch_id in range(MB):
        picks = lax.dynamic_slice_in_dim(order, batch_id * snaps, snaps)
        state = jnp.take(states, picks, axis=0).astype(jnp.float32)
        target = jnp.take(targets, picks, axis=0).astype(jnp.float32)
        sea = jnp.take(ocean, picks, axis=0).astype(jnp.float32) * jnp.take(
            sea_temp, picks, axis=0
        ).astype(jnp.float32)
        weight = jnp.take(valid, picks, axis=0).astype(jnp.float32) * area[None, None, :]
        kept = []
        for layer_id in range(layers):
            state, saved = layer_forward(
                state,
                sea,
                enc_low[layer_id],
                mid_low[layer_id],
                dec_low[layer_id],
                biases[layer_id],
                tabs,
            )
            kept.append(saved)
        diff = state - target
        loss = loss + jnp.sum(weight[..., None] * diff * diff)
        total = total + jnp.sum(weight)
        grad_state = 2.0 * weight[..., None] * diff
        for layer_id in reversed(range(layers)):
            grad_state, found = layer_backward(
                grad_state,
                sea,
                enc_low[layer_id],
                mid_low[layer_id],
                dec_low[layer_id],
                kept[layer_id],
                tabs,
            )
            sums = [acc.at[layer_id].add(part) for acc, part in zip(sums, found)]
    g_enc, g_mid, g_dec, g_vec, loss, total = lax.psum(
        (sums[0], sums[1], sums[2], sums[3], loss, total), ("lon", "lat")
    )
    return g_enc.reshape(w_enc.shape), g_mid, g_dec, g_vec, loss, total


def body(
    states,
    targets,
    sea_temp,
    ocean,
    valid,
    order,
    w_enc,
    w_mid,
    w_dec,
    biases,
    mom_enc,
    mom_mid,
    mom_dec,
    mom_bias,
    avg_enc,
    avg_mid,
    avg_dec,
    avg_bias,
):
    pool, lon_t, lat_t = states.shape[:3]
    lon_n, lat_n = lax.axis_size("lon"), lax.axis_size("lat")
    if fits(states, w_mid, lon_n, lat_n):
        found = fast_grads(states, targets, sea_temp, ocean, valid, w_enc, w_mid, w_dec, biases)
    else:
        found = general_grads(
            states, targets, sea_temp, ocean, valid, order, w_enc, w_mid, w_dec, biases
        )
    loss, total = found[4:]
    grads = (found[0].reshape(w_enc.shape),) + found[1:4]
    rate = RATE_BASE * math.sqrt(pool * lon_t * lon_n * lat_t * lat_n)
    news, moms, avgs, copies = ([], [], [], [])
    for weight_now, grad, mom, avg in zip(
        (w_enc, w_mid, w_dec, biases),
        grads,
        (mom_enc, mom_mid, mom_dec, mom_bias),
        (avg_enc, avg_mid, avg_dec, avg_bias),
    ):
        scaled = grad / total
        mom_new = MOMENTUM * mom + scaled
        fresh = weight_now - rate * (scaled + MOMENTUM * mom_new)
        news.append(fresh)
        moms.append(mom_new)
        avgs.append(AVERAGE * avg + (1.0 - AVERAGE) * fresh)
        copies.append(fresh.astype(jnp.bfloat16))
    return (
        loss,
        total,
        news[0],
        news[1],
        news[2],
        news[3],
        moms[0],
        moms[1],
        moms[2],
        moms[3],
        avgs[0],
        avgs[1],
        avgs[2],
        avgs[3],
        copies[0],
        copies[1],
        copies[2],
        copies[3],
    )


def solution(mesh):
    placed = (
        P(None, "lon", "lat", None),
        P(None, "lon", "lat", None),
        P(None, "lon", "lat"),
        P(None, "lon", "lat"),
        P(None, "lon", "lat"),
        P(),
        P(),
        P(),
        P(),
        P(),
        P(),
        P(),
        P(),
        P(),
        P(),
        P(),
        P(),
        P(),
    )
    return jax.shard_map(
        body,
        mesh=mesh,
        in_specs=placed,
        out_specs=(
            P(),
            P(),
            P(),
            P(),
            P(),
            P(),
            P(),
            P(),
            P(),
            P(),
            P(),
            P(),
            P(),
            P(),
            P(),
            P(),
            P(),
            P(),
        ),
        check_vma=False,
    )
```

```python
import functools
import math

import jax
import jax.numpy as jnp
import numpy as np
from jax import lax
from jax.experimental import pallas as pl
from jax.experimental.pallas import tpu as pltpu
from jax.sharding import PartitionSpec as P

MW = 86
NDEG = 86
MB = 4


HIGH = lax.Precision.HIGHEST
MOMENTUM = 0.9
AVERAGE = 0.99
RATE_BASE = 0.0006

F32 = jnp.float32
BF16 = jnp.bfloat16
CHUNK = 4
VMEM = 56 * 1024 * 1024
GELU_A = math.sqrt(2.0 / math.pi)
GELU_B = 0.044715


def split_table(table):
    table = np.asarray(table, np.float32)
    high = table.astype(BF16)
    low = (table - high.astype(np.float32)).astype(BF16)
    return np.concatenate([high, low], axis=0)


def host_tables(nlon, nlat, deg):
    kept = np.arange(2 * MW)
    wave = np.where(kept < MW, kept, kept - MW + 1).astype(np.float64)
    angle = 2.0 * np.pi * wave[:, None] * np.arange(nlon)[None, :] / nlon
    fourier = np.where((kept < MW)[:, None], np.cos(angle), np.sin(angle)) * np.sqrt(2.0 / nlon)
    zonal = (fourier * (1.0 - 0.5 * wave / MW)[:, None]).T @ fourier
    phase = ((np.arange(nlat) + 0.5) / nlat - 0.5) * np.pi
    sine, area = np.sin(phase), np.cos(phase)
    polys = [np.ones_like(sine), sine]
    for n in range(1, NDEG - 1):
        polys.append(((2 * n + 1) * sine * polys[-1] - n * polys[-2]) / (n + 1))
    degrees = np.arange(NDEG)
    legendre = np.sqrt((2 * degrees + 1) / 2)[:, None] * np.sqrt(area * np.pi / nlat)[None, :]
    legendre = legendre * np.stack(polys)
    damping = 1.5 * (1.0 - 2.0 * degrees * (degrees + 1) / (NDEG * (NDEG + 1)))
    forward = np.zeros((deg, nlat))
    forward[:NDEG] = legendre
    inverse = np.zeros((nlat, -(-deg // 32) * 32))
    inverse[:, :NDEG] = (legendre * damping[:, None]).T
    return split_table(zonal), split_table(forward), split_table(inverse), area


def mm(a, b):
    return jnp.dot(a, b, preferred_element_type=F32)


def mm_rows(a, b):
    return lax.dot_general(a, b, (((0,), (0,)), ((), ())), preferred_element_type=F32)


def whole(shape):
    return pl.BlockSpec(shape, lambda *_: (0,) * len(shape))


def params():
    return pltpu.CompilerParams(vmem_limit_bytes=VMEM)


HALF = CHUNK // 2


def any_spec():
    return pl.BlockSpec(memory_space=pl.ANY)


def shape_of(dims, dtype):
    return jax.ShapeDtypeStruct(dims, dtype)


def grid_of(count, in_specs, out_specs, scratch):
    return pltpu.PrefetchScalarGridSpec(
        num_scalar_prefetch=1,
        grid=(count,),
        in_specs=in_specs,
        out_specs=out_specs,
        scratch_shapes=scratch,
    )


def first_of(chunk, half, info):
    if chunk is None:
        return 0
    return chunk * CHUNK + HALF * (info[0] if half == 0 else 1 - info[0])


def snap_spec(dims, chunk=None, half=0):
    return pl.BlockSpec(
        (1,) + dims, lambda g, info: (first_of(chunk, half, info) + g,) + (0,) * len(dims)
    )


def legendre_kernel(wide, info, own_ref, other_ref, l_ref, dep_ref, o_ref, tmp):
    parts, rows, lon_t, chans = o_ref.shape
    lat_t = own_ref.shape[2]
    deg = l_ref.shape[0] // 2
    count = lon_t + 2 if wide else lon_t
    each = deg // parts
    place = lax.broadcasted_iota(jnp.int32, (lat_t, chans), 0)
    south = info[0] == 1
    inner = place == jnp.where(south, 0, lat_t - 1)
    other_inner = place == jnp.where(south, lat_t - 1, 0)

    def column(x):
        own, other = own_ref[0, x], other_ref[0, x]
        if wide:
            to_own = other_ref[0, count, x : x + 1].astype(F32)
            to_other = own_ref[0, count, x : x + 1].astype(F32)
            own = (own.astype(F32) + jnp.where(inner, to_own, 0.0)).astype(BF16)
            other = (other.astype(F32) + jnp.where(other_inner, to_other, 0.0)).astype(BF16)
        return jnp.concatenate([own, other], axis=0)

    for base in range(0, count, 4):
        span = range(base, min(base + 4, count))
        r = mm(l_ref[...], jnp.concatenate([column(x) for x in span], axis=1))
        r = r[:deg] + r[deg:]
        for x in span:
            tmp[:, x, :] = r[:, (x - base) * chans : (x - base + 1) * chans]
    o_ref[:, :each] = tmp[:, :lon_t, :].astype(BF16).reshape(parts, each, lon_t, chans)
    if wide:
        rest = jnp.zeros((lon_t - each, chans), F32)
        for p in range(parts):
            for side in range(2):
                edge = tmp[p * each : (p + 1) * each, lon_t + side, :]
                o_ref[p, each + side] = jnp.concatenate([edge, rest], axis=0).astype(BF16)


def legendre_call(info, own, chunk, half, other, table, dep, wide):
    snaps, slabs, lat_t, chans = other.shape
    deg = table.shape[0] // 2
    parts = 8
    lon_t = slabs - 3 if wide else slabs
    rows = deg // parts + (2 if wide else 0)
    return pl.pallas_call(
        functools.partial(legendre_kernel, wide),
        grid_spec=grid_of(
            snaps,
            [
                snap_spec(own.shape[1:], chunk, half),
                snap_spec(other.shape[1:]),
                whole(table.shape),
                any_spec(),
            ],
            pl.BlockSpec((parts, rows, lon_t, chans), lambda s, info: (s, 0, 0, 0)),
            [pltpu.VMEM((deg, lon_t + 8 if wide else lon_t, chans), F32)],
        ),
        out_shape=shape_of((snaps * parts, rows, lon_t, chans), BF16),
        compiler_params=params(),
        cost_estimate=cost(3.2),
        name="legendre",
    )(info, own, other, table, dep)


def zonal_kernel(wide_in, x_ref, a_ref, dep_ref, o_ref, tmp):
    groups, _, lon_t, chans = x_ref.shape
    nlon = groups * lon_t
    rows = min(x_ref.shape[1], o_ref.shape[1])
    if wide_in:
        for side in range(2):
            tmp[side * groups : (side + 1) * groups] = x_ref[:, rows + side].astype(F32)
    else:
        tmp[...] = jnp.zeros_like(tmp)
    for base in range(0, rows, 4):
        span = range(base, min(base + 4, rows))
        fields = jnp.concatenate([x_ref[:, n].reshape(nlon, chans) for n in span], axis=1)
        if wide_in:
            edges = jnp.concatenate([tmp[:, n, :] for n in span], axis=1).astype(BF16)
            r = mm(a_ref[:, :nlon], fields) + mm(a_ref[:, nlon:], edges)
            r = r[:nlon] + r[nlon:]
        else:
            r = mm(a_ref[...], fields)
            size = r.shape[0] // 2
            r = r[:size] + r[size:]
        low = r[:nlon].astype(BF16)
        for n in span:
            lanes = slice((n - base) * chans, (n - base + 1) * chans)
            o_ref[:, n] = low[:, lanes].reshape(groups, lon_t, chans)
            if not wide_in:
                tmp[:, n, :] = r[nlon:, lanes]
    if not wide_in:
        for side in range(2):
            o_ref[:, rows + side] = tmp[side * groups : (side + 1) * groups].astype(BF16)


def zonal_call(fields, table, dep, wide_in):
    groups, rows, lon_t, chans = fields.shape
    out = (groups, rows - 2 if wide_in else rows + 2, lon_t, chans)
    return pl.pallas_call(
        functools.partial(zonal_kernel, wide_in),
        in_specs=[pl.BlockSpec(memory_space=pltpu.VMEM)] * 2 + [any_spec()],
        out_specs=pl.BlockSpec(memory_space=pltpu.VMEM),
        out_shape=shape_of(out, BF16),
        scratch_shapes=[pltpu.VMEM((2 * groups, lon_t, chans), F32)],
        compiler_params=params(),
        cost_estimate=cost(2.8),
        name="zonal",
    )(fields, table, dep)


def synthesis_kernel(wide, info, x_ref, l_ref, dep_ref, own_ref, send_ref, tmp):
    parts, rows, lon_t, chans = x_ref.shape
    each = rows - 2 if wide else rows
    deg = parts * each
    count = lon_t + 2 if wide else lon_t
    nlat = l_ref.shape[0] // 2
    half = nlat // 2
    south = info[0] == 1
    tmp[:deg, :lon_t, :] = x_ref[:, :each].reshape(deg, lon_t, chans).astype(F32)
    if wide:
        for p in range(parts):
            for side in range(2):
                tmp[p * each : (p + 1) * each, lon_t + side, :] = x_ref[p, each + side, :each].astype(F32)
    tmp[deg:] = jnp.zeros((tmp.shape[0] - deg,) + tmp.shape[1:], F32)
    for base in range(0, count, 4):
        span = range(base, min(base + 4, count))
        cols = jnp.concatenate([tmp[:, x, :] for x in span], axis=1).astype(BF16)
        r = mm(l_ref[...], cols)
        r = r[:nlat] + r[nlat:]
        for x in span:
            one = r[:, (x - base) * chans : (x - base + 1) * chans]
            own_ref[0, x] = one[:half].astype(BF16)
            send_ref[0, x] = one[half:].astype(BF16)
            if wide:
                tmp[0, x : x + 1, :] = jnp.where(south, one[2 * half - 1 :], one[half : half + 1])
                tmp[1, x : x + 1, :] = jnp.where(south, one[:1], one[half - 1 : half])
    if wide:
        size = tmp.shape[1]
        rest = jnp.zeros((half - size, chans), F32)
        for h, ref in enumerate((own_ref, send_ref)):
            ref[0, count] = jnp.concatenate([tmp[h], rest], axis=0).astype(BF16)


def synthesis_call(info, coeffs, table, snaps, wide, dep):
    total, rows, lon_t, chans = coeffs.shape
    parts = total // snaps
    nlat = table.shape[0] // 2
    slabs = lon_t + 3 if wide else lon_t
    out = snap_spec((slabs, nlat // 2, chans))
    return pl.pallas_call(
        functools.partial(synthesis_kernel, wide),
        grid_spec=grid_of(
            snaps,
            [
                pl.BlockSpec((parts, rows, lon_t, chans), lambda s, info: (s, 0, 0, 0)),
                whole(table.shape),
                any_spec(),
            ],
            [out, out],
            [pltpu.VMEM((table.shape[1], lon_t + 8 if wide else lon_t, chans), F32)],
        ),
        out_shape=[shape_of((snaps, slabs, nlat // 2, chans), BF16)] * 2,
        compiler_params=params(),
        cost_estimate=cost(3.4),
        name="synthesis",
    )(info, coeffs, table, dep)


def gelu_of(x):
    t = jnp.tanh(x * (GELU_A + (GELU_A * GELU_B) * (x * x)))
    return 0.5 * x * (1.0 + t)


def gelu_and_slope(x):
    sq = x * x
    t = jnp.tanh(x * (GELU_A + (GELU_A * GELU_B) * sq))
    cdf = 0.5 + 0.5 * t
    slope = cdf + (0.5 * x) * (1.0 - t * t) * (GELU_A + (3.0 * GELU_A * GELU_B) * sq)
    return x * cdf, slope


def fill_patches(patches, slabs, ends, masks):
    lat_t, chans = slabs[0].shape
    lon_t = len(slabs) - 2
    place = lax.broadcasted_iota(jnp.int32, (lat_t, chans), 0)
    for i in range(lon_t + 2):
        low_row, high_row = ends[i] * masks[0:1], ends[i] * masks[1:2]
        down = jnp.where(place == 0, low_row, pltpu.roll(slabs[i], 1, 0)).astype(BF16)
        up = jnp.where(place == lat_t - 1, high_row, pltpu.roll(slabs[i], lat_t - 1, 0)).astype(BF16)
        mid = slabs[i].astype(BF16)
        for a in range(3):
            x = i - a
            if 0 <= x < lon_t:
                for b, piece in enumerate((down, mid, up)):
                    k = 3 * a + b
                    patches[x * lat_t : (x + 1) * lat_t, k * chans : (k + 1) * chans] = piece


def assemble(patches, field_refs, moved):
    state_ref, s_ref, row_ref, lo_ref, hi_ref, extra_ref, masks_ref = field_refs
    lon_t, lat_t, chans = moved.shape
    moved[...] = state_ref[0].astype(F32) + s_ref[0, :lon_t].astype(F32)
    rows = row_ref[0].astype(F32) + s_ref[0, lon_t + 2, : lon_t + 2].astype(F32)
    slabs = [lo_ref[0].astype(F32) + s_ref[0, lon_t].astype(F32)]
    slabs += [moved[i] for i in range(lon_t)]
    slabs += [hi_ref[0].astype(F32) + s_ref[0, lon_t + 1].astype(F32)]
    ends = [rows[i : i + 1] for i in [lon_t] + list(range(lon_t)) + [lon_t + 1]]
    fill_patches(patches, slabs, ends, masks_ref[...])
    patches[:, 9 * chans :] = extra_ref[0]


def forward_kernel(info, *refs):
    field_refs, (w1_ref, mid_ref, dec_ref, bias_ref, dep_ref) = refs[:7], refs[7:12]
    state_out, low_out, row_out, up_out, down_out, pre1_out, pre2_out, patches, moved = refs[12:]
    lon_t, lat_t, chans = moved.shape
    hid = mid_ref.shape[0]
    assemble(patches, field_refs, moved)
    pre1 = mm(patches[...], w1_ref[...])
    pre1_out[0] = pre1
    active1 = gelu_of(pre1).astype(BF16)
    pre2 = mm(active1, mid_ref[...]) + bias_ref[0:1, :hid]
    pre2_out[0] = pre2
    active2 = gelu_of(pre2).astype(BF16)
    out = mm(active2, dec_ref[...]) + bias_ref[1:2, :chans]
    state_out[0] = moved[...] + out.reshape(lon_t, lat_t, chans)
    row_out[0] = jnp.where(info[0] == 1, state_out[0, :, 0, :], state_out[0, :, lat_t - 1, :])
    low_out[0] = state_out[0].astype(BF16)
    up_out[0] = state_out[0, lon_t - 1]
    down_out[0] = state_out[0, 0]


GRAD_PAD = 128


def grad_layout(chans, hid):
    one, two, three = 9 * chans, 9 * chans + hid, 9 * chans + hid + chans
    return (one, two, three, -(-(three + 8) // GRAD_PAD) * GRAD_PAD)


def add_grads(first, patches, active1, active2, g_out, g_pre2, g_pre1, acc_enc, acc_mid, acc_dec):
    enc = mm_rows(patches[...], g_pre1[...])
    mid = mm_rows(active1[...], g_pre2[...])
    dec = mm_rows(g_out[...], active2[...])

    @pl.when(first)
    def _():
        acc_enc[...] = enc
        acc_mid[...] = mid
        acc_dec[...] = dec

    @pl.when(jnp.logical_not(first))
    def _():
        acc_enc[...] += enc
        acc_mid[...] += mid
        acc_dec[...] += dec


def pack_grads(out, before, chans, hid, acc_enc, acc_mid, acc_dec, vecs):
    one, two, three, rows = grad_layout(chans, hid)
    tail = jnp.concatenate([vecs[2:3, :chans], vecs[1:2, :chans]], axis=1)
    out[three:] = jnp.zeros((rows - three, hid), F32)
    pieces = [
        (0, one, lambda: acc_enc[:one]),
        (one, two, lambda: acc_mid[...]),
        (two, three, lambda: acc_dec[...]),
        (three, three + 1, lambda: acc_enc[one + 3 : one + 4]),
        (three + 1, three + 2, lambda: acc_enc[one : one + 1]),
        (three + 2, three + 3, lambda: vecs[0:1]),
        (three + 3, three + 4, lambda: tail),
        (three + 4, three + 5, lambda: vecs[3:4]),
    ]
    for start, stop, piece in pieces:
        if before is None:
            out[start:stop] = piece()
        else:
            out[start:stop] = before[start:stop] + piece()


def turn_kernel(more, info, *refs):
    field_refs, (w1_ref, mid_ref, dec_ref, bias_ref) = refs[:7], refs[7:11]
    extra_ref, masks_ref = field_refs[5:]
    target_ref, area_ref, w1t_ref, midt_ref, dect_ref, dep_ref = refs[11:17]
    before = refs[17] if more else None
    (
        gm_out, low_out, lo_out, hi_out, rows_out, grads_out,
        patches, moved, active1, active2, slope1, slope2, g_out, g_pre2, g_pre1, spread,
        acc_enc, acc_mid, acc_dec, vecs,
    ) = refs[18 if more else 17 :]
    lon_t, lat_t, chans = moved.shape
    hid = mid_ref.shape[0]
    first = pl.program_id(0) == 0
    assemble(patches, field_refs, moved)
    spread[...] = jnp.zeros_like(spread)

    @pl.when(first)
    def _():
        vecs[...] = jnp.zeros_like(vecs)

    step = 8
    for x in range(0, lon_t, step):
        rows = slice(x * lat_t, (x + step) * lat_t)
        pre1 = mm(patches[rows], w1_ref[...])
        a1, d1 = gelu_and_slope(pre1)
        active1[rows] = a1.astype(BF16)
        slope1[rows] = d1
        pre2 = mm(active1[rows], mid_ref[...]) + bias_ref[0:1, :hid]
        a2, d2 = gelu_and_slope(pre2)
        active2[rows] = a2.astype(BF16)
        slope2[rows] = d2
        out = mm(active2[rows], dec_ref[...]) + bias_ref[1:2, :chans]
        fresh = moved[x : x + step] + out.reshape(step, lat_t, chans)
        diff = fresh - target_ref[0, x : x + step].astype(F32)
        valid = jnp.broadcast_to(extra_ref[0, rows, 6:7].astype(F32), (step * lat_t, chans))
        weight = valid.reshape(step, lat_t, chans) * area_ref[...][None]
        vecs[3:4, :chans] += jnp.sum(weight.reshape(step * lat_t, chans), 0, keepdims=True)
        weighted = weight * diff
        vecs[1:2, :chans] += jnp.sum((weighted * diff).reshape(step * lat_t, chans), 0, keepdims=True)
        grad = 2.0 * weighted
        moved[x : x + step] = grad
        low = grad.reshape(step * lat_t, chans).astype(BF16)
        g_out[rows] = low
        vecs[2:3, :chans] += jnp.sum(low.astype(F32), 0, keepdims=True)
        gp2 = (mm(low, dect_ref[...]) * slope2[rows]).astype(BF16)
        g_pre2[rows] = gp2
        vecs[0:1] += jnp.sum(gp2.astype(F32), 0, keepdims=True)
        gp1 = (mm(gp2, midt_ref[...]) * slope1[rows]).astype(BF16)
        g_pre1[rows] = gp1
        taps = mm(gp1, w1t_ref[...])
        for a in range(3):
            for b in range(3):
                k = 3 * a + b
                spread[b, x + a : x + a + step] += taps[:, k * chans : (k + 1) * chans].reshape(
                    step, lat_t, chans
                )
    place = lax.broadcasted_iota(jnp.int32, (lat_t, chans), 0)
    masks = masks_ref[...]
    for i in range(lon_t + 2):
        down, here, up = spread[0, i], spread[1, i], spread[2, i]
        got = here + jnp.where(place == lat_t - 1, 0.0, pltpu.roll(down, lat_t - 1, 0))
        got = got + jnp.where(place == 0, 0.0, pltpu.roll(up, 1, 0))
        beyond = down[0:1] * masks[0:1] + up[lat_t - 1 : lat_t] * masks[1:2]
        if i in (0, lon_t + 1):
            at = lon_t if i == 0 else lon_t + 1
            edge = lo_out if i == 0 else hi_out
            edge[0, :lat_t] = got.astype(BF16)
            edge[0, lat_t:] = jnp.broadcast_to(beyond, (edge.shape[1] - lat_t, chans)).astype(BF16)
            low_out[0, at] = got.astype(BF16)
        else:
            at = i - 1
            total = got + moved[at]
            gm_out[0, at] = total
            low_out[0, at] = total.astype(BF16)
        rows_out[0, at : at + 1] = beyond
    rest = jnp.zeros((lat_t - rows_out.shape[1], chans), F32)
    low_out[0, lon_t + 2] = jnp.concatenate([rows_out[0], rest], axis=0).astype(BF16)
    add_grads(first, patches, active1, active2, g_out, g_pre2, g_pre1, acc_enc, acc_mid, acc_dec)

    @pl.when(pl.program_id(0) == pl.num_programs(0) - 1)
    def _():
        pack_grads(grads_out, before, chans, hid, acc_enc, acc_mid, acc_dec, vecs)


def bottom_kernel(more, info, *refs):
    field_refs = refs[:7]
    pre1_ref, pre2_ref, gm_ref, glo_ref, ghi_ref, grow_ref, gs_ref, midt_ref, dect_ref, dep_ref = refs[7:17]
    before = refs[17] if more else None
    (
        grads_out, patches, moved, active1, active2, g_out, g_pre2, g_pre1, acc_enc, acc_mid, acc_dec, vecs,
    ) = refs[17 + more :]
    lon_t, lat_t, chans = moved.shape
    hid = midt_ref.shape[0]
    first = pl.program_id(0) == 0
    assemble(patches, field_refs, moved)

    moved[...] = gm_ref[0] + gs_ref[0].astype(F32)
    moved[0] += glo_ref[0, :lat_t].astype(F32)
    moved[lon_t - 1] += ghi_ref[0, :lat_t].astype(F32)
    place = lax.broadcasted_iota(jnp.int32, (lat_t, chans), 0)
    inner = place == jnp.where(info[0] == 1, 0, lat_t - 1)
    for x in range(lon_t):
        moved[x] += jnp.where(inner, grow_ref[0, x : x + 1], 0.0)

    @pl.when(first)
    def _():
        vecs[...] = jnp.zeros_like(vecs)

    step = 8
    for x in range(0, lon_t, step):
        rows = slice(x * lat_t, (x + step) * lat_t)
        a1, d1 = gelu_and_slope(pre1_ref[0, rows])
        active1[rows] = a1.astype(BF16)
        a2, d2 = gelu_and_slope(pre2_ref[0, rows])
        active2[rows] = a2.astype(BF16)
        low = moved[x : x + step].reshape(step * lat_t, chans).astype(BF16)
        g_out[rows] = low
        vecs[2:3, :chans] += jnp.sum(low.astype(F32), 0, keepdims=True)
        gp2 = (mm(low, dect_ref[...]) * d2).astype(BF16)
        g_pre2[rows] = gp2
        vecs[0:1] += jnp.sum(gp2.astype(F32), 0, keepdims=True)
        g_pre1[rows] = (mm(gp2, midt_ref[...]) * d1).astype(BF16)
    add_grads(first, patches, active1, active2, g_out, g_pre2, g_pre1, acc_enc, acc_mid, acc_dec)

    @pl.when(pl.program_id(0) == pl.num_programs(0) - 1)
    def _():
        pack_grads(grads_out, before, chans, hid, acc_enc, acc_mid, acc_dec, vecs)


def field_specs(field, chunk, half, pool_state):
    state, s_ext, row, lo, hi, extra, masks = field
    there = chunk if pool_state else None
    return [
        snap_spec(state.shape[1:], there, half),
        snap_spec(s_ext.shape[1:]),
        snap_spec(row.shape[1:], there, half),
        snap_spec(lo.shape[1:], there, half),
        snap_spec(hi.shape[1:], there, half),
        snap_spec(extra.shape[1:], chunk, half),
        whole(masks.shape),
    ]


def cost(micros):
    return pl.CostEstimate(flops=int(micros * 1e9), bytes_accessed=int(micros * 3e6), transcendentals=0)


def forward_call(info, chunk, half, field, weights, dep):
    dims = field[0].shape[1:]
    lon_t, lat_t, chans = dims
    cells = lon_t * lat_t
    hid = weights["mid"].shape[0]
    ws = [weights[k] for k in ("w1", "mid", "dec", "bias")]
    edge = ((lat_t, chans), F32)
    outs = [(dims, F32), (dims, BF16), ((lon_t, chans), F32), edge, edge, ((cells, hid), F32), ((cells, hid), F32)]
    return pl.pallas_call(
        forward_kernel,
        grid_spec=grid_of(
            HALF,
            field_specs(field, chunk, half, True) + [whole(w.shape) for w in ws] + [any_spec()],
            [snap_spec(d) for d, _ in outs],
            [pltpu.VMEM((cells, 10 * chans), BF16), pltpu.VMEM(dims, F32)],
        ),
        out_shape=[shape_of((HALF,) + d, t) for d, t in outs],
        compiler_params=params(),
        cost_estimate=cost(6.5),
        name="forward",
    )(info, *field, *ws, dep)


def back_scratch(dims, hid):
    lon_t, lat_t, chans = dims
    cells = lon_t * lat_t
    return [
        pltpu.VMEM((cells, chans), BF16),
        pltpu.VMEM((cells, hid), BF16),
        pltpu.VMEM((cells, hid), BF16),
    ], [
        pltpu.VMEM((10 * chans, hid), F32),
        pltpu.VMEM((hid, hid), F32),
        pltpu.VMEM((chans, hid), F32),
        pltpu.VMEM((8, hid), F32),
    ]


def turn_call(info, chunk, half, field, weights, targets, area, dep, before):
    dims = field[0].shape[1:]
    lon_t, lat_t, chans = dims
    cells = lon_t * lat_t
    hid = weights["mid"].shape[0]
    ws = [weights[k] for k in ("w1", "mid", "dec", "bias")]
    wt = [weights[k] for k in ("w1t", "midt", "dect")]
    grad_rows = grad_layout(chans, hid)[-1]
    more = before is not None
    last = [before] if more else []
    edge = ((lat_t + 16, chans), BF16)
    low = ((lon_t + 3, lat_t, chans), BF16)
    outs = [(dims, F32), low, edge, edge, ((lon_t + 8, chans), F32)]
    grads, sums = back_scratch(dims, hid)
    return pl.pallas_call(
        functools.partial(turn_kernel, more),
        grid_spec=grid_of(
            HALF,
            field_specs(field, chunk, half, False)
            + [whole(w.shape) for w in ws]
            + [snap_spec(dims, chunk, half), whole(area.shape)]
            + [whole(w.shape) for w in wt]
            + [any_spec()]
            + [whole(w.shape) for w in last],
            [snap_spec(d) for d, _ in outs] + [whole((grad_rows, hid))],
            [
                pltpu.VMEM((cells, 10 * chans), BF16),
                pltpu.VMEM(dims, F32),
                pltpu.VMEM((cells, hid), BF16),
                pltpu.VMEM((cells, hid), BF16),
                pltpu.VMEM((cells, hid), F32),
                pltpu.VMEM((cells, hid), F32),
            ]
            + grads
            + [pltpu.VMEM((3, lon_t + 2, lat_t, chans), F32)]
            + sums,
        ),
        out_shape=[shape_of((HALF,) + d, t) for d, t in outs] + [shape_of((grad_rows, hid), F32)],
        compiler_params=params(),
        cost_estimate=cost(13.0),
        name="turn",
    )(info, *field, *ws, targets, area, *wt, dep, *last)


def bottom_call(info, chunk, half, field, weights, pre, gm, gs, dep, before):
    dims = field[0].shape[1:]
    lon_t, lat_t, chans = dims
    cells = lon_t * lat_t
    hid = weights["mid"].shape[0]
    wt = [weights[k] for k in ("midt", "dect")]
    grad_rows = grad_layout(chans, hid)[-1]
    more = before is not None
    last = [before] if more else []
    grads, sums = back_scratch(dims, hid)
    return pl.pallas_call(
        functools.partial(bottom_kernel, more),
        grid_spec=grid_of(
            HALF,
            field_specs(field, chunk, half, True)
            + [snap_spec(v.shape[1:]) for v in (*pre, *gm, gs)]
            + [whole(w.shape) for w in wt]
            + [any_spec()]
            + [whole(w.shape) for w in last],
            whole((grad_rows, hid)),
            [
                pltpu.VMEM((cells, 10 * chans), BF16),
                pltpu.VMEM(dims, F32),
                pltpu.VMEM((cells, hid), BF16),
                pltpu.VMEM((cells, hid), BF16),
            ]
            + grads
            + sums,
        ),
        out_shape=shape_of((grad_rows, hid), F32),
        compiler_params=params(),
        cost_estimate=cost(8.0),
        name="bottom",
    )(info, *field, *pre, *gm, gs, *wt, dep, *last)


def three_parts(vec):
    high = lax.reduce_precision(vec, 8, 7)
    rest = vec - high
    mid = lax.reduce_precision(rest, 8, 7)
    low = lax.reduce_precision(rest - mid, 8, 7)
    return jnp.stack([high, mid, low], axis=-2)


def layer_weights(enc, mid, dec, vec):
    taps, chans, hid = enc.shape
    parts = jnp.concatenate([three_parts(vec[hid : 2 * hid]), three_parts(vec[:hid])], axis=0)
    parts = jnp.pad(parts, ((0, chans - 6), (0, 0)))
    w1 = jnp.concatenate([enc.reshape(taps * chans, hid), parts], axis=0).astype(BF16)
    pad = jnp.zeros((hid - chans,), F32)
    bias = jnp.stack([vec[2 * hid : 3 * hid], jnp.concatenate([vec[3 * hid :], pad])])
    return {
        "w1": w1,
        "mid": mid.astype(BF16),
        "dec": dec.astype(BF16),
        "bias": bias,
        "w1t": jnp.transpose(enc, (2, 0, 1)).reshape(hid, taps * chans).astype(BF16),
        "midt": mid.T.astype(BF16),
        "dect": dec.T.astype(BF16),
    }


def reduce_all(part):
    lon_n = lax.axis_size("lon")
    me = lax.axis_index("lon")

    def over(stride):
        return "lon", (me // stride) % 2, [(i, i ^ stride) for i in range(lon_n)]

    stages = [over(1), over(2), ("lat", lax.axis_index("lat"), [(0, 1), (1, 0)]), over(8)]
    for axis, bit, perm in stages:
        half = part.shape[0] // 2
        give = lax.dynamic_slice_in_dim(part, (1 - bit) * half, half)
        mine = lax.dynamic_slice_in_dim(part, bit * half, half)
        part = mine + lax.ppermute(give, axis, perm)
    axis, _, perm = over(4)
    part = part + lax.ppermute(part, axis, perm)
    for axis, bit, perm in reversed(stages):
        got = lax.ppermute(part, axis, perm)
        part = jnp.concatenate([jnp.where(bit == 0, part, got), jnp.where(bit == 0, got, part)])
    return part


def fast_grads(states, targets, sea_temp, ocean, valid, w_enc, w_mid, w_dec, biases):
    pool, lon_t, lat_t, chans = states.shape
    lon_n, lat_n = lax.axis_size("lon"), lax.axis_size("lat")
    nlon, nlat = lon_t * lon_n, lat_t * lat_n
    zonal, forward, inverse, area_all = host_tables(nlon, nlat, 88)
    hemi = lax.axis_index("lat")
    info = hemi[None].astype(jnp.int32)
    flip = np.concatenate([np.arange(lat_t, nlat), np.arange(lat_t)])
    flip2 = np.concatenate([flip, nlat + flip])
    ends = (np.arange(0, nlon, lon_t)[None, :] + np.array([[-1], [lon_t]])).reshape(-1) % nlon
    zonal_in = jnp.asarray(np.concatenate([zonal, zonal[:, ends]], axis=1))
    zonal_out = jnp.asarray(
        np.concatenate([zonal[:nlon], zonal[:nlon][ends], zonal[nlon:], zonal[nlon:][ends]], axis=0)
    )
    forward = jnp.where(hemi == 0, jnp.asarray(forward), jnp.asarray(forward[:, flip]))
    inverse = jnp.where(hemi == 0, jnp.asarray(inverse), jnp.asarray(inverse[flip2]))
    side = jnp.stack([hemi == 1, hemi == 0]).astype(F32)
    masks = jnp.broadcast_to(side[:, None], (2, chans))
    area = lax.dynamic_slice_in_dim(jnp.asarray(area_all, F32), hemi * lat_t, lat_t)
    area_wide = jnp.broadcast_to(area[:, None], (lat_t, chans))
    up = [(i, (i + 1) % lon_n) for i in range(lon_n)]
    down = [(t, s) for s, t in up]
    swap = [(0, 1), (1, 0)]
    chunks = range(pool // CHUNK)

    traded = [
        lax.ppermute(lax.dynamic_slice_in_dim(states, first_of(c, 1, info), HALF), "lat", swap)
        for c in chunks
    ]
    def inner_row(column):
        return jnp.where(hemi == 0, column[..., -1:, :], column[..., 0:1, :])

    def edge_rows(row, lo, hi):
        return lax.ppermute(jnp.concatenate([row, inner_row(lo), inner_row(hi)], axis=1), "lat", swap)

    lo0, hi0 = lax.ppermute(states[:, -1], "lon", up), lax.ppermute(states[:, 0], "lon", down)
    rows0 = edge_rows(inner_row(states)[:, :, 0], lo0, hi0)
    sea = ocean.astype(F32) * sea_temp.astype(F32)
    cells = lon_t * lat_t
    lane = jnp.arange(chans)
    wide_sea = sea.reshape(pool, cells, 1).astype(BF16)
    wide_valid = valid.reshape(pool, cells, 1).astype(BF16)
    extra = jnp.where(lane < 3, wide_sea, jnp.where(lane < 6, jnp.ones((), BF16), wide_valid))
    extra = jnp.where(lane < 7, extra, jnp.zeros((), BF16))
    layers = [layer_weights(w_enc[i], w_mid[i], w_dec[i], biases[i]) for i in range(2)]

    last = [forward]

    def then(result, pick=None):
        last[0] = result if pick is None else result[pick]
        return result

    def over_lon(spec):
        return lax.all_to_all(spec, "lon", split_axis=0, concat_axis=0, tiled=True)

    class Chunk:
        def __init__(self, c):
            self.c = c
            self.early = 0
            self.round = 0
            self.other = traded[c]
            self.field0, self.pres = [None, None], [None, None]
            self.low, self.s_ext, self.gm = [None, None], [None, None], [None, None]
            self.fresh, self.edge, self.row = [None, None], [None, None], [None, None]
            self.back, self.beyond = [None, None], [None, None]

        def legendre(self):
            half = self.early
            own = states if self.round == 0 else self.low[half]
            there = self.c if self.round == 0 else None
            got = legendre_call(
                info, own, there, half, self.other, forward, last[0], self.round == 2
            )
            self.spec = over_lon(then(got))

        def zonal(self):
            table = zonal_in if self.round == 2 else zonal_out
            self.spec = over_lon(then(zonal_call(self.spec, table, last[0], self.round == 2)))

        def synthesis(self):
            got = synthesis_call(info, self.spec, inverse, HALF, self.round < 2, last[0])
            own, send = then(got, 0)
            self.s_ext[self.early] = own
            self.s_ext[1 - self.early] = lax.ppermute(send, "lat", swap)

        def forward(self, late):
            half = self.early ^ late
            field = (states, self.s_ext[half], rows0, lo0, hi0, extra, masks)
            self.field0[half] = field
            got = forward_call(info, self.c, half, field, layers[0], last[0])
            fresh, low, row, to_up, to_down, *pre = then(got, 1)
            self.fresh[half], self.low[half], self.pres[half] = fresh, low, pre
            self.send(half, late)
            lo, hi = lax.ppermute(to_up, "lon", up), lax.ppermute(to_down, "lon", down)
            self.edge[half] = (lo, hi)
            self.row[1 - half] = edge_rows(row, lo, hi)

        def turn(self, late, before):
            half = self.early ^ late
            field = (self.fresh[half], self.s_ext[half], self.row[half], *self.edge[half], extra, masks)
            got = turn_call(info, self.c, half, field, layers[1], targets, area_wide, last[0], before)
            gm, low, to_lo, to_hi, rows, before = then(got, 1)
            self.low[half] = low
            self.send(half, late)
            from_lo, from_hi = lax.ppermute(to_hi, "lon", up), lax.ppermute(to_lo, "lon", down)
            self.back[half] = (gm, from_lo, from_hi)
            rows = rows[:, :lon_t]
            place = jnp.arange(lon_t)[:, None]
            rows = rows + jnp.where(place == 0, from_lo[:, lat_t : lat_t + 1].astype(F32), 0.0)
            rows = rows + jnp.where(place == lon_t - 1, from_hi[:, lat_t : lat_t + 1].astype(F32), 0.0)
            self.beyond[1 - half] = lax.ppermute(rows, "lat", swap)
            return before

        def send(self, half, late):
            if not late:
                self.other = lax.ppermute(self.low[half], "lat", swap)

        def flip(self):
            self.early = 1 - self.early
            self.round += 1

        def bottom(self, late, before):
            half = self.early ^ late
            gm = (*self.back[half], self.beyond[half])
            got = bottom_call(
                info, self.c, half, self.field0[half], layers[0], self.pres[half], gm,
                self.s_ext[half], last[0], before,
            )
            return then(got)

    a, b = (Chunk(c) for c in chunks)
    top, low = None, None
    a.legendre()
    a.zonal()
    b.legendre()
    for one, two in ((a, b), (b, a)):
        one.synthesis()
        one.forward(0)
        two.zonal()
        one.forward(1)
        one.flip()
        one.legendre()
    for one, two in ((a, b), (b, a)):
        one.synthesis()
        top = one.turn(0, top)
        two.zonal()
        top = one.turn(1, top)
        one.flip()
        one.legendre()
    upper = reduce_all(top)
    a.synthesis()
    low = a.bottom(0, low)
    b.zonal()
    low = a.bottom(1, low)
    b.synthesis()
    low = b.bottom(0, low)
    low = b.bottom(1, low)
    return reduce_all(low), upper


def update_kernel(
    rate, pick_ref, g0_ref, g1_ref, v_ref, *refs,
):
    ins, outs = refs[:12], refs[12:]
    layer, part = pl.program_id(0), pl.program_id(1)
    chans = ins[0].shape[2]
    hid = ins[0].shape[3]
    scale = 1.0 / v_ref[1, 4:5, 0:1]
    one, two, three, _ = grad_layout(chans, hid)

    def apply(group, at, grad):
        w_ref, m_ref, a_ref = (ins[4 * i + group] for i in range(3))
        new_ref, mom_ref, avg_ref, copy_ref = (outs[4 * i + group] for i in range(4))
        scaled = grad * scale
        mom = MOMENTUM * m_ref[at] + scaled
        fresh = w_ref[at] - rate * (scaled + MOMENTUM * mom)
        new_ref[at] = fresh
        mom_ref[at] = mom
        avg_ref[at] = AVERAGE * a_ref[at] + (1.0 - AVERAGE) * fresh
        copy_ref[at] = fresh.astype(BF16)

    def layer_step(g_ref):
        for tap in range(3):
            rows = pl.ds(pl.multiple_of((part * 3 + tap) * chans, chans), chans)
            apply(0, (0, tap), g_ref[rows].astype(F32))

        @pl.when(part == 0)
        def _():
            apply(1, (0,), g_ref[one:two].astype(F32))
            apply(2, (0,), g_ref[two:three].astype(F32).T)

    pl.when(layer == 0)(lambda: layer_step(g0_ref))
    pl.when(layer == 1)(lambda: layer_step(g1_ref))

    @pl.when((layer == 0) & (part == 0))
    def _():
        for i in range(2):
            for r in range(4):
                wide = hid if r < 3 else chans
                at = (slice(i, i + 1), slice(r * hid, r * hid + wide))
                apply(3, at, v_ref[i, r : r + 1, :wide])


def update_call(rate, sums, arrays):
    w_enc, w_mid, w_dec, biases = arrays[:4]
    layers, taps, chans, hid = w_enc.shape
    three = grad_layout(chans, hid)[2]
    vecs = jnp.stack([s[three : three + 8].astype(F32) for s in sums])
    enc = pl.BlockSpec((1, taps // 3, chans, hid), lambda i, p, pick: (i, p, 0, 0))
    mid = pl.BlockSpec((1, hid, hid), lambda i, p, pick: (i, 0, 0))
    dec = pl.BlockSpec((1, hid, chans), lambda i, p, pick: (i, 0, 0))
    bias = whole(biases.shape)
    specs = [enc, mid, dec, bias]
    shapes = [w_enc.shape, w_mid.shape, w_dec.shape, biases.shape]
    got = pl.pallas_call(
        functools.partial(update_kernel, rate),
        grid_spec=pltpu.PrefetchScalarGridSpec(
            num_scalar_prefetch=1,
            grid=(layers, 3),
            in_specs=[whole(sums[0].shape), whole(sums[1].shape), whole(vecs.shape)]
            + specs * 3,
            out_specs=specs * 4,
        ),
        out_shape=[shape_of(s, F32) for s in shapes * 3] + [shape_of(s, BF16) for s in shapes],
        compiler_params=params(),
        cost_estimate=cost(8.0),
        name="update",
    )(jnp.zeros((1,), jnp.int32), sums[0], sums[1], vecs, *arrays)
    return (jnp.sum(vecs[1, 3, chans:]), vecs[1, 4, 0], *got)


def fits(states, w_mid, lon_n, lat_n):
    pool, lon_t, lat_t, chans = states.shape
    return (
        lat_n == 2
        and lon_n == 16
        and lon_t == 16
        and lat_t == 64
        and pool == 2 * CHUNK
        and chans == 128
        and w_mid.shape[1] == 2 * chans
        and w_mid.shape[0] == 2
    )


def with_halo(block, sides, width, periodic):
    for axis, dim in sides:
        count = lax.axis_size(axis)
        forward = [(i, i + 1) for i in range(count - 1)]
        if periodic:
            forward.append((count - 1, 0))
        backward = [(target, source) for source, target in forward]
        low = lax.ppermute(
            lax.slice_in_dim(block, block.shape[dim] - width, None, axis=dim), axis, forward
        )
        high = lax.ppermute(lax.slice_in_dim(block, 0, width, axis=dim), axis, backward)
        block = jnp.concatenate([low, block, high], axis=dim)
    return block


def tables(nlon, nlat, groups):
    coeffs = jnp.arange(2 * MW)
    wave = jnp.where(coeffs < MW, coeffs, coeffs - MW + 1).astype(jnp.float32)
    places = jnp.arange(nlon).astype(jnp.float32)
    angle = 2.0 * math.pi * wave[:, None] * places[None, :] / nlon
    fourier = jnp.where((coeffs < MW)[:, None], jnp.cos(angle), jnp.sin(angle)) * math.sqrt(
        2.0 / nlon
    )
    phase = ((jnp.arange(nlat).astype(jnp.float32) + 0.5) / nlat - 0.5) * math.pi
    sine = jnp.sin(phase)
    quad = jnp.cos(phase) * math.pi / nlat
    polys = [jnp.ones_like(sine), sine]
    for degree in range(1, NDEG - 1):
        polys.append(((2 * degree + 1) * sine * polys[-1] - degree * polys[-2]) / (degree + 1))
    stacked = jnp.stack(polys[:NDEG])
    degrees = jnp.arange(NDEG).astype(jnp.float32)
    legendre = jnp.sqrt((2 * degrees + 1) / 2)[:, None] * jnp.sqrt(quad)[None, :] * stacked
    damping = 1.5 * (1.0 - 2.0 * degrees * (degrees + 1) / (NDEG * (NDEG + 1)))
    filters = damping[None, :] * (1.0 - 0.5 * wave / MW)[:, None]
    kept = 2 * MW
    slots = (kept + groups - 1) // groups * groups
    fourier = jnp.pad(fourier, ((0, slots - kept), (0, 0)))
    filters = jnp.pad(filters, ((0, slots - kept), (0, 0)))
    return (fourier, legendre, filters)


def spectral(values, tabs):
    fourier, legendre, filters = tabs
    cycles = lax.all_to_all(
        values.astype(jnp.bfloat16), "lon", split_axis=3, concat_axis=1, tiled=True
    ).astype(values.dtype)
    coeff = jnp.einsum("kx,sxjc->skjc", fourier, cycles, precision=HIGH)
    block = fourier.shape[0] // lax.axis_size("lat")
    where = lax.axis_index("lat")
    block_filter = lax.dynamic_slice_in_dim(filters, where * block, block, 0)
    columns = lax.all_to_all(
        coeff.astype(jnp.bfloat16), "lat", split_axis=1, concat_axis=2, tiled=True
    ).astype(coeff.dtype)
    spec = (
        jnp.einsum("nj,skjc->sknc", legendre, columns, precision=HIGH)
        * block_filter[None, :, :, None]
    )
    back = jnp.einsum("nj,sknc->skjc", legendre, spec, precision=HIGH)
    coeff_back = lax.all_to_all(
        back.astype(jnp.bfloat16), "lat", split_axis=2, concat_axis=1, tiled=True
    ).astype(back.dtype)
    grid = jnp.einsum("kx,skjc->sxjc", fourier, coeff_back, precision=HIGH)
    return lax.all_to_all(
        grid.astype(jnp.bfloat16), "lon", split_axis=1, concat_axis=3, tiled=True
    ).astype(grid.dtype)


def extend(field):
    wider = with_halo(field, (("lon", 1),), 1, True)
    return with_halo(wider, (("lat", 2),), 1, False)


def neighbours(padded, flipped, lon_t, lat_t):
    parts = []
    for row_off in range(3):
        for col_off in range(3):
            first = 2 - row_off if flipped else row_off
            second = 2 - col_off if flipped else col_off
            parts.append(padded[:, first : first + lon_t, second : second + lat_t])
    stacked = jnp.stack(parts, axis=3)
    return stacked.reshape(-1, 9 * padded.shape[-1])


def gelu_fn(value):
    return jax.nn.gelu(value, approximate=True)


def gelu_back(value, grad):
    return jax.vjp(gelu_fn, value)[1](grad)[0]


def layer_forward(state, sea, enc, mid, dec, vec, tabs):
    hid = mid.shape[0]
    lon_t, lat_t = (state.shape[1], state.shape[2])
    moved = state + spectral(state, tabs)
    patches = neighbours(extend(moved.astype(jnp.bfloat16)), False, lon_t, lat_t)
    pre1 = jnp.dot(patches, enc, preferred_element_type=jnp.float32)
    pre1 = pre1 + sea.reshape(-1, 1) * vec[hid : 2 * hid] + vec[:hid]
    active1 = gelu_fn(pre1).astype(jnp.bfloat16)
    pre2 = jnp.dot(active1, mid, preferred_element_type=jnp.float32) + vec[2 * hid : 3 * hid]
    active2 = gelu_fn(pre2).astype(jnp.bfloat16)
    output = jnp.dot(active2, dec, preferred_element_type=jnp.float32) + vec[3 * hid :]
    return (moved + output.reshape(state.shape), (patches, pre1, active1, pre2, active2))


def layer_backward(grad_state, sea, enc, mid, dec, saved, tabs):
    patches, pre1, active1, pre2, active2 = saved
    hid = mid.shape[0]
    shape = grad_state.shape
    chans = shape[-1]
    g_out = grad_state.reshape(-1, chans).astype(jnp.bfloat16)
    g_dec = jnp.einsum("rh,rc->hc", active2, g_out, preferred_element_type=jnp.float32)
    g_act2 = jnp.einsum("rc,hc->rh", g_out, dec, preferred_element_type=jnp.float32)
    g_pre2 = gelu_back(pre2, g_act2).astype(jnp.bfloat16)
    g_mid = jnp.einsum("rh,rg->hg", active1, g_pre2, preferred_element_type=jnp.float32)
    g_act1 = jnp.einsum("rg,hg->rh", g_pre2, mid, preferred_element_type=jnp.float32)
    g_pre1 = gelu_back(pre1, g_act1).astype(jnp.bfloat16)
    g_enc = jnp.einsum("rk,rh->kh", patches, g_pre1, preferred_element_type=jnp.float32)
    wide1 = g_pre1.astype(jnp.float32)
    g_vec = jnp.concatenate(
        [
            jnp.sum(wide1, 0),
            jnp.sum(sea.reshape(-1, 1) * wide1, 0),
            jnp.sum(g_pre2.astype(jnp.float32), 0),
            jnp.sum(g_out.astype(jnp.float32), 0),
        ]
    )
    spread = extend(g_pre1.reshape(shape[0], shape[1], shape[2], hid))
    gathered = neighbours(spread, True, shape[1], shape[2]).reshape(-1, 9, hid)
    g_input = jnp.einsum(
        "rkh,kch->rc", gathered, enc.reshape(9, chans, hid), preferred_element_type=jnp.float32
    )
    grad_moved = grad_state + g_input.reshape(shape)
    return (grad_moved + spectral(grad_moved, tabs), (g_enc, g_mid, g_dec, g_vec))


def general_grads(states, targets, sea_temp, ocean, valid, order, w_enc, w_mid, w_dec, biases):
    pool, lon_t, lat_t, chans = states.shape
    layers, hid = (w_mid.shape[0], w_mid.shape[1])
    nlon = lon_t * lax.axis_size("lon")
    nlat = lat_t * lax.axis_size("lat")
    tabs = tables(nlon, nlat, lax.axis_size("lat"))
    lat_glob = (lax.axis_index("lat") * lat_t + jnp.arange(lat_t)).astype(jnp.float32)
    area = jnp.cos(((lat_glob + 0.5) / nlat - 0.5) * math.pi)
    enc_low = w_enc.astype(jnp.bfloat16).reshape(layers, 9 * chans, hid)
    mid_low = w_mid.astype(jnp.bfloat16)
    dec_low = w_dec.astype(jnp.bfloat16)
    snaps = pool // MB
    sums = [
        jnp.zeros((layers, 9 * chans, hid), jnp.float32),
        jnp.zeros_like(w_mid),
        jnp.zeros_like(w_dec),
        jnp.zeros_like(biases),
    ]
    loss = jnp.zeros((), jnp.float32)
    total = jnp.zeros((), jnp.float32)
    for batch_id in range(MB):
        picks = lax.dynamic_slice_in_dim(order, batch_id * snaps, snaps)
        state = jnp.take(states, picks, axis=0).astype(jnp.float32)
        target = jnp.take(targets, picks, axis=0).astype(jnp.float32)
        sea = jnp.take(ocean, picks, axis=0).astype(jnp.float32) * jnp.take(
            sea_temp, picks, axis=0
        ).astype(jnp.float32)
        weight = jnp.take(valid, picks, axis=0).astype(jnp.float32) * area[None, None, :]
        kept = []
        for layer_id in range(layers):
            state, saved = layer_forward(
                state,
                sea,
                enc_low[layer_id],
                mid_low[layer_id],
                dec_low[layer_id],
                biases[layer_id],
                tabs,
            )
            kept.append(saved)
        diff = state - target
        loss = loss + jnp.sum(weight[..., None] * diff * diff)
        total = total + jnp.sum(weight)
        grad_state = 2.0 * weight[..., None] * diff
        for layer_id in reversed(range(layers)):
            grad_state, found = layer_backward(
                grad_state,
                sea,
                enc_low[layer_id],
                mid_low[layer_id],
                dec_low[layer_id],
                kept[layer_id],
                tabs,
            )
            sums = [acc.at[layer_id].add(part) for acc, part in zip(sums, found)]
    g_enc, g_mid, g_dec, g_vec, loss, total = lax.psum(
        (sums[0], sums[1], sums[2], sums[3], loss, total), ("lon", "lat")
    )
    return g_enc.reshape(w_enc.shape), g_mid, g_dec, g_vec, loss, total


def body(
    states,
    targets,
    sea_temp,
    ocean,
    valid,
    order,
    w_enc,
    w_mid,
    w_dec,
    biases,
    mom_enc,
    mom_mid,
    mom_dec,
    mom_bias,
    avg_enc,
    avg_mid,
    avg_dec,
    avg_bias,
):
    pool, lon_t, lat_t = states.shape[:3]
    lon_n, lat_n = lax.axis_size("lon"), lax.axis_size("lat")
    rate = RATE_BASE * math.sqrt(pool * lon_t * lon_n * lat_t * lat_n)
    if fits(states, w_mid, lon_n, lat_n):
        sums = fast_grads(states, targets, sea_temp, ocean, valid, w_enc, w_mid, w_dec, biases)
        arrays = (w_enc, w_mid, w_dec, biases, mom_enc, mom_mid, mom_dec, mom_bias)
        arrays += (avg_enc, avg_mid, avg_dec, avg_bias)
        return update_call(rate, sums, arrays)
    found = general_grads(
        states, targets, sea_temp, ocean, valid, order, w_enc, w_mid, w_dec, biases
    )
    loss, total = found[4:]
    grads = (found[0].reshape(w_enc.shape),) + found[1:4]
    news, moms, avgs, copies = ([], [], [], [])
    for weight_now, grad, mom, avg in zip(
        (w_enc, w_mid, w_dec, biases),
        grads,
        (mom_enc, mom_mid, mom_dec, mom_bias),
        (avg_enc, avg_mid, avg_dec, avg_bias),
    ):
        scaled = grad / total
        mom_new = MOMENTUM * mom + scaled
        fresh = weight_now - rate * (scaled + MOMENTUM * mom_new)
        news.append(fresh)
        moms.append(mom_new)
        avgs.append(AVERAGE * avg + (1.0 - AVERAGE) * fresh)
        copies.append(fresh.astype(jnp.bfloat16))
    return (
        loss,
        total,
        news[0],
        news[1],
        news[2],
        news[3],
        moms[0],
        moms[1],
        moms[2],
        moms[3],
        avgs[0],
        avgs[1],
        avgs[2],
        avgs[3],
        copies[0],
        copies[1],
        copies[2],
        copies[3],
    )


def solution(mesh):
    placed = (
        P(None, "lon", "lat", None),
        P(None, "lon", "lat", None),
        P(None, "lon", "lat"),
        P(None, "lon", "lat"),
        P(None, "lon", "lat"),
        P(),
        P(),
        P(),
        P(),
        P(),
        P(),
        P(),
        P(),
        P(),
        P(),
        P(),
        P(),
        P(),
    )
    return jax.shard_map(
        body,
        mesh=mesh,
        in_specs=placed,
        out_specs=(
            P(),
            P(),
            P(),
            P(),
            P(),
            P(),
            P(),
            P(),
            P(),
            P(),
            P(),
            P(),
            P(),
            P(),
            P(),
            P(),
            P(),
            P(),
        ),
        check_vma=False,
    )
```

```python
import functools
import math

import jax
import jax.numpy as jnp
import numpy as np
from jax import lax
from jax.experimental import pallas as pl
from jax.experimental.pallas import tpu as pltpu
from jax.sharding import PartitionSpec as P

MW = 86
NDEG = 86
MB = 4


HIGH = lax.Precision.HIGHEST
MOMENTUM = 0.9
AVERAGE = 0.99
RATE_BASE = 0.0006

F32 = jnp.float32
BF16 = jnp.bfloat16
CHUNK = 4
VMEM = 56 * 1024 * 1024
GELU_A = math.sqrt(2.0 / math.pi)
GELU_B = 0.044715


def split_table(table):
    table = np.asarray(table, np.float32)
    high = table.astype(BF16)
    low = (table - high.astype(np.float32)).astype(BF16)
    return np.concatenate([high, low], axis=0)


def host_tables(nlon, nlat, deg):
    kept = np.arange(2 * MW)
    wave = np.where(kept < MW, kept, kept - MW + 1).astype(np.float64)
    angle = 2.0 * np.pi * wave[:, None] * np.arange(nlon)[None, :] / nlon
    fourier = np.where((kept < MW)[:, None], np.cos(angle), np.sin(angle)) * np.sqrt(2.0 / nlon)
    zonal = (fourier * (1.0 - 0.5 * wave / MW)[:, None]).T @ fourier
    phase = ((np.arange(nlat) + 0.5) / nlat - 0.5) * np.pi
    sine, area = np.sin(phase), np.cos(phase)
    polys = [np.ones_like(sine), sine]
    for n in range(1, NDEG - 1):
        polys.append(((2 * n + 1) * sine * polys[-1] - n * polys[-2]) / (n + 1))
    degrees = np.arange(NDEG)
    legendre = np.sqrt((2 * degrees + 1) / 2)[:, None] * np.sqrt(area * np.pi / nlat)[None, :]
    legendre = legendre * np.stack(polys)
    damping = 1.5 * (1.0 - 2.0 * degrees * (degrees + 1) / (NDEG * (NDEG + 1)))
    forward = np.zeros((deg, nlat))
    forward[:NDEG] = legendre
    inverse = np.zeros((nlat, -(-deg // 32) * 32))
    inverse[:, :NDEG] = (legendre * damping[:, None]).T
    return split_table(zonal), split_table(forward), split_table(inverse), area


def mm(a, b):
    return jnp.dot(a, b, preferred_element_type=F32)


def mm_rows(a, b):
    return lax.dot_general(a, b, (((0,), (0,)), ((), ())), preferred_element_type=F32)


def whole(shape):
    return pl.BlockSpec(shape, lambda *_: (0,) * len(shape))


def params():
    return pltpu.CompilerParams(vmem_limit_bytes=VMEM)


HALF = CHUNK // 2


def any_spec():
    return pl.BlockSpec(memory_space=pl.ANY)


def shape_of(dims, dtype):
    return jax.ShapeDtypeStruct(dims, dtype)


def grid_of(count, in_specs, out_specs, scratch):
    return pltpu.PrefetchScalarGridSpec(
        num_scalar_prefetch=1,
        grid=(count,),
        in_specs=in_specs,
        out_specs=out_specs,
        scratch_shapes=scratch,
    )


def first_of(chunk, half, info):
    if chunk is None:
        return 0
    return chunk * CHUNK + HALF * (info[0] if half == 0 else 1 - info[0])


def snap_spec(dims, chunk=None, half=0):
    return pl.BlockSpec(
        (1,) + dims, lambda g, info: (first_of(chunk, half, info) + g,) + (0,) * len(dims)
    )


def pick_kernel(info, x_ref, *refs):
    refs[-1][...] = x_ref[...]


def pick_call(info, fields, chunk, half, deps):
    dims = fields.shape[1:]
    return pl.pallas_call(
        pick_kernel,
        grid_spec=grid_of(
            HALF, [snap_spec(dims, chunk, half)] + [any_spec()] * len(deps), snap_spec(dims), []
        ),
        out_shape=shape_of((HALF,) + dims, fields.dtype),
        compiler_params=params(),
        cost_estimate=cost(1.0),
        name="pick",
    )(info, fields, *deps)


def legendre_kernel(
    wide, info, own_ref, other_ref, first_ref, last_ref, l_ref, *refs
):
    o_ref, up_ref, down_ref, rows_ref, tmp = refs[-5:]
    parts, rows, lon_t, chans = o_ref.shape
    lat_t = own_ref.shape[2]
    deg = l_ref.shape[0] // 2
    count = lon_t + 2 if wide else lon_t
    each = deg // parts
    place = lax.broadcasted_iota(jnp.int32, (lat_t, chans), 0)
    south = info[0] == 1
    inner = place == jnp.where(south, 0, lat_t - 1)
    other_inner = place == jnp.where(south, lat_t - 1, 0)

    def column(x):
        own, other = own_ref[0, x], other_ref[0, x]
        if wide:
            to_own = other_ref[0, count, x : x + 1].astype(F32)
            to_other = own_ref[0, count, x : x + 1].astype(F32)
            own = (own.astype(F32) + jnp.where(inner, to_own, 0.0)).astype(BF16)
            other = (other.astype(F32) + jnp.where(other_inner, to_other, 0.0)).astype(BF16)
        else:
            own_f, other_f = own.astype(F32), other.astype(F32)
            ends = [(own_f[:1], own_f[lat_t - 1 :]), (other_f[lat_t - 1 :], other_f[:1])]
            for i, (if_south, if_north) in enumerate(ends):
                rows_ref[0, i, x : x + 1] = jnp.where(south, if_south, if_north)
        return jnp.concatenate([own, other], axis=0)

    for base in range(0, count, 4):
        span = range(base, min(base + 4, count))
        r = mm(l_ref[...], jnp.concatenate([column(x) for x in span], axis=1))
        r = r[:deg] + r[deg:]
        for x in span:
            tmp[:, x, :] = r[:, (x - base) * chans : (x - base + 1) * chans]
    o_ref[:, :each] = tmp[:, :lon_t, :].astype(BF16).reshape(parts, each, lon_t, chans)
    if wide:
        rest = jnp.zeros((lon_t - each, chans), F32)
        for p in range(parts):
            for side in range(2):
                edge = tmp[p * each : (p + 1) * each, lon_t + side, :]
                o_ref[p, each + side] = jnp.concatenate([edge, rest], axis=0).astype(BF16)
        rows_ref[...] = jnp.zeros_like(rows_ref)
    for ref, late_ref, x in ((down_ref, first_ref, 0), (up_ref, last_ref, lon_t - 1)):
        if wide:
            at = lon_t if x == 0 else lon_t + 1
            corner, far = other_ref[0, count, at : at + 1], own_ref[0, count, at : at + 1]
            pieces = [jnp.broadcast_to(v.astype(F32), (8, chans)) for v in (corner, far)]
        else:
            at = x
            pieces = [jnp.broadcast_to(rows_ref[0, 1, x : x + 1], (16, chans))]
        ref[0, 0, :lat_t] = own_ref[0, at]
        ref[0, 0, lat_t:] = jnp.concatenate(pieces, axis=0).astype(BF16)
        ref[0, 1, :lat_t] = late_ref[0, 0]
        ref[0, 1, lat_t:] = jnp.zeros((16, chans), BF16)


def legendre_call(info, own, late, chunk, half, other, table, deps, wide):
    snaps, slabs, lat_t, chans = other.shape
    deg = table.shape[0] // 2
    parts = 8
    lon_t = slabs - 3 if wide else slabs
    rows = deg // parts + (2 if wide else 0)
    message = (2, lat_t + 16, chans)
    sides = (2, lon_t, chans)

    def late_column(x):
        return pl.BlockSpec(
            (1, 1, lat_t, chans), lambda g, info: (first_of(chunk, 1 - half, info) + g, x, 0, 0)
        )

    columns = (lon_t, lon_t + 1) if wide else (0, lon_t - 1)
    return pl.pallas_call(
        functools.partial(legendre_kernel, wide),
        grid_spec=grid_of(
            snaps,
            [
                snap_spec(own.shape[1:], chunk, half),
                snap_spec(other.shape[1:]),
                late_column(columns[0]),
                late_column(columns[1]),
                whole(table.shape),
            ]
            + [any_spec()] * len(deps),
            [
                pl.BlockSpec((parts, rows, lon_t, chans), lambda s, info: (s, 0, 0, 0)),
                snap_spec(message),
                snap_spec(message),
                snap_spec(sides),
            ],
            [pltpu.VMEM((deg, lon_t + 8 if wide else lon_t, chans), F32)],
        ),
        out_shape=[
            shape_of((snaps * parts, rows, lon_t, chans), BF16),
            shape_of((snaps,) + message, BF16),
            shape_of((snaps,) + message, BF16),
            shape_of((snaps,) + sides, F32),
        ],
        compiler_params=params(),
        cost_estimate=cost(3.4),
        name="legendre",
    )(info, own, other, late, late, table, *deps)


def zonal_kernel(wide_in, x_ref, a_ref, *refs):
    o_ref, tmp = refs[-2:]
    groups, _, lon_t, chans = x_ref.shape
    nlon = groups * lon_t
    rows = min(x_ref.shape[1], o_ref.shape[1])
    if wide_in:
        for side in range(2):
            tmp[side * groups : (side + 1) * groups] = x_ref[:, rows + side].astype(F32)
    else:
        tmp[...] = jnp.zeros_like(tmp)
    for base in range(0, rows, 4):
        span = range(base, min(base + 4, rows))
        fields = jnp.concatenate([x_ref[:, n].reshape(nlon, chans) for n in span], axis=1)
        if wide_in:
            edges = jnp.concatenate([tmp[:, n, :] for n in span], axis=1).astype(BF16)
            r = mm(a_ref[:, :nlon], fields) + mm(a_ref[:, nlon:], edges)
            r = r[:nlon] + r[nlon:]
        else:
            r = mm(a_ref[...], fields)
            size = r.shape[0] // 2
            r = r[:size] + r[size:]
        low = r[:nlon].astype(BF16)
        for n in span:
            lanes = slice((n - base) * chans, (n - base + 1) * chans)
            o_ref[:, n] = low[:, lanes].reshape(groups, lon_t, chans)
            if not wide_in:
                tmp[:, n, :] = r[nlon:, lanes]
    if not wide_in:
        for side in range(2):
            o_ref[:, rows + side] = tmp[side * groups : (side + 1) * groups].astype(BF16)


def zonal_call(fields, table, deps, wide_in):
    groups, rows, lon_t, chans = fields.shape
    out = (groups, rows - 2 if wide_in else rows + 2, lon_t, chans)
    return pl.pallas_call(
        functools.partial(zonal_kernel, wide_in),
        in_specs=[pl.BlockSpec(memory_space=pltpu.VMEM)] * 2 + [any_spec()] * len(deps),
        out_specs=pl.BlockSpec(memory_space=pltpu.VMEM),
        out_shape=shape_of(out, BF16),
        scratch_shapes=[pltpu.VMEM((2 * groups, lon_t, chans), F32)],
        compiler_params=params(),
        cost_estimate=cost(2.8),
        name="zonal",
    )(fields, table, *deps)


def synthesis_kernel(wide, info, x_ref, lo_ref, hi_ref, l_ref, *refs):
    rows_refs = refs[: 1 if wide else 2]
    own_ref, send_ref, tmp, side = refs[-4:]
    parts, rows, lon_t, chans = x_ref.shape
    each = rows - 2 if wide else rows
    deg = parts * each
    count = lon_t + 2 if wide else lon_t
    nlat = l_ref.shape[0] // 2
    half = nlat // 2
    south = info[0] == 1
    tmp[:deg, :lon_t, :] = x_ref[:, :each].reshape(deg, lon_t, chans).astype(F32)
    if wide:
        for p in range(parts):
            for e in range(2):
                tmp[p * each : (p + 1) * each, lon_t + e, :] = x_ref[p, each + e, :each].astype(F32)
    tmp[deg:] = jnp.zeros((tmp.shape[0] - deg,) + tmp.shape[1:], F32)
    side[...] = jnp.zeros_like(side)
    low, high = lo_ref[0, 0].astype(F32), hi_ref[0, 0].astype(F32)
    if wide:
        sides_ref = rows_refs[0]
        for i in range(2):
            side[i, :lon_t] = sides_ref[0, 1 - i]
        for at, edge in ((lon_t, low), (lon_t + 1, high)):
            side[0, at : at + 1] = edge[half : half + 1]
            side[1, at : at + 1] = jnp.where(south, edge[:1], edge[half - 1 : half])
    else:
        for i, ref in enumerate(rows_refs[::-1]):
            side[i, :lon_t] = ref[0, 0, :lon_t].astype(F32)
            for at, edge in ((0, low), (lon_t - 1, high)):
                side[i, at : at + 1] += edge[half + 8 * i : half + 8 * i + 1]
    for base in range(0, count, 4):
        span = range(base, min(base + 4, count))
        cols = jnp.concatenate([tmp[:, x, :] for x in span], axis=1).astype(BF16)
        r = mm(l_ref[...], cols)
        r = r[:nlat] + r[nlat:]
        for x in span:
            one = r[:, (x - base) * chans : (x - base + 1) * chans]
            own_ref[0, x] = one[:half].astype(BF16)
            send_ref[0, x] = one[half:].astype(BF16)
            if wide:
                side[0, x : x + 1] += jnp.where(south, one[2 * half - 1 :], one[half : half + 1])
                side[1, x : x + 1] += jnp.where(south, one[:1], one[half - 1 : half])
    rest = jnp.zeros((half - side.shape[1], chans), F32)
    for i, ref in enumerate((own_ref, send_ref)):
        ref[0, count] = jnp.concatenate([side[i], rest], axis=0).astype(BF16)


def synthesis_call(info, coeffs, lo, hi, table, rows_of, snaps, wide, deps):
    total, rows, lon_t, chans = coeffs.shape
    parts = total // snaps
    nlat = table.shape[0] // 2
    slabs = lon_t + 3 if wide else lon_t + 1
    out = snap_spec((slabs, nlat // 2, chans))
    message = pl.BlockSpec((1, 1) + lo.shape[2:], lambda s, info: (s, 0, 0, 0))
    if wide:
        row_specs = [snap_spec(r.shape[1:]) for r in rows_of]
    else:
        last = pl.BlockSpec((1, 1) + rows_of[0].shape[2:], lambda s, info: (s, lon_t + 2, 0, 0))
        row_specs = [last for _ in rows_of]
    return pl.pallas_call(
        functools.partial(synthesis_kernel, wide),
        grid_spec=grid_of(
            snaps,
            [
                pl.BlockSpec((parts, rows, lon_t, chans), lambda s, info: (s, 0, 0, 0)),
                message,
                message,
                whole(table.shape),
            ]
            + row_specs
            + [any_spec()] * len(deps),
            [out, out],
            [
                pltpu.VMEM((table.shape[1], lon_t + 8 if wide else lon_t, chans), F32),
                pltpu.VMEM((2, lon_t + 8, chans), F32),
            ],
        ),
        out_shape=[shape_of((snaps, slabs, nlat // 2, chans), BF16)] * 2,
        compiler_params=params(),
        cost_estimate=cost(3.6),
        name="synthesis",
    )(info, coeffs, lo, hi, table, *rows_of, *deps)


def gelu_of(x):
    t = jnp.tanh(x * (GELU_A + (GELU_A * GELU_B) * (x * x)))
    return 0.5 * x * (1.0 + t)


def gelu_and_slope(x):
    sq = x * x
    t = jnp.tanh(x * (GELU_A + (GELU_A * GELU_B) * sq))
    cdf = 0.5 + 0.5 * t
    slope = cdf + (0.5 * x) * (1.0 - t * t) * (GELU_A + (3.0 * GELU_A * GELU_B) * sq)
    return x * cdf, slope


def fill_patches(patches, slabs, ends, masks):
    lat_t, chans = slabs[0].shape
    lon_t = len(slabs) - 2
    place = lax.broadcasted_iota(jnp.int32, (lat_t, chans), 0)
    for i in range(lon_t + 2):
        low_row, high_row = ends[i] * masks[0:1], ends[i] * masks[1:2]
        down = jnp.where(place == 0, low_row, pltpu.roll(slabs[i], 1, 0)).astype(BF16)
        up = jnp.where(place == lat_t - 1, high_row, pltpu.roll(slabs[i], lat_t - 1, 0)).astype(BF16)
        mid = slabs[i].astype(BF16)
        for a in range(3):
            x = i - a
            if 0 <= x < lon_t:
                for b, piece in enumerate((down, mid, up)):
                    k = 3 * a + b
                    patches[x * lat_t : (x + 1) * lat_t, k * chans : (k + 1) * chans] = piece


def assemble(patches, field_refs, moved):
    state_ref, s_ref, lo_ref, hi_ref, extra_ref, masks_ref = field_refs
    lon_t, lat_t, chans = moved.shape
    moved[...] = state_ref[0].astype(F32) + s_ref[0, :lon_t].astype(F32)
    rows = s_ref[0, lon_t + 2].astype(F32)
    slabs = [lo_ref[0, 0, :lat_t].astype(F32) + s_ref[0, lon_t].astype(F32)]
    slabs += [moved[i] for i in range(lon_t)]
    slabs += [hi_ref[0, 0, :lat_t].astype(F32) + s_ref[0, lon_t + 1].astype(F32)]
    ends = [rows[i : i + 1] for i in [lon_t] + list(range(lon_t)) + [lon_t + 1]]
    fill_patches(patches, slabs, ends, masks_ref[...])
    patches[:, 9 * chans :] = extra_ref[0]


def forward_kernel(info, *refs):
    field_refs, (w1_ref, mid_ref, dec_ref, bias_ref) = refs[:6], refs[6:10]
    state_out, low_out, pre1_out, pre2_out, patches, moved = refs[-6:]
    lon_t, lat_t, chans = moved.shape
    hid = mid_ref.shape[0]
    assemble(patches, field_refs, moved)
    pre1 = mm(patches[...], w1_ref[...])
    pre1_out[0] = pre1
    active1 = gelu_of(pre1).astype(BF16)
    pre2 = mm(active1, mid_ref[...]) + bias_ref[0:1, :hid]
    pre2_out[0] = pre2
    active2 = gelu_of(pre2).astype(BF16)
    out = mm(active2, dec_ref[...]) + bias_ref[1:2, :chans]
    state_out[0] = moved[...] + out.reshape(lon_t, lat_t, chans)
    low_out[0] = state_out[0].astype(BF16)


GRAD_PAD = 128


def grad_layout(chans, hid):
    one, two, three = 9 * chans, 9 * chans + hid, 9 * chans + hid + chans
    return (one, two, three, -(-(three + 8) // GRAD_PAD) * GRAD_PAD)


def add_grads(first, patches, active1, active2, g_out, g_pre2, g_pre1, acc_enc, acc_mid, acc_dec):
    enc = mm_rows(patches[...], g_pre1[...])
    mid = mm_rows(active1[...], g_pre2[...])
    dec = mm_rows(g_out[...], active2[...])

    @pl.when(first)
    def _():
        acc_enc[...] = enc
        acc_mid[...] = mid
        acc_dec[...] = dec

    @pl.when(jnp.logical_not(first))
    def _():
        acc_enc[...] += enc
        acc_mid[...] += mid
        acc_dec[...] += dec


def pack_grads(out, before, chans, hid, acc_enc, acc_mid, acc_dec, vecs):
    one, two, three, rows = grad_layout(chans, hid)
    tail = jnp.concatenate([vecs[2:3, :chans], vecs[1:2, :chans]], axis=1)
    out[three:] = jnp.zeros((rows - three, hid), F32)
    pieces = [
        (0, one, lambda: acc_enc[:one]),
        (one, two, lambda: acc_mid[...]),
        (two, three, lambda: acc_dec[...]),
        (three, three + 1, lambda: acc_enc[one + 3 : one + 4]),
        (three + 1, three + 2, lambda: acc_enc[one : one + 1]),
        (three + 2, three + 3, lambda: vecs[0:1]),
        (three + 3, three + 4, lambda: tail),
        (three + 4, three + 5, lambda: vecs[3:4]),
    ]
    for start, stop, piece in pieces:
        if before is None:
            out[start:stop] = piece()
        else:
            out[start:stop] = before[start:stop] + piece()


def turn_kernel(more, info, *refs):
    field_refs, (w1_ref, mid_ref, dec_ref, bias_ref) = refs[:6], refs[6:10]
    extra_ref, masks_ref = field_refs[4:]
    target_ref, area_ref, w1t_ref, midt_ref, dect_ref = refs[10:15]
    before = refs[15] if more else None
    (
        gm_out, low_out, grads_out,
        patches, moved, active1, active2, slope1, slope2, g_out, g_pre2, g_pre1, spread,
        acc_enc, acc_mid, acc_dec, vecs, side,
    ) = refs[-18:]
    lon_t, lat_t, chans = moved.shape
    hid = mid_ref.shape[0]
    first = pl.program_id(0) == 0
    assemble(patches, field_refs, moved)
    spread[...] = jnp.zeros_like(spread)

    @pl.when(first)
    def _():
        vecs[...] = jnp.zeros_like(vecs)
        side[...] = jnp.zeros_like(side)

    step = 8
    for x in range(0, lon_t, step):
        rows = slice(x * lat_t, (x + step) * lat_t)
        pre1 = mm(patches[rows], w1_ref[...])
        a1, d1 = gelu_and_slope(pre1)
        active1[rows] = a1.astype(BF16)
        slope1[rows] = d1
        pre2 = mm(active1[rows], mid_ref[...]) + bias_ref[0:1, :hid]
        a2, d2 = gelu_and_slope(pre2)
        active2[rows] = a2.astype(BF16)
        slope2[rows] = d2
        out = mm(active2[rows], dec_ref[...]) + bias_ref[1:2, :chans]
        fresh = moved[x : x + step] + out.reshape(step, lat_t, chans)
        diff = fresh - target_ref[0, x : x + step].astype(F32)
        valid = jnp.broadcast_to(extra_ref[0, rows, 6:7].astype(F32), (step * lat_t, chans))
        weight = valid.reshape(step, lat_t, chans) * area_ref[...][None]
        vecs[3:4, :chans] += jnp.sum(weight.reshape(step * lat_t, chans), 0, keepdims=True)
        weighted = weight * diff
        vecs[1:2, :chans] += jnp.sum((weighted * diff).reshape(step * lat_t, chans), 0, keepdims=True)
        grad = 2.0 * weighted
        moved[x : x + step] = grad
        low = grad.reshape(step * lat_t, chans).astype(BF16)
        g_out[rows] = low
        vecs[2:3, :chans] += jnp.sum(low.astype(F32), 0, keepdims=True)
        gp2 = (mm(low, dect_ref[...]) * slope2[rows]).astype(BF16)
        g_pre2[rows] = gp2
        vecs[0:1] += jnp.sum(gp2.astype(F32), 0, keepdims=True)
        gp1 = (mm(gp2, midt_ref[...]) * slope1[rows]).astype(BF16)
        g_pre1[rows] = gp1
        taps = mm(gp1, w1t_ref[...])
        for a in range(3):
            for b in range(3):
                k = 3 * a + b
                spread[b, x + a : x + a + step] += taps[:, k * chans : (k + 1) * chans].reshape(
                    step, lat_t, chans
                )
    place = lax.broadcasted_iota(jnp.int32, (lat_t, chans), 0)
    masks = masks_ref[...]
    for i in range(lon_t + 2):
        down, here, up = spread[0, i], spread[1, i], spread[2, i]
        got = here + jnp.where(place == lat_t - 1, 0.0, pltpu.roll(down, lat_t - 1, 0))
        got = got + jnp.where(place == 0, 0.0, pltpu.roll(up, 1, 0))
        beyond = down[0:1] * masks[0:1] + up[lat_t - 1 : lat_t] * masks[1:2]
        if i in (0, lon_t + 1):
            at = lon_t if i == 0 else lon_t + 1
            low_out[0, at] = got.astype(BF16)
        else:
            at = i - 1
            total = got + moved[at]
            gm_out[0, at] = total
            low_out[0, at] = total.astype(BF16)
        side[at : at + 1] = beyond
    rest = jnp.zeros((lat_t - side.shape[0], chans), F32)
    low_out[0, lon_t + 2] = jnp.concatenate([side[...], rest], axis=0).astype(BF16)
    add_grads(first, patches, active1, active2, g_out, g_pre2, g_pre1, acc_enc, acc_mid, acc_dec)

    @pl.when(pl.program_id(0) == pl.num_programs(0) - 1)
    def _():
        pack_grads(grads_out, before, chans, hid, acc_enc, acc_mid, acc_dec, vecs)


def bottom_kernel(more, info, *refs):
    field_refs = refs[:6]
    pre1_ref, pre2_ref, gm_ref, glo_ref, ghi_ref, gs_ref, midt_ref, dect_ref = refs[6:14]
    before = refs[14] if more else None
    (
        grads_out, patches, moved, active1, active2, g_out, g_pre2, g_pre1, acc_enc, acc_mid, acc_dec, vecs,
    ) = refs[-12:]
    lon_t, lat_t, chans = moved.shape
    hid = midt_ref.shape[0]
    first = pl.program_id(0) == 0
    assemble(patches, field_refs, moved)

    moved[...] = gm_ref[0] + gs_ref[0, :lon_t].astype(F32)
    moved[0] += glo_ref[0, 0, :lat_t].astype(F32)
    moved[lon_t - 1] += ghi_ref[0, 0, :lat_t].astype(F32)
    place = lax.broadcasted_iota(jnp.int32, (lat_t, chans), 0)
    inner = place == jnp.where(info[0] == 1, 0, lat_t - 1)
    for x in range(lon_t):
        moved[x] += jnp.where(inner, gs_ref[0, lon_t, x : x + 1].astype(F32), 0.0)

    @pl.when(first)
    def _():
        vecs[...] = jnp.zeros_like(vecs)

    step = 8
    for x in range(0, lon_t, step):
        rows = slice(x * lat_t, (x + step) * lat_t)
        a1, d1 = gelu_and_slope(pre1_ref[0, rows])
        active1[rows] = a1.astype(BF16)
        a2, d2 = gelu_and_slope(pre2_ref[0, rows])
        active2[rows] = a2.astype(BF16)
        low = moved[x : x + step].reshape(step * lat_t, chans).astype(BF16)
        g_out[rows] = low
        vecs[2:3, :chans] += jnp.sum(low.astype(F32), 0, keepdims=True)
        gp2 = (mm(low, dect_ref[...]) * d2).astype(BF16)
        g_pre2[rows] = gp2
        vecs[0:1] += jnp.sum(gp2.astype(F32), 0, keepdims=True)
        g_pre1[rows] = (mm(gp2, midt_ref[...]) * d1).astype(BF16)
    add_grads(first, patches, active1, active2, g_out, g_pre2, g_pre1, acc_enc, acc_mid, acc_dec)

    @pl.when(pl.program_id(0) == pl.num_programs(0) - 1)
    def _():
        pack_grads(grads_out, before, chans, hid, acc_enc, acc_mid, acc_dec, vecs)


def message_spec(dims, late):
    return pl.BlockSpec((1, 1) + dims, lambda g, info: (g, late, 0, 0))


def field_specs(field, chunk, half, late, pool_state):
    state, s_ext, lo, hi, extra, masks = field
    return [
        snap_spec(state.shape[1:], chunk if pool_state else None, half),
        snap_spec(s_ext.shape[1:]),
        message_spec(lo.shape[2:], late),
        message_spec(hi.shape[2:], late),
        snap_spec(extra.shape[1:], chunk, half),
        whole(masks.shape),
    ]


def cost(micros):
    return pl.CostEstimate(flops=int(micros * 3e10), bytes_accessed=int(micros * 1e8), transcendentals=0)


def forward_call(info, chunk, half, late, field, weights, deps):
    dims = field[0].shape[1:]
    lon_t, lat_t, chans = dims
    cells = lon_t * lat_t
    hid = weights["mid"].shape[0]
    ws = [weights[k] for k in ("w1", "mid", "dec", "bias")]
    outs = [(dims, F32), (dims, BF16), ((cells, hid), F32), ((cells, hid), F32)]
    return pl.pallas_call(
        forward_kernel,
        grid_spec=grid_of(
            HALF,
            field_specs(field, chunk, half, late, True) + [whole(w.shape) for w in ws] + [any_spec()] * len(deps),
            [snap_spec(d) for d, _ in outs],
            [pltpu.VMEM((cells, 10 * chans), BF16), pltpu.VMEM(dims, F32)],
        ),
        out_shape=[shape_of((HALF,) + d, t) for d, t in outs],
        compiler_params=params(),
        cost_estimate=cost(6.5),
        name="forward",
    )(info, *field, *ws, *deps)


def back_scratch(dims, hid):
    lon_t, lat_t, chans = dims
    cells = lon_t * lat_t
    return [
        pltpu.VMEM((cells, chans), BF16),
        pltpu.VMEM((cells, hid), BF16),
        pltpu.VMEM((cells, hid), BF16),
    ], [
        pltpu.VMEM((10 * chans, hid), F32),
        pltpu.VMEM((hid, hid), F32),
        pltpu.VMEM((chans, hid), F32),
        pltpu.VMEM((8, hid), F32),
    ]


def turn_call(info, chunk, half, late, field, weights, targets, area, deps, before):
    dims = field[0].shape[1:]
    lon_t, lat_t, chans = dims
    cells = lon_t * lat_t
    hid = weights["mid"].shape[0]
    ws = [weights[k] for k in ("w1", "mid", "dec", "bias")]
    wt = [weights[k] for k in ("w1t", "midt", "dect")]
    grad_rows = grad_layout(chans, hid)[-1]
    more = before is not None
    last = [before] if more else []
    outs = [(dims, F32), ((lon_t + 3, lat_t, chans), BF16)]
    grads, sums = back_scratch(dims, hid)
    return pl.pallas_call(
        functools.partial(turn_kernel, more),
        grid_spec=grid_of(
            HALF,
            field_specs(field, chunk, half, late, False)
            + [whole(w.shape) for w in ws]
            + [snap_spec(dims, chunk, half), whole(area.shape)]
            + [whole(w.shape) for w in wt + last]
            + [any_spec()] * len(deps),
            [snap_spec(d) for d, _ in outs] + [whole((grad_rows, hid))],
            [
                pltpu.VMEM((cells, 10 * chans), BF16),
                pltpu.VMEM(dims, F32),
                pltpu.VMEM((cells, hid), BF16),
                pltpu.VMEM((cells, hid), BF16),
                pltpu.VMEM((cells, hid), F32),
                pltpu.VMEM((cells, hid), F32),
            ]
            + grads
            + [pltpu.VMEM((3, lon_t + 2, lat_t, chans), F32)]
            + sums
            + [pltpu.VMEM((lon_t + 8, chans), F32)],
        ),
        out_shape=[shape_of((HALF,) + d, t) for d, t in outs] + [shape_of((grad_rows, hid), F32)],
        compiler_params=params(),
        cost_estimate=cost(13.0),
        name="turn",
    )(info, *field, *ws, targets, area, *wt, *last, *deps)


def bottom_call(info, chunk, half, late, field, weights, pre, gm, glo, ghi, glate, gs, deps, before):
    dims = field[0].shape[1:]
    lon_t, lat_t, chans = dims
    cells = lon_t * lat_t
    hid = weights["mid"].shape[0]
    wt = [weights[k] for k in ("midt", "dect")]
    grad_rows = grad_layout(chans, hid)[-1]
    more = before is not None
    last = [before] if more else []
    grads, sums = back_scratch(dims, hid)
    return pl.pallas_call(
        functools.partial(bottom_kernel, more),
        grid_spec=grid_of(
            HALF,
            field_specs(field, chunk, half, late, True)
            + [snap_spec(v.shape[1:]) for v in (*pre, gm)]
            + [message_spec(glo.shape[2:], glate)] * 2
            + [snap_spec(gs.shape[1:])]
            + [whole(w.shape) for w in wt + last]
            + [any_spec()] * len(deps),
            whole((grad_rows, hid)),
            [
                pltpu.VMEM((cells, 10 * chans), BF16),
                pltpu.VMEM(dims, F32),
                pltpu.VMEM((cells, hid), BF16),
                pltpu.VMEM((cells, hid), BF16),
            ]
            + grads
            + sums,
        ),
        out_shape=shape_of((grad_rows, hid), F32),
        compiler_params=params(),
        cost_estimate=cost(8.0),
        name="bottom",
    )(info, *field, *pre, gm, glo, ghi, gs, *wt, *last, *deps)


def three_parts(vec):
    high = lax.reduce_precision(vec, 8, 7)
    rest = vec - high
    mid = lax.reduce_precision(rest, 8, 7)
    low = lax.reduce_precision(rest - mid, 8, 7)
    return jnp.stack([high, mid, low], axis=-2)


def layer_weights(enc, mid, dec, vec):
    taps, chans, hid = enc.shape
    parts = jnp.concatenate([three_parts(vec[hid : 2 * hid]), three_parts(vec[:hid])], axis=0)
    parts = jnp.pad(parts, ((0, chans - 6), (0, 0)))
    w1 = jnp.concatenate([enc.reshape(taps * chans, hid), parts], axis=0).astype(BF16)
    pad = jnp.zeros((hid - chans,), F32)
    bias = jnp.stack([vec[2 * hid : 3 * hid], jnp.concatenate([vec[3 * hid :], pad])])
    return {
        "w1": w1,
        "mid": mid.astype(BF16),
        "dec": dec.astype(BF16),
        "bias": bias,
        "w1t": jnp.transpose(enc, (2, 0, 1)).reshape(hid, taps * chans).astype(BF16),
        "midt": mid.T.astype(BF16),
        "dect": dec.T.astype(BF16),
    }


def reduce_steps(part):
    lon_n = lax.axis_size("lon")
    me = lax.axis_index("lon")

    def over(stride):
        return "lon", (me // stride) % 2, [(i, i ^ stride) for i in range(lon_n)]

    stages = [over(1), over(2), ("lat", lax.axis_index("lat"), [(0, 1), (1, 0)]), over(8)]
    for axis, bit, perm in stages:
        half = part.shape[0] // 2
        give = lax.dynamic_slice_in_dim(part, (1 - bit) * half, half)
        mine = lax.dynamic_slice_in_dim(part, bit * half, half)
        part = mine + lax.ppermute(give, axis, perm)
        yield part
    axis, _, perm = over(4)
    part = part + lax.ppermute(part, axis, perm)
    yield part
    for axis, bit, perm in reversed(stages):
        got = lax.ppermute(part, axis, perm)
        part = jnp.concatenate([jnp.where(bit == 0, part, got), jnp.where(bit == 0, got, part)])
        yield part


def fast_grads(states, targets, sea_temp, ocean, valid, w_enc, w_mid, w_dec, biases):
    pool, lon_t, lat_t, chans = states.shape
    lon_n, lat_n = lax.axis_size("lon"), lax.axis_size("lat")
    nlon, nlat = lon_t * lon_n, lat_t * lat_n
    zonal, forward, inverse, area_all = host_tables(nlon, nlat, 88)
    hemi = lax.axis_index("lat")
    info = hemi[None].astype(jnp.int32)
    flip = np.concatenate([np.arange(lat_t, nlat), np.arange(lat_t)])
    flip2 = np.concatenate([flip, nlat + flip])
    ends = (np.arange(0, nlon, lon_t)[None, :] + np.array([[-1], [lon_t]])).reshape(-1) % nlon
    zonal_in = jnp.asarray(np.concatenate([zonal, zonal[:, ends]], axis=1))
    zonal_out = jnp.asarray(
        np.concatenate([zonal[:nlon], zonal[:nlon][ends], zonal[nlon:], zonal[nlon:][ends]], axis=0)
    )
    forward = jnp.where(hemi == 0, jnp.asarray(forward), jnp.asarray(forward[:, flip]))
    inverse = jnp.where(hemi == 0, jnp.asarray(inverse), jnp.asarray(inverse[flip2]))
    side = jnp.stack([hemi == 1, hemi == 0]).astype(F32)
    masks = jnp.broadcast_to(side[:, None], (2, chans))
    area = lax.dynamic_slice_in_dim(jnp.asarray(area_all, F32), hemi * lat_t, lat_t)
    area_wide = jnp.broadcast_to(area[:, None], (lat_t, chans))
    up = [(i, (i + 1) % lon_n) for i in range(lon_n)]
    down = [(t, s) for s, t in up]
    swap = [(0, 1), (1, 0)]
    chunks = range(pool // CHUNK)

    traded, deps = [], []
    for c in chunks:
        traded.append(lax.ppermute(pick_call(info, states, c, 1, deps), "lat", swap))
        deps = traded[:1]
    sea = ocean.astype(F32) * sea_temp.astype(F32)
    cells = lon_t * lat_t
    lane = jnp.arange(chans)
    wide_sea = sea.reshape(pool, cells, 1).astype(BF16)
    wide_valid = valid.reshape(pool, cells, 1).astype(BF16)
    extra = jnp.where(lane < 3, wide_sea, jnp.where(lane < 6, jnp.ones((), BF16), wide_valid))
    extra = jnp.where(lane < 7, extra, jnp.zeros((), BF16))
    layers = [layer_weights(w_enc[i], w_mid[i], w_dec[i], biases[i]) for i in range(2)]

    last = [forward]

    def then(result, pick=None):
        last[:] = [result if pick is None else result[pick]]
        return result

    def over_lon(spec):
        return lax.all_to_all(spec, "lon", split_axis=0, concat_axis=0, tiled=True)

    class Chunk:
        def __init__(self, c):
            self.c = c
            self.early = 0
            self.round = 0
            self.other = traded[c]
            self.field0, self.pres = [None, None], [None, None]
            self.fresh, self.low, self.s_ext, self.gm = ([None, None] for _ in range(4))

        def legendre(self):
            half = self.early
            own, late = (states, states) if self.round == 0 else (self.low[half], self.low[1 - half])
            there = self.c if self.round == 0 else None
            wide = self.round == 2
            got = legendre_call(info, own, late, there, half, self.other, forward, last, wide)
            spec, to_up, to_down, sides = then(got, 0)
            self.spec = over_lon(spec)
            self.lo, self.hi = lax.ppermute(to_up, "lon", up), lax.ppermute(to_down, "lon", down)
            self.rows_of = (own, self.other) if wide else (sides,)

        def zonal(self):
            table = zonal_in if self.round == 2 else zonal_out
            self.spec = over_lon(then(zonal_call(self.spec, table, last, self.round == 2)))

        def synthesis(self):
            got = synthesis_call(
                info, self.spec, self.lo, self.hi, inverse, self.rows_of, HALF, self.round < 2, last
            )
            own, send = then(got, 0)
            self.s_ext[self.early] = own
            self.s_ext[1 - self.early] = lax.ppermute(send, "lat", swap)

        def forward(self, late):
            half = self.early ^ late
            field = (states, self.s_ext[half], self.lo, self.hi, extra, masks)
            self.field0[half] = field
            got = forward_call(info, self.c, half, late, field, layers[0], last)
            self.fresh[half], self.low[half], *pre = then(got, 1)
            self.pres[half] = pre
            self.send(half, late)

        def turn(self, late, before):
            half = self.early ^ late
            field = (self.fresh[half], self.s_ext[half], self.lo, self.hi, extra, masks)
            got = turn_call(
                info, self.c, half, late, field, layers[1], targets, area_wide, last, before
            )
            self.gm[half], self.low[half], before = then(got, 1)
            self.send(half, late)
            return before

        def send(self, half, late):
            if not late:
                self.other = lax.ppermute(self.low[half], "lat", swap)

        def flip(self):
            self.early = 1 - self.early
            self.round += 1

        def bottom(self, late, before):
            half = self.early ^ late
            got = bottom_call(
                info, self.c, half, late, self.field0[half], layers[0], self.pres[half],
                self.gm[half], self.lo, self.hi, late, self.s_ext[half], last, before,
            )
            return then(got)

    a, b = (Chunk(c) for c in chunks)
    top, low = None, None
    a.legendre()
    a.zonal()
    b.legendre()
    for one, two in ((a, b), (b, a)):
        one.synthesis()
        one.forward(0)
        two.zonal()
        one.forward(1)
        one.flip()
        one.legendre()
    for one, two in ((a, b), (b, a)):
        one.synthesis()
        top = one.turn(0, top)
        two.zonal()
        top = one.turn(1, top)
        one.flip()
        one.legendre()
    upper = reduce_steps(top)

    a.synthesis()
    low = a.bottom(0, low)
    b.zonal()
    low = a.bottom(1, low)
    b.synthesis()
    low = b.bottom(0, low)
    low = b.bottom(1, low)
    return list(reduce_steps(low))[-1], list(upper)[-1]


def update_kernel(
    rate, pick_ref, g0_ref, g1_ref, v_ref, *refs,
):
    ins, outs = refs[:12], refs[12:]
    layer, part = pl.program_id(0), pl.program_id(1)
    chans = ins[0].shape[2]
    hid = ins[0].shape[3]
    scale = 1.0 / v_ref[1, 4:5, 0:1]
    one, two, three, _ = grad_layout(chans, hid)

    def apply(group, at, grad):
        w_ref, m_ref, a_ref = (ins[4 * i + group] for i in range(3))
        new_ref, mom_ref, avg_ref, copy_ref = (outs[4 * i + group] for i in range(4))
        scaled = grad * scale
        mom = MOMENTUM * m_ref[at] + scaled
        fresh = w_ref[at] - rate * (scaled + MOMENTUM * mom)
        new_ref[at] = fresh
        mom_ref[at] = mom
        avg_ref[at] = AVERAGE * a_ref[at] + (1.0 - AVERAGE) * fresh
        copy_ref[at] = fresh.astype(BF16)

    def layer_step(g_ref):
        for tap in range(3):
            rows = pl.ds(pl.multiple_of((part * 3 + tap) * chans, chans), chans)
            apply(0, (0, tap), g_ref[rows].astype(F32))

        @pl.when(part == 0)
        def _():
            apply(1, (0,), g_ref[one:two].astype(F32))
            apply(2, (0,), g_ref[two:three].astype(F32).T)

    pl.when(layer == 0)(lambda: layer_step(g0_ref))
    pl.when(layer == 1)(lambda: layer_step(g1_ref))

    @pl.when((layer == 0) & (part == 0))
    def _():
        for i in range(2):
            for r in range(4):
                wide = hid if r < 3 else chans
                at = (slice(i, i + 1), slice(r * hid, r * hid + wide))
                apply(3, at, v_ref[i, r : r + 1, :wide])


def update_call(rate, sums, arrays):
    w_enc, w_mid, w_dec, biases = arrays[:4]
    layers, taps, chans, hid = w_enc.shape
    three = grad_layout(chans, hid)[2]
    vecs = jnp.stack([s[three : three + 8].astype(F32) for s in sums])
    enc = pl.BlockSpec((1, taps // 3, chans, hid), lambda i, p, pick: (i, p, 0, 0))
    mid = pl.BlockSpec((1, hid, hid), lambda i, p, pick: (i, 0, 0))
    dec = pl.BlockSpec((1, hid, chans), lambda i, p, pick: (i, 0, 0))
    bias = whole(biases.shape)
    specs = [enc, mid, dec, bias]
    shapes = [w_enc.shape, w_mid.shape, w_dec.shape, biases.shape]
    got = pl.pallas_call(
        functools.partial(update_kernel, rate),
        grid_spec=pltpu.PrefetchScalarGridSpec(
            num_scalar_prefetch=1,
            grid=(layers, 3),
            in_specs=[whole(sums[0].shape), whole(sums[1].shape), whole(vecs.shape)]
            + specs * 3,
            out_specs=specs * 4,
        ),
        out_shape=[shape_of(s, F32) for s in shapes * 3] + [shape_of(s, BF16) for s in shapes],
        compiler_params=params(),
        cost_estimate=cost(8.0),
        name="update",
    )(jnp.zeros((1,), jnp.int32), sums[0], sums[1], vecs, *arrays)
    return (jnp.sum(vecs[1, 3, chans:]), vecs[1, 4, 0], *got)


def fits(states, w_mid, lon_n, lat_n):
    pool, lon_t, lat_t, chans = states.shape
    return (
        lat_n == 2
        and lon_n == 16
        and lon_t == 16
        and lat_t == 64
        and pool == 2 * CHUNK
        and chans == 128
        and w_mid.shape[1] == 2 * chans
        and w_mid.shape[0] == 2
    )


def with_halo(block, sides, width, periodic):
    for axis, dim in sides:
        count = lax.axis_size(axis)
        forward = [(i, i + 1) for i in range(count - 1)]
        if periodic:
            forward.append((count - 1, 0))
        backward = [(target, source) for source, target in forward]
        low = lax.ppermute(
            lax.slice_in_dim(block, block.shape[dim] - width, None, axis=dim), axis, forward
        )
        high = lax.ppermute(lax.slice_in_dim(block, 0, width, axis=dim), axis, backward)
        block = jnp.concatenate([low, block, high], axis=dim)
    return block


def tables(nlon, nlat, groups):
    coeffs = jnp.arange(2 * MW)
    wave = jnp.where(coeffs < MW, coeffs, coeffs - MW + 1).astype(jnp.float32)
    places = jnp.arange(nlon).astype(jnp.float32)
    angle = 2.0 * math.pi * wave[:, None] * places[None, :] / nlon
    fourier = jnp.where((coeffs < MW)[:, None], jnp.cos(angle), jnp.sin(angle)) * math.sqrt(
        2.0 / nlon
    )
    phase = ((jnp.arange(nlat).astype(jnp.float32) + 0.5) / nlat - 0.5) * math.pi
    sine = jnp.sin(phase)
    quad = jnp.cos(phase) * math.pi / nlat
    polys = [jnp.ones_like(sine), sine]
    for degree in range(1, NDEG - 1):
        polys.append(((2 * degree + 1) * sine * polys[-1] - degree * polys[-2]) / (degree + 1))
    stacked = jnp.stack(polys[:NDEG])
    degrees = jnp.arange(NDEG).astype(jnp.float32)
    legendre = jnp.sqrt((2 * degrees + 1) / 2)[:, None] * jnp.sqrt(quad)[None, :] * stacked
    damping = 1.5 * (1.0 - 2.0 * degrees * (degrees + 1) / (NDEG * (NDEG + 1)))
    filters = damping[None, :] * (1.0 - 0.5 * wave / MW)[:, None]
    kept = 2 * MW
    slots = (kept + groups - 1) // groups * groups
    fourier = jnp.pad(fourier, ((0, slots - kept), (0, 0)))
    filters = jnp.pad(filters, ((0, slots - kept), (0, 0)))
    return (fourier, legendre, filters)


def spectral(values, tabs):
    fourier, legendre, filters = tabs
    cycles = lax.all_to_all(
        values.astype(jnp.bfloat16), "lon", split_axis=3, concat_axis=1, tiled=True
    ).astype(values.dtype)
    coeff = jnp.einsum("kx,sxjc->skjc", fourier, cycles, precision=HIGH)
    block = fourier.shape[0] // lax.axis_size("lat")
    where = lax.axis_index("lat")
    block_filter = lax.dynamic_slice_in_dim(filters, where * block, block, 0)
    columns = lax.all_to_all(
        coeff.astype(jnp.bfloat16), "lat", split_axis=1, concat_axis=2, tiled=True
    ).astype(coeff.dtype)
    spec = (
        jnp.einsum("nj,skjc->sknc", legendre, columns, precision=HIGH)
        * block_filter[None, :, :, None]
    )
    back = jnp.einsum("nj,sknc->skjc", legendre, spec, precision=HIGH)
    coeff_back = lax.all_to_all(
        back.astype(jnp.bfloat16), "lat", split_axis=2, concat_axis=1, tiled=True
    ).astype(back.dtype)
    grid = jnp.einsum("kx,skjc->sxjc", fourier, coeff_back, precision=HIGH)
    return lax.all_to_all(
        grid.astype(jnp.bfloat16), "lon", split_axis=1, concat_axis=3, tiled=True
    ).astype(grid.dtype)


def extend(field):
    wider = with_halo(field, (("lon", 1),), 1, True)
    return with_halo(wider, (("lat", 2),), 1, False)


def neighbours(padded, flipped, lon_t, lat_t):
    parts = []
    for row_off in range(3):
        for col_off in range(3):
            first = 2 - row_off if flipped else row_off
            second = 2 - col_off if flipped else col_off
            parts.append(padded[:, first : first + lon_t, second : second + lat_t])
    stacked = jnp.stack(parts, axis=3)
    return stacked.reshape(-1, 9 * padded.shape[-1])


def gelu_fn(value):
    return jax.nn.gelu(value, approximate=True)


def gelu_back(value, grad):
    return jax.vjp(gelu_fn, value)[1](grad)[0]


def layer_forward(state, sea, enc, mid, dec, vec, tabs):
    hid = mid.shape[0]
    lon_t, lat_t = (state.shape[1], state.shape[2])
    moved = state + spectral(state, tabs)
    patches = neighbours(extend(moved.astype(jnp.bfloat16)), False, lon_t, lat_t)
    pre1 = jnp.dot(patches, enc, preferred_element_type=jnp.float32)
    pre1 = pre1 + sea.reshape(-1, 1) * vec[hid : 2 * hid] + vec[:hid]
    active1 = gelu_fn(pre1).astype(jnp.bfloat16)
    pre2 = jnp.dot(active1, mid, preferred_element_type=jnp.float32) + vec[2 * hid : 3 * hid]
    active2 = gelu_fn(pre2).astype(jnp.bfloat16)
    output = jnp.dot(active2, dec, preferred_element_type=jnp.float32) + vec[3 * hid :]
    return (moved + output.reshape(state.shape), (patches, pre1, active1, pre2, active2))


def layer_backward(grad_state, sea, enc, mid, dec, saved, tabs):
    patches, pre1, active1, pre2, active2 = saved
    hid = mid.shape[0]
    shape = grad_state.shape
    chans = shape[-1]
    g_out = grad_state.reshape(-1, chans).astype(jnp.bfloat16)
    g_dec = jnp.einsum("rh,rc->hc", active2, g_out, preferred_element_type=jnp.float32)
    g_act2 = jnp.einsum("rc,hc->rh", g_out, dec, preferred_element_type=jnp.float32)
    g_pre2 = gelu_back(pre2, g_act2).astype(jnp.bfloat16)
    g_mid = jnp.einsum("rh,rg->hg", active1, g_pre2, preferred_element_type=jnp.float32)
    g_act1 = jnp.einsum("rg,hg->rh", g_pre2, mid, preferred_element_type=jnp.float32)
    g_pre1 = gelu_back(pre1, g_act1).astype(jnp.bfloat16)
    g_enc = jnp.einsum("rk,rh->kh", patches, g_pre1, preferred_element_type=jnp.float32)
    wide1 = g_pre1.astype(jnp.float32)
    g_vec = jnp.concatenate(
        [
            jnp.sum(wide1, 0),
            jnp.sum(sea.reshape(-1, 1) * wide1, 0),
            jnp.sum(g_pre2.astype(jnp.float32), 0),
            jnp.sum(g_out.astype(jnp.float32), 0),
        ]
    )
    spread = extend(g_pre1.reshape(shape[0], shape[1], shape[2], hid))
    gathered = neighbours(spread, True, shape[1], shape[2]).reshape(-1, 9, hid)
    g_input = jnp.einsum(
        "rkh,kch->rc", gathered, enc.reshape(9, chans, hid), preferred_element_type=jnp.float32
    )
    grad_moved = grad_state + g_input.reshape(shape)
    return (grad_moved + spectral(grad_moved, tabs), (g_enc, g_mid, g_dec, g_vec))


def general_grads(states, targets, sea_temp, ocean, valid, order, w_enc, w_mid, w_dec, biases):
    pool, lon_t, lat_t, chans = states.shape
    layers, hid = (w_mid.shape[0], w_mid.shape[1])
    nlon = lon_t * lax.axis_size("lon")
    nlat = lat_t * lax.axis_size("lat")
    tabs = tables(nlon, nlat, lax.axis_size("lat"))
    lat_glob = (lax.axis_index("lat") * lat_t + jnp.arange(lat_t)).astype(jnp.float32)
    area = jnp.cos(((lat_glob + 0.5) / nlat - 0.5) * math.pi)
    enc_low = w_enc.astype(jnp.bfloat16).reshape(layers, 9 * chans, hid)
    mid_low = w_mid.astype(jnp.bfloat16)
    dec_low = w_dec.astype(jnp.bfloat16)
    snaps = pool // MB
    sums = [
        jnp.zeros((layers, 9 * chans, hid), jnp.float32),
        jnp.zeros_like(w_mid),
        jnp.zeros_like(w_dec),
        jnp.zeros_like(biases),
    ]
    loss = jnp.zeros((), jnp.float32)
    total = jnp.zeros((), jnp.float32)
    for batch_id in range(MB):
        picks = lax.dynamic_slice_in_dim(order, batch_id * snaps, snaps)
        state = jnp.take(states, picks, axis=0).astype(jnp.float32)
        target = jnp.take(targets, picks, axis=0).astype(jnp.float32)
        sea = jnp.take(ocean, picks, axis=0).astype(jnp.float32) * jnp.take(
            sea_temp, picks, axis=0
        ).astype(jnp.float32)
        weight = jnp.take(valid, picks, axis=0).astype(jnp.float32) * area[None, None, :]
        kept = []
        for layer_id in range(layers):
            state, saved = layer_forward(
                state,
                sea,
                enc_low[layer_id],
                mid_low[layer_id],
                dec_low[layer_id],
                biases[layer_id],
                tabs,
            )
            kept.append(saved)
        diff = state - target
        loss = loss + jnp.sum(weight[..., None] * diff * diff)
        total = total + jnp.sum(weight)
        grad_state = 2.0 * weight[..., None] * diff
        for layer_id in reversed(range(layers)):
            grad_state, found = layer_backward(
                grad_state,
                sea,
                enc_low[layer_id],
                mid_low[layer_id],
                dec_low[layer_id],
                kept[layer_id],
                tabs,
            )
            sums = [acc.at[layer_id].add(part) for acc, part in zip(sums, found)]
    g_enc, g_mid, g_dec, g_vec, loss, total = lax.psum(
        (sums[0], sums[1], sums[2], sums[3], loss, total), ("lon", "lat")
    )
    return g_enc.reshape(w_enc.shape), g_mid, g_dec, g_vec, loss, total


def body(
    states,
    targets,
    sea_temp,
    ocean,
    valid,
    order,
    w_enc,
    w_mid,
    w_dec,
    biases,
    mom_enc,
    mom_mid,
    mom_dec,
    mom_bias,
    avg_enc,
    avg_mid,
    avg_dec,
    avg_bias,
):
    pool, lon_t, lat_t = states.shape[:3]
    lon_n, lat_n = lax.axis_size("lon"), lax.axis_size("lat")
    rate = RATE_BASE * math.sqrt(pool * lon_t * lon_n * lat_t * lat_n)
    if fits(states, w_mid, lon_n, lat_n):
        sums = fast_grads(states, targets, sea_temp, ocean, valid, w_enc, w_mid, w_dec, biases)
        arrays = (w_enc, w_mid, w_dec, biases, mom_enc, mom_mid, mom_dec, mom_bias)
        arrays += (avg_enc, avg_mid, avg_dec, avg_bias)
        return update_call(rate, sums, arrays)
    found = general_grads(
        states, targets, sea_temp, ocean, valid, order, w_enc, w_mid, w_dec, biases
    )
    loss, total = found[4:]
    grads = (found[0].reshape(w_enc.shape),) + found[1:4]
    news, moms, avgs, copies = ([], [], [], [])
    for weight_now, grad, mom, avg in zip(
        (w_enc, w_mid, w_dec, biases),
        grads,
        (mom_enc, mom_mid, mom_dec, mom_bias),
        (avg_enc, avg_mid, avg_dec, avg_bias),
    ):
        scaled = grad / total
        mom_new = MOMENTUM * mom + scaled
        fresh = weight_now - rate * (scaled + MOMENTUM * mom_new)
        news.append(fresh)
        moms.append(mom_new)
        avgs.append(AVERAGE * avg + (1.0 - AVERAGE) * fresh)
        copies.append(fresh.astype(jnp.bfloat16))
    return (
        loss,
        total,
        news[0],
        news[1],
        news[2],
        news[3],
        moms[0],
        moms[1],
        moms[2],
        moms[3],
        avgs[0],
        avgs[1],
        avgs[2],
        avgs[3],
        copies[0],
        copies[1],
        copies[2],
        copies[3],
    )


def solution(mesh):
    placed = (
        P(None, "lon", "lat", None),
        P(None, "lon", "lat", None),
        P(None, "lon", "lat"),
        P(None, "lon", "lat"),
        P(None, "lon", "lat"),
        P(),
        P(),
        P(),
        P(),
        P(),
        P(),
        P(),
        P(),
        P(),
        P(),
        P(),
        P(),
        P(),
    )
    return jax.shard_map(
        body,
        mesh=mesh,
        in_specs=placed,
        out_specs=(
            P(),
            P(),
            P(),
            P(),
            P(),
            P(),
            P(),
            P(),
            P(),
            P(),
            P(),
            P(),
            P(),
            P(),
            P(),
            P(),
            P(),
            P(),
        ),
        check_vma=False,
    )
```

```python
import functools
import math

import jax
import jax.numpy as jnp
import numpy as np
from jax import lax
from jax.experimental import pallas as pl
from jax.experimental.pallas import tpu as pltpu
from jax.sharding import PartitionSpec as P

MW = 86
NDEG = 86
MB = 4


HIGH = lax.Precision.HIGHEST
MOMENTUM = 0.9
AVERAGE = 0.99
RATE_BASE = 0.0006

F32 = jnp.float32
BF16 = jnp.bfloat16
CHUNK = 4
VMEM = 56 * 1024 * 1024
GELU_A = math.sqrt(2.0 / math.pi)
GELU_B = 0.044715


def split_table(table):
    table = np.asarray(table, np.float32)
    high = table.astype(BF16)
    low = (table - high.astype(np.float32)).astype(BF16)
    return np.concatenate([high, low], axis=0)


def host_tables(nlon, nlat, deg):
    kept = np.arange(2 * MW)
    wave = np.where(kept < MW, kept, kept - MW + 1).astype(np.float64)
    angle = 2.0 * np.pi * wave[:, None] * np.arange(nlon)[None, :] / nlon
    fourier = np.where((kept < MW)[:, None], np.cos(angle), np.sin(angle)) * np.sqrt(2.0 / nlon)
    zonal = (fourier * (1.0 - 0.5 * wave / MW)[:, None]).T @ fourier
    phase = ((np.arange(nlat) + 0.5) / nlat - 0.5) * np.pi
    sine, area = np.sin(phase), np.cos(phase)
    polys = [np.ones_like(sine), sine]
    for n in range(1, NDEG - 1):
        polys.append(((2 * n + 1) * sine * polys[-1] - n * polys[-2]) / (n + 1))
    degrees = np.arange(NDEG)
    legendre = np.sqrt((2 * degrees + 1) / 2)[:, None] * np.sqrt(area * np.pi / nlat)[None, :]
    legendre = legendre * np.stack(polys)
    damping = 1.5 * (1.0 - 2.0 * degrees * (degrees + 1) / (NDEG * (NDEG + 1)))
    forward = np.zeros((deg, nlat))
    forward[:NDEG] = legendre
    inverse = np.zeros((nlat, -(-deg // 32) * 32))
    inverse[:, :NDEG] = (legendre * damping[:, None]).T
    return split_table(zonal), split_table(forward), split_table(inverse), area


def mm(a, b):
    return jnp.dot(a, b, preferred_element_type=F32)


def mm_rows(a, b):
    return lax.dot_general(a, b, (((0,), (0,)), ((), ())), preferred_element_type=F32)


def whole(shape):
    return pl.BlockSpec(shape, lambda *_: (0,) * len(shape))


def params():
    return pltpu.CompilerParams(vmem_limit_bytes=VMEM)


HALF = CHUNK // 2


def any_spec():
    return pl.BlockSpec(memory_space=pl.ANY)


def shape_of(dims, dtype):
    return jax.ShapeDtypeStruct(dims, dtype)


def grid_of(count, in_specs, out_specs, scratch):
    return pltpu.PrefetchScalarGridSpec(
        num_scalar_prefetch=1,
        grid=(count,),
        in_specs=in_specs,
        out_specs=out_specs,
        scratch_shapes=scratch,
    )


def first_of(chunk, half, info):
    if chunk is None:
        return 0
    return chunk * CHUNK + HALF * (info[0] if half == 0 else 1 - info[0])


def snap_spec(dims, chunk=None, half=0):
    return pl.BlockSpec(
        (1,) + dims, lambda g, info: (first_of(chunk, half, info) + g,) + (0,) * len(dims)
    )


def pick_kernel(info, x_ref, *refs):
    refs[-1][...] = x_ref[...]


def pick_call(info, fields, chunk, half, deps):
    dims = fields.shape[1:]
    return pl.pallas_call(
        pick_kernel,
        grid_spec=grid_of(
            HALF, [snap_spec(dims, chunk, half)] + [any_spec()] * len(deps), snap_spec(dims), []
        ),
        out_shape=shape_of((HALF,) + dims, fields.dtype),
        compiler_params=params(),
        cost_estimate=cost(1.0),
        name="pick",
    )(info, fields, *deps)


def legendre_kernel(
    wide, info, own_ref, other_ref, first_ref, last_ref, l_ref, *refs
):
    o_ref, up_ref, down_ref, rows_ref, tmp = refs[-5:]
    parts, rows, lon_t, chans = o_ref.shape
    lat_t = own_ref.shape[2]
    deg = l_ref.shape[0] // 2
    count = lon_t + 2 if wide else lon_t
    each = deg // parts
    place = lax.broadcasted_iota(jnp.int32, (lat_t, chans), 0)
    south = info[0] == 1
    inner = place == jnp.where(south, 0, lat_t - 1)
    other_inner = place == jnp.where(south, lat_t - 1, 0)

    def column(x):
        own, other = own_ref[0, x], other_ref[0, x]
        if wide:
            to_own = other_ref[0, count, x : x + 1].astype(F32)
            to_other = own_ref[0, count, x : x + 1].astype(F32)
            own = (own.astype(F32) + jnp.where(inner, to_own, 0.0)).astype(BF16)
            other = (other.astype(F32) + jnp.where(other_inner, to_other, 0.0)).astype(BF16)
        else:
            own_f, other_f = own.astype(F32), other.astype(F32)
            ends = [(own_f[:1], own_f[lat_t - 1 :]), (other_f[lat_t - 1 :], other_f[:1])]
            for i, (if_south, if_north) in enumerate(ends):
                rows_ref[0, i, x : x + 1] = jnp.where(south, if_south, if_north)
        return jnp.concatenate([own, other], axis=0)

    for base in range(0, count, 4):
        span = range(base, min(base + 4, count))
        r = mm(l_ref[...], jnp.concatenate([column(x) for x in span], axis=1))
        r = r[:deg] + r[deg:]
        for x in span:
            tmp[:, x, :] = r[:, (x - base) * chans : (x - base + 1) * chans]
    o_ref[:, :each] = tmp[:, :lon_t, :].astype(BF16).reshape(parts, each, lon_t, chans)
    if wide:
        rest = jnp.zeros((lon_t - each, chans), F32)
        for p in range(parts):
            for side in range(2):
                edge = tmp[p * each : (p + 1) * each, lon_t + side, :]
                o_ref[p, each + side] = jnp.concatenate([edge, rest], axis=0).astype(BF16)
        rows_ref[...] = jnp.zeros_like(rows_ref)
    for ref, late_ref, x in ((down_ref, first_ref, 0), (up_ref, last_ref, lon_t - 1)):
        if wide:
            at = lon_t if x == 0 else lon_t + 1
            corner, far = other_ref[0, count, at : at + 1], own_ref[0, count, at : at + 1]
            pieces = [jnp.broadcast_to(v.astype(F32), (8, chans)) for v in (corner, far)]
        else:
            at = x
            pieces = [jnp.broadcast_to(rows_ref[0, 1, x : x + 1], (16, chans))]
        ref[0, 0, :lat_t] = own_ref[0, at]
        ref[0, 0, lat_t:] = jnp.concatenate(pieces, axis=0).astype(BF16)
        ref[0, 1, :lat_t] = late_ref[0, 0]
        ref[0, 1, lat_t:] = jnp.zeros((16, chans), BF16)


def legendre_call(info, own, late, chunk, half, other, table, deps, wide):
    snaps, slabs, lat_t, chans = other.shape
    deg = table.shape[0] // 2
    parts = 8
    lon_t = slabs - 3 if wide else slabs
    rows = deg // parts + (2 if wide else 0)
    message = (2, lat_t + 16, chans)
    sides = (2, lon_t, chans)

    def late_column(x):
        return pl.BlockSpec(
            (1, 1, lat_t, chans), lambda g, info: (first_of(chunk, 1 - half, info) + g, x, 0, 0)
        )

    columns = (lon_t, lon_t + 1) if wide else (0, lon_t - 1)
    return pl.pallas_call(
        functools.partial(legendre_kernel, wide),
        grid_spec=grid_of(
            snaps,
            [
                snap_spec(own.shape[1:], chunk, half),
                snap_spec(other.shape[1:]),
                late_column(columns[0]),
                late_column(columns[1]),
                whole(table.shape),
            ]
            + [any_spec()] * len(deps),
            [
                pl.BlockSpec((parts, rows, lon_t, chans), lambda s, info: (s, 0, 0, 0)),
                snap_spec(message),
                snap_spec(message),
                snap_spec(sides),
            ],
            [pltpu.VMEM((deg, lon_t + 8 if wide else lon_t, chans), F32)],
        ),
        out_shape=[
            shape_of((snaps * parts, rows, lon_t, chans), BF16),
            shape_of((snaps,) + message, BF16),
            shape_of((snaps,) + message, BF16),
            shape_of((snaps,) + sides, F32),
        ],
        compiler_params=params(),
        cost_estimate=cost(3.4),
        name="legendre",
    )(info, own, other, late, late, table, *deps)


def zonal_kernel(wide_in, x_ref, a_ref, *refs):
    o_ref, tmp = refs[-2:]
    groups, _, lon_t, chans = x_ref.shape
    nlon = groups * lon_t
    rows = min(x_ref.shape[1], o_ref.shape[1])
    if wide_in:
        for side in range(2):
            tmp[side * groups : (side + 1) * groups] = x_ref[:, rows + side].astype(F32)
    else:
        tmp[...] = jnp.zeros_like(tmp)
    for base in range(0, rows, 4):
        span = range(base, min(base + 4, rows))
        fields = jnp.concatenate([x_ref[:, n].reshape(nlon, chans) for n in span], axis=1)
        if wide_in:
            edges = jnp.concatenate([tmp[:, n, :] for n in span], axis=1).astype(BF16)
            r = mm(a_ref[:, :nlon], fields) + mm(a_ref[:, nlon:], edges)
            r = r[:nlon] + r[nlon:]
        else:
            r = mm(a_ref[...], fields)
            size = r.shape[0] // 2
            r = r[:size] + r[size:]
        low = r[:nlon].astype(BF16)
        for n in span:
            lanes = slice((n - base) * chans, (n - base + 1) * chans)
            o_ref[:, n] = low[:, lanes].reshape(groups, lon_t, chans)
            if not wide_in:
                tmp[:, n, :] = r[nlon:, lanes]
    if not wide_in:
        for side in range(2):
            o_ref[:, rows + side] = tmp[side * groups : (side + 1) * groups].astype(BF16)


def zonal_call(fields, table, deps, wide_in):
    groups, rows, lon_t, chans = fields.shape
    out = (groups, rows - 2 if wide_in else rows + 2, lon_t, chans)
    return pl.pallas_call(
        functools.partial(zonal_kernel, wide_in),
        in_specs=[pl.BlockSpec(memory_space=pltpu.VMEM)] * 2 + [any_spec()] * len(deps),
        out_specs=pl.BlockSpec(memory_space=pltpu.VMEM),
        out_shape=shape_of(out, BF16),
        scratch_shapes=[pltpu.VMEM((2 * groups, lon_t, chans), F32)],
        compiler_params=params(),
        cost_estimate=cost(2.8),
        name="zonal",
    )(fields, table, *deps)


def synthesis_kernel(wide, info, x_ref, lo_ref, hi_ref, l_ref, *refs):
    rows_refs = refs[: 1 if wide else 2]
    own_ref, send_ref, tmp, side = refs[-4:]
    parts, rows, lon_t, chans = x_ref.shape
    each = rows - 2 if wide else rows
    deg = parts * each
    count = lon_t + 2 if wide else lon_t
    nlat = l_ref.shape[0] // 2
    half = nlat // 2
    south = info[0] == 1
    tmp[:deg, :lon_t, :] = x_ref[:, :each].reshape(deg, lon_t, chans).astype(F32)
    if wide:
        for p in range(parts):
            for e in range(2):
                tmp[p * each : (p + 1) * each, lon_t + e, :] = x_ref[p, each + e, :each].astype(F32)
    tmp[deg:] = jnp.zeros((tmp.shape[0] - deg,) + tmp.shape[1:], F32)
    side[...] = jnp.zeros_like(side)
    low, high = lo_ref[0, 0].astype(F32), hi_ref[0, 0].astype(F32)
    if wide:
        sides_ref = rows_refs[0]
        for i in range(2):
            side[i, :lon_t] = sides_ref[0, 1 - i]
        for at, edge in ((lon_t, low), (lon_t + 1, high)):
            side[0, at : at + 1] = edge[half : half + 1]
            side[1, at : at + 1] = jnp.where(south, edge[:1], edge[half - 1 : half])
    else:
        for i, ref in enumerate(rows_refs[::-1]):
            side[i, :lon_t] = ref[0, 0, :lon_t].astype(F32)
            for at, edge in ((0, low), (lon_t - 1, high)):
                side[i, at : at + 1] += edge[half + 8 * i : half + 8 * i + 1]
    for base in range(0, count, 4):
        span = range(base, min(base + 4, count))
        cols = jnp.concatenate([tmp[:, x, :] for x in span], axis=1).astype(BF16)
        r = mm(l_ref[...], cols)
        r = r[:nlat] + r[nlat:]
        for x in span:
            one = r[:, (x - base) * chans : (x - base + 1) * chans]
            own_ref[0, x] = one[:half].astype(BF16)
            send_ref[0, x] = one[half:].astype(BF16)
            if wide:
                side[0, x : x + 1] += jnp.where(south, one[2 * half - 1 :], one[half : half + 1])
                side[1, x : x + 1] += jnp.where(south, one[:1], one[half - 1 : half])
    rest = jnp.zeros((half - side.shape[1], chans), F32)
    for i, ref in enumerate((own_ref, send_ref)):
        ref[0, count] = jnp.concatenate([side[i], rest], axis=0).astype(BF16)


def synthesis_call(info, coeffs, lo, hi, table, rows_of, snaps, wide, deps):
    total, rows, lon_t, chans = coeffs.shape
    parts = total // snaps
    nlat = table.shape[0] // 2
    slabs = lon_t + 3 if wide else lon_t + 1
    out = snap_spec((slabs, nlat // 2, chans))
    message = pl.BlockSpec((1, 1) + lo.shape[2:], lambda s, info: (s, 0, 0, 0))
    if wide:
        row_specs = [snap_spec(r.shape[1:]) for r in rows_of]
    else:
        last = pl.BlockSpec((1, 1) + rows_of[0].shape[2:], lambda s, info: (s, lon_t + 2, 0, 0))
        row_specs = [last for _ in rows_of]
    return pl.pallas_call(
        functools.partial(synthesis_kernel, wide),
        grid_spec=grid_of(
            snaps,
            [
                pl.BlockSpec((parts, rows, lon_t, chans), lambda s, info: (s, 0, 0, 0)),
                message,
                message,
                whole(table.shape),
            ]
            + row_specs
            + [any_spec()] * len(deps),
            [out, out],
            [
                pltpu.VMEM((table.shape[1], lon_t + 8 if wide else lon_t, chans), F32),
                pltpu.VMEM((2, lon_t + 8, chans), F32),
            ],
        ),
        out_shape=[shape_of((snaps, slabs, nlat // 2, chans), BF16)] * 2,
        compiler_params=params(),
        cost_estimate=cost(3.6),
        name="synthesis",
    )(info, coeffs, lo, hi, table, *rows_of, *deps)


def gelu_of(x):
    t = jnp.tanh(x * (GELU_A + (GELU_A * GELU_B) * (x * x)))
    return 0.5 * x * (1.0 + t)


def gelu_and_slope(x):
    sq = x * x
    t = jnp.tanh(x * (GELU_A + (GELU_A * GELU_B) * sq))
    cdf = 0.5 + 0.5 * t
    slope = cdf + (0.5 * x) * (1.0 - t * t) * (GELU_A + (3.0 * GELU_A * GELU_B) * sq)
    return x * cdf, slope


def fill_patches(patches, slabs, ends, masks):
    lat_t, chans = slabs[0].shape
    lon_t = len(slabs) - 2
    place = lax.broadcasted_iota(jnp.int32, (lat_t, chans), 0)
    for i in range(lon_t + 2):
        low_row, high_row = ends[i] * masks[0:1], ends[i] * masks[1:2]
        down = jnp.where(place == 0, low_row, pltpu.roll(slabs[i], 1, 0)).astype(BF16)
        up = jnp.where(place == lat_t - 1, high_row, pltpu.roll(slabs[i], lat_t - 1, 0)).astype(BF16)
        mid = slabs[i].astype(BF16)
        for a in range(3):
            x = i - a
            if 0 <= x < lon_t:
                for b, piece in enumerate((down, mid, up)):
                    k = 3 * a + b
                    patches[x * lat_t : (x + 1) * lat_t, k * chans : (k + 1) * chans] = piece


def assemble(patches, field_refs, moved):
    state_ref, s_ref, lo_ref, hi_ref, extra_ref, masks_ref = field_refs
    lon_t, lat_t, chans = moved.shape
    moved[...] = state_ref[0].astype(F32) + s_ref[0, :lon_t].astype(F32)
    rows = s_ref[0, lon_t + 2].astype(F32)
    slabs = [lo_ref[0, 0, :lat_t].astype(F32) + s_ref[0, lon_t].astype(F32)]
    slabs += [moved[i] for i in range(lon_t)]
    slabs += [hi_ref[0, 0, :lat_t].astype(F32) + s_ref[0, lon_t + 1].astype(F32)]
    ends = [rows[i : i + 1] for i in [lon_t] + list(range(lon_t)) + [lon_t + 1]]
    fill_patches(patches, slabs, ends, masks_ref[...])
    patches[:, 9 * chans :] = extra_ref[0]


def forward_kernel(info, *refs):
    field_refs, (w1_ref, mid_ref, dec_ref, bias_ref) = refs[:6], refs[6:10]
    state_out, low_out, pre1_out, pre2_out, patches, moved = refs[-6:]
    lon_t, lat_t, chans = moved.shape
    hid = mid_ref.shape[0]
    assemble(patches, field_refs, moved)
    pre1 = mm(patches[...], w1_ref[...])
    pre1_out[0] = pre1
    active1 = gelu_of(pre1).astype(BF16)
    pre2 = mm(active1, mid_ref[...]) + bias_ref[0:1, :hid]
    pre2_out[0] = pre2
    active2 = gelu_of(pre2).astype(BF16)
    out = mm(active2, dec_ref[...]) + bias_ref[1:2, :chans]
    state_out[0] = moved[...] + out.reshape(lon_t, lat_t, chans)
    low_out[0] = state_out[0].astype(BF16)


GRAD_PAD = 128


def grad_layout(chans, hid):
    one, two, three = 9 * chans, 9 * chans + hid, 9 * chans + hid + chans
    return (one, two, three, -(-(three + 8) // GRAD_PAD) * GRAD_PAD)


def add_grads(first, patches, active1, active2, g_out, g_pre2, g_pre1, acc_enc, acc_mid, acc_dec):
    enc = mm_rows(patches[...], g_pre1[...])
    mid = mm_rows(active1[...], g_pre2[...])
    dec = mm_rows(g_out[...], active2[...])

    @pl.when(first)
    def _():
        acc_enc[...] = enc
        acc_mid[...] = mid
        acc_dec[...] = dec

    @pl.when(jnp.logical_not(first))
    def _():
        acc_enc[...] += enc
        acc_mid[...] += mid
        acc_dec[...] += dec


def pack_grads(out, before, chans, hid, acc_enc, acc_mid, acc_dec, vecs):
    one, two, three, rows = grad_layout(chans, hid)
    tail = jnp.concatenate([vecs[2:3, :chans], vecs[1:2, :chans]], axis=1)
    out[three:] = jnp.zeros((rows - three, hid), F32)
    pieces = [
        (0, one, lambda: acc_enc[:one]),
        (one, two, lambda: acc_mid[...]),
        (two, three, lambda: acc_dec[...]),
        (three, three + 1, lambda: acc_enc[one + 3 : one + 4]),
        (three + 1, three + 2, lambda: acc_enc[one : one + 1]),
        (three + 2, three + 3, lambda: vecs[0:1]),
        (three + 3, three + 4, lambda: tail),
        (three + 4, three + 5, lambda: vecs[3:4]),
    ]
    for start, stop, piece in pieces:
        if before is None:
            out[start:stop] = piece()
        else:
            out[start:stop] = before[start:stop] + piece()


def turn_kernel(more, info, *refs):
    field_refs, (w1_ref, mid_ref, dec_ref, bias_ref) = refs[:6], refs[6:10]
    extra_ref, masks_ref = field_refs[4:]
    target_ref, area_ref, w1t_ref, midt_ref, dect_ref = refs[10:15]
    before = refs[15] if more else None
    (
        gm_out, low_out, grads_out,
        patches, moved, active1, active2, slope1, slope2, g_out, g_pre2, g_pre1, spread,
        acc_enc, acc_mid, acc_dec, vecs, side,
    ) = refs[-18:]
    lon_t, lat_t, chans = moved.shape
    hid = mid_ref.shape[0]
    first = pl.program_id(0) == 0
    assemble(patches, field_refs, moved)
    spread[...] = jnp.zeros_like(spread)

    @pl.when(first)
    def _():
        vecs[...] = jnp.zeros_like(vecs)
        side[...] = jnp.zeros_like(side)

    step = 8
    for x in range(0, lon_t, step):
        rows = slice(x * lat_t, (x + step) * lat_t)
        pre1 = mm(patches[rows], w1_ref[...])
        a1, d1 = gelu_and_slope(pre1)
        active1[rows] = a1.astype(BF16)
        slope1[rows] = d1
        pre2 = mm(active1[rows], mid_ref[...]) + bias_ref[0:1, :hid]
        a2, d2 = gelu_and_slope(pre2)
        active2[rows] = a2.astype(BF16)
        slope2[rows] = d2
        out = mm(active2[rows], dec_ref[...]) + bias_ref[1:2, :chans]
        fresh = moved[x : x + step] + out.reshape(step, lat_t, chans)
        diff = fresh - target_ref[0, x : x + step].astype(F32)
        valid = jnp.broadcast_to(extra_ref[0, rows, 6:7].astype(F32), (step * lat_t, chans))
        weight = valid.reshape(step, lat_t, chans) * area_ref[...][None]
        vecs[3:4, :chans] += jnp.sum(weight.reshape(step * lat_t, chans), 0, keepdims=True)
        weighted = weight * diff
        vecs[1:2, :chans] += jnp.sum((weighted * diff).reshape(step * lat_t, chans), 0, keepdims=True)
        grad = 2.0 * weighted
        moved[x : x + step] = grad
        low = grad.reshape(step * lat_t, chans).astype(BF16)
        g_out[rows] = low
        vecs[2:3, :chans] += jnp.sum(low.astype(F32), 0, keepdims=True)
        gp2 = (mm(low, dect_ref[...]) * slope2[rows]).astype(BF16)
        g_pre2[rows] = gp2
        vecs[0:1] += jnp.sum(gp2.astype(F32), 0, keepdims=True)
        gp1 = (mm(gp2, midt_ref[...]) * slope1[rows]).astype(BF16)
        g_pre1[rows] = gp1
        taps = mm(gp1, w1t_ref[...])
        for a in range(3):
            for b in range(3):
                k = 3 * a + b
                spread[b, x + a : x + a + step] += taps[:, k * chans : (k + 1) * chans].reshape(
                    step, lat_t, chans
                )
    place = lax.broadcasted_iota(jnp.int32, (lat_t, chans), 0)
    masks = masks_ref[...]
    for i in range(lon_t + 2):
        down, here, up = spread[0, i], spread[1, i], spread[2, i]
        got = here + jnp.where(place == lat_t - 1, 0.0, pltpu.roll(down, lat_t - 1, 0))
        got = got + jnp.where(place == 0, 0.0, pltpu.roll(up, 1, 0))
        beyond = down[0:1] * masks[0:1] + up[lat_t - 1 : lat_t] * masks[1:2]
        if i in (0, lon_t + 1):
            at = lon_t if i == 0 else lon_t + 1
            low_out[0, at] = got.astype(BF16)
        else:
            at = i - 1
            total = got + moved[at]
            gm_out[0, at] = total
            low_out[0, at] = total.astype(BF16)
        side[at : at + 1] = beyond
    rest = jnp.zeros((lat_t - side.shape[0], chans), F32)
    low_out[0, lon_t + 2] = jnp.concatenate([side[...], rest], axis=0).astype(BF16)
    add_grads(first, patches, active1, active2, g_out, g_pre2, g_pre1, acc_enc, acc_mid, acc_dec)

    @pl.when(pl.program_id(0) == pl.num_programs(0) - 1)
    def _():
        pack_grads(grads_out, before, chans, hid, acc_enc, acc_mid, acc_dec, vecs)


def bottom_kernel(more, info, *refs):
    field_refs = refs[:6]
    pre1_ref, pre2_ref, gm_ref, glo_ref, ghi_ref, gs_ref, midt_ref, dect_ref = refs[6:14]
    before = refs[14] if more else None
    (
        grads_out, patches, moved, active1, active2, g_out, g_pre2, g_pre1, acc_enc, acc_mid, acc_dec, vecs,
    ) = refs[-12:]
    lon_t, lat_t, chans = moved.shape
    hid = midt_ref.shape[0]
    first = pl.program_id(0) == 0
    assemble(patches, field_refs, moved)

    moved[...] = gm_ref[0] + gs_ref[0, :lon_t].astype(F32)
    moved[0] += glo_ref[0, 0, :lat_t].astype(F32)
    moved[lon_t - 1] += ghi_ref[0, 0, :lat_t].astype(F32)
    place = lax.broadcasted_iota(jnp.int32, (lat_t, chans), 0)
    inner = place == jnp.where(info[0] == 1, 0, lat_t - 1)
    for x in range(lon_t):
        moved[x] += jnp.where(inner, gs_ref[0, lon_t, x : x + 1].astype(F32), 0.0)

    @pl.when(first)
    def _():
        vecs[...] = jnp.zeros_like(vecs)

    step = 8
    for x in range(0, lon_t, step):
        rows = slice(x * lat_t, (x + step) * lat_t)
        a1, d1 = gelu_and_slope(pre1_ref[0, rows])
        active1[rows] = a1.astype(BF16)
        a2, d2 = gelu_and_slope(pre2_ref[0, rows])
        active2[rows] = a2.astype(BF16)
        low = moved[x : x + step].reshape(step * lat_t, chans).astype(BF16)
        g_out[rows] = low
        vecs[2:3, :chans] += jnp.sum(low.astype(F32), 0, keepdims=True)
        gp2 = (mm(low, dect_ref[...]) * d2).astype(BF16)
        g_pre2[rows] = gp2
        vecs[0:1] += jnp.sum(gp2.astype(F32), 0, keepdims=True)
        g_pre1[rows] = (mm(gp2, midt_ref[...]) * d1).astype(BF16)
    add_grads(first, patches, active1, active2, g_out, g_pre2, g_pre1, acc_enc, acc_mid, acc_dec)

    @pl.when(pl.program_id(0) == pl.num_programs(0) - 1)
    def _():
        pack_grads(grads_out, before, chans, hid, acc_enc, acc_mid, acc_dec, vecs)


def message_spec(dims, late):
    return pl.BlockSpec((1, 1) + dims, lambda g, info: (g, late, 0, 0))


def field_specs(field, chunk, half, late, pool_state):
    state, s_ext, lo, hi, extra, masks = field
    return [
        snap_spec(state.shape[1:], chunk if pool_state else None, half),
        snap_spec(s_ext.shape[1:]),
        message_spec(lo.shape[2:], late),
        message_spec(hi.shape[2:], late),
        snap_spec(extra.shape[1:], chunk, half),
        whole(masks.shape),
    ]


def cost(micros):
    return pl.CostEstimate(flops=int(micros * 3e10), bytes_accessed=int(micros * 1e8), transcendentals=0)


def forward_call(info, chunk, half, late, field, weights, deps):
    dims = field[0].shape[1:]
    lon_t, lat_t, chans = dims
    cells = lon_t * lat_t
    hid = weights["mid"].shape[0]
    ws = [weights[k] for k in ("w1", "mid", "dec", "bias")]
    outs = [(dims, F32), (dims, BF16), ((cells, hid), F32), ((cells, hid), F32)]
    return pl.pallas_call(
        forward_kernel,
        grid_spec=grid_of(
            HALF,
            field_specs(field, chunk, half, late, True) + [whole(w.shape) for w in ws] + [any_spec()] * len(deps),
            [snap_spec(d) for d, _ in outs],
            [pltpu.VMEM((cells, 10 * chans), BF16), pltpu.VMEM(dims, F32)],
        ),
        out_shape=[shape_of((HALF,) + d, t) for d, t in outs],
        compiler_params=params(),
        cost_estimate=cost(6.5),
        name="forward",
    )(info, *field, *ws, *deps)


def back_scratch(dims, hid):
    lon_t, lat_t, chans = dims
    cells = lon_t * lat_t
    return [
        pltpu.VMEM((cells, chans), BF16),
        pltpu.VMEM((cells, hid), BF16),
        pltpu.VMEM((cells, hid), BF16),
    ], [
        pltpu.VMEM((10 * chans, hid), F32),
        pltpu.VMEM((hid, hid), F32),
        pltpu.VMEM((chans, hid), F32),
        pltpu.VMEM((8, hid), F32),
    ]


def turn_call(info, chunk, half, late, field, weights, targets, area, deps, before):
    dims = field[0].shape[1:]
    lon_t, lat_t, chans = dims
    cells = lon_t * lat_t
    hid = weights["mid"].shape[0]
    ws = [weights[k] for k in ("w1", "mid", "dec", "bias")]
    wt = [weights[k] for k in ("w1t", "midt", "dect")]
    grad_rows = grad_layout(chans, hid)[-1]
    more = before is not None
    last = [before] if more else []
    outs = [(dims, F32), ((lon_t + 3, lat_t, chans), BF16)]
    grads, sums = back_scratch(dims, hid)
    return pl.pallas_call(
        functools.partial(turn_kernel, more),
        grid_spec=grid_of(
            HALF,
            field_specs(field, chunk, half, late, False)
            + [whole(w.shape) for w in ws]
            + [snap_spec(dims, chunk, half), whole(area.shape)]
            + [whole(w.shape) for w in wt + last]
            + [any_spec()] * len(deps),
            [snap_spec(d) for d, _ in outs] + [whole((grad_rows, hid))],
            [
                pltpu.VMEM((cells, 10 * chans), BF16),
                pltpu.VMEM(dims, F32),
                pltpu.VMEM((cells, hid), BF16),
                pltpu.VMEM((cells, hid), BF16),
                pltpu.VMEM((cells, hid), F32),
                pltpu.VMEM((cells, hid), F32),
            ]
            + grads
            + [pltpu.VMEM((3, lon_t + 2, lat_t, chans), F32)]
            + sums
            + [pltpu.VMEM((lon_t + 8, chans), F32)],
        ),
        out_shape=[shape_of((HALF,) + d, t) for d, t in outs] + [shape_of((grad_rows, hid), F32)],
        compiler_params=params(),
        cost_estimate=cost(13.0),
        name="turn",
    )(info, *field, *ws, targets, area, *wt, *last, *deps)


def bottom_call(info, chunk, half, late, field, weights, pre, gm, glo, ghi, glate, gs, deps, before):
    dims = field[0].shape[1:]
    lon_t, lat_t, chans = dims
    cells = lon_t * lat_t
    hid = weights["mid"].shape[0]
    wt = [weights[k] for k in ("midt", "dect")]
    grad_rows = grad_layout(chans, hid)[-1]
    more = before is not None
    last = [before] if more else []
    grads, sums = back_scratch(dims, hid)
    return pl.pallas_call(
        functools.partial(bottom_kernel, more),
        grid_spec=grid_of(
            HALF,
            field_specs(field, chunk, half, late, True)
            + [snap_spec(v.shape[1:]) for v in (*pre, gm)]
            + [message_spec(glo.shape[2:], glate)] * 2
            + [snap_spec(gs.shape[1:])]
            + [whole(w.shape) for w in wt + last]
            + [any_spec()] * len(deps),
            whole((grad_rows, hid)),
            [
                pltpu.VMEM((cells, 10 * chans), BF16),
                pltpu.VMEM(dims, F32),
                pltpu.VMEM((cells, hid), BF16),
                pltpu.VMEM((cells, hid), BF16),
            ]
            + grads
            + sums,
        ),
        out_shape=shape_of((grad_rows, hid), F32),
        compiler_params=params(),
        cost_estimate=cost(8.0),
        name="bottom",
    )(info, *field, *pre, gm, glo, ghi, gs, *wt, *last, *deps)


def three_parts(vec):
    high = lax.reduce_precision(vec, 8, 7)
    rest = vec - high
    mid = lax.reduce_precision(rest, 8, 7)
    low = lax.reduce_precision(rest - mid, 8, 7)
    return jnp.stack([high, mid, low], axis=-2)


def layer_weights(enc, mid, dec, vec):
    taps, chans, hid = enc.shape
    parts = jnp.concatenate([three_parts(vec[hid : 2 * hid]), three_parts(vec[:hid])], axis=0)
    parts = jnp.pad(parts, ((0, chans - 6), (0, 0)))
    w1 = jnp.concatenate([enc.reshape(taps * chans, hid), parts], axis=0).astype(BF16)
    pad = jnp.zeros((hid - chans,), F32)
    bias = jnp.stack([vec[2 * hid : 3 * hid], jnp.concatenate([vec[3 * hid :], pad])])
    return {
        "w1": w1,
        "mid": mid.astype(BF16),
        "dec": dec.astype(BF16),
        "bias": bias,
        "w1t": jnp.transpose(enc, (2, 0, 1)).reshape(hid, taps * chans).astype(BF16),
        "midt": mid.T.astype(BF16),
        "dect": dec.T.astype(BF16),
    }


def reduce_steps(part, order):
    lon_n = lax.axis_size("lon")
    me = lax.axis_index("lon")

    def over(stride):
        return "lon", (me // stride) % 2, [(i, i ^ stride) for i in range(lon_n)]

    links = {"core": over(1), "x": over(2), "y": ("lat", lax.axis_index("lat"), [(0, 1), (1, 0)]), "z": over(8)}
    stages = [links[name] for name in order]

    def after(x, hold):
        return x if hold is None else lax.optimization_barrier((x, hold))[0]

    hold = None
    for axis, bit, perm in stages:
        half = part.shape[0] // 2
        give = lax.dynamic_slice_in_dim(part, (1 - bit) * half, half)
        mine = lax.dynamic_slice_in_dim(part, bit * half, half)
        part = after(mine, hold) + lax.ppermute(give, axis, perm)
        hold = yield part
    axis, _, perm = over(4)
    part = after(part, hold) + lax.ppermute(part, axis, perm)
    hold = yield part
    for axis, bit, perm in reversed(stages):
        got = lax.ppermute(part, axis, perm)
        part = after(part, hold)
        part = jnp.concatenate([jnp.where(bit == 0, part, got), jnp.where(bit == 0, got, part)])
        hold = yield part


def fast_grads(states, targets, sea_temp, ocean, valid, w_enc, w_mid, w_dec, biases):
    pool, lon_t, lat_t, chans = states.shape
    lon_n, lat_n = lax.axis_size("lon"), lax.axis_size("lat")
    nlon, nlat = lon_t * lon_n, lat_t * lat_n
    zonal, forward, inverse, area_all = host_tables(nlon, nlat, 88)
    hemi = lax.axis_index("lat")
    info = hemi[None].astype(jnp.int32)
    flip = np.concatenate([np.arange(lat_t, nlat), np.arange(lat_t)])
    flip2 = np.concatenate([flip, nlat + flip])
    ends = (np.arange(0, nlon, lon_t)[None, :] + np.array([[-1], [lon_t]])).reshape(-1) % nlon
    zonal_in = jnp.asarray(np.concatenate([zonal, zonal[:, ends]], axis=1))
    zonal_out = jnp.asarray(
        np.concatenate([zonal[:nlon], zonal[:nlon][ends], zonal[nlon:], zonal[nlon:][ends]], axis=0)
    )
    forward = jnp.where(hemi == 0, jnp.asarray(forward), jnp.asarray(forward[:, flip]))
    inverse = jnp.where(hemi == 0, jnp.asarray(inverse), jnp.asarray(inverse[flip2]))
    side = jnp.stack([hemi == 1, hemi == 0]).astype(F32)
    masks = jnp.broadcast_to(side[:, None], (2, chans))
    area = lax.dynamic_slice_in_dim(jnp.asarray(area_all, F32), hemi * lat_t, lat_t)
    area_wide = jnp.broadcast_to(area[:, None], (lat_t, chans))
    up = [(i, (i + 1) % lon_n) for i in range(lon_n)]
    down = [(t, s) for s, t in up]
    swap = [(0, 1), (1, 0)]
    chunks = range(pool // CHUNK)

    traded, deps = [], []
    for c in chunks:
        traded.append(lax.ppermute(pick_call(info, states, c, 1, deps), "lat", swap))
        deps = traded[:1]
    held = lax.optimization_barrier((traded[0], ocean, sea_temp, valid, w_enc, w_mid, w_dec, biases))
    _, ocean, sea_temp, valid, w_enc, w_mid, w_dec, biases = held
    sea = ocean.astype(F32) * sea_temp.astype(F32)
    cells = lon_t * lat_t
    lane = jnp.arange(chans)
    wide_sea = sea.reshape(pool, cells, 1).astype(BF16)
    wide_valid = valid.reshape(pool, cells, 1).astype(BF16)
    extra = jnp.where(lane < 3, wide_sea, jnp.where(lane < 6, jnp.ones((), BF16), wide_valid))
    extra = jnp.where(lane < 7, extra, jnp.zeros((), BF16))
    layers = [layer_weights(w_enc[i], w_mid[i], w_dec[i], biases[i]) for i in range(2)]

    last = [forward]

    def then(result, pick=None):
        last[:] = [result if pick is None else result[pick]]
        return result

    def over_lon(spec):
        return lax.all_to_all(spec, "lon", split_axis=0, concat_axis=0, tiled=True)

    class Chunk:
        def __init__(self, c):
            self.c = c
            self.early = 0
            self.round = 0
            self.other = traded[c]
            self.field0, self.pres = [None, None], [None, None]
            self.fresh, self.low, self.s_ext, self.gm = ([None, None] for _ in range(4))

        def legendre(self):
            half = self.early
            own, late = (states, states) if self.round == 0 else (self.low[half], self.low[1 - half])
            there = self.c if self.round == 0 else None
            wide = self.round == 2
            got = legendre_call(info, own, late, there, half, self.other, forward, last, wide)
            spec, to_up, to_down, sides = then(got, 0)
            self.spec = over_lon(spec)
            self.lo, self.hi = lax.ppermute(to_up, "lon", up), lax.ppermute(to_down, "lon", down)
            self.rows_of = (own, self.other) if wide else (sides,)

        def zonal(self):
            table = zonal_in if self.round == 2 else zonal_out
            self.spec = over_lon(then(zonal_call(self.spec, table, last, self.round == 2)))

        def synthesis(self):
            got = synthesis_call(
                info, self.spec, self.lo, self.hi, inverse, self.rows_of, HALF, self.round < 2, last
            )
            own, send = then(got, 0)
            self.s_ext[self.early] = own
            self.s_ext[1 - self.early] = lax.ppermute(send, "lat", swap)

        def forward(self, late):
            half = self.early ^ late
            field = (states, self.s_ext[half], self.lo, self.hi, extra, masks)
            self.field0[half] = field
            got = forward_call(info, self.c, half, late, field, layers[0], last)
            self.fresh[half], self.low[half], *pre = then(got, 1)
            self.pres[half] = pre
            self.send(half, late)

        def turn(self, late, before):
            half = self.early ^ late
            field = (self.fresh[half], self.s_ext[half], self.lo, self.hi, extra, masks)
            got = turn_call(
                info, self.c, half, late, field, layers[1], targets, area_wide, last, before
            )
            self.gm[half], self.low[half], before = then(got, 1)
            self.send(half, late)
            return before

        def send(self, half, late):
            if not late:
                self.other = lax.ppermute(self.low[half], "lat", swap)

        def flip(self):
            self.early = 1 - self.early
            self.round += 1

        def bottom(self, late, before):
            half = self.early ^ late
            got = bottom_call(
                info, self.c, half, late, self.field0[half], layers[0], self.pres[half],
                self.gm[half], self.lo, self.hi, late, self.s_ext[half], last, before,
            )
            return then(got)

    a, b = (Chunk(c) for c in chunks)
    top, low = None, None
    a.legendre()
    a.zonal()
    b.legendre()
    for one, two in ((a, b), (b, a)):
        one.synthesis()
        one.forward(0)
        two.zonal()
        one.forward(1)
        one.flip()
        one.legendre()
    for one, two in ((a, b), (b, a)):
        one.synthesis()
        top = one.turn(0, top)
        two.zonal()
        top = one.turn(1, top)
        one.flip()
        one.legendre()
    a.synthesis()
    top, _ = lax.optimization_barrier((top, last[0]))
    upper = reduce_steps(top, ("core", "y", "x", "z"))
    low = a.bottom(0, low)
    b.zonal()
    last.append(next(upper))
    low = a.bottom(1, low)
    last.append(next(upper))
    b.synthesis()
    last.append(next(upper))
    low = b.bottom(0, low)
    last.append(next(upper))
    low = b.bottom(1, low)
    lower = reduce_steps(low, ("core", "x", "y", "z"))
    *_, high = upper
    *_, low = lower
    return low, high


def update_kernel(rate, taps_each, info, g0_ref, g1_ref, m0_ref, m1_ref, v0_ref, v1_ref, *refs):
    ins, outs = refs[:12], refs[12:]
    layer, part = pl.program_id(0), pl.program_id(1)
    chans, hid = ins[0].shape[2:]
    scale = 1.0 / v1_ref[4:5, 0:1]

    def apply(group, at, grad):
        w_ref, m_ref, a_ref = (ins[4 * i + group] for i in range(3))
        new_ref, mom_ref, avg_ref, copy_ref = (outs[4 * i + group] for i in range(4))
        scaled = grad * scale
        mom = MOMENTUM * m_ref[at] + scaled
        fresh = w_ref[at] - rate * (scaled + MOMENTUM * mom)
        new_ref[at] = fresh
        mom_ref[at] = mom
        avg_ref[at] = AVERAGE * a_ref[at] + (1.0 - AVERAGE) * fresh
        copy_ref[at] = fresh.astype(BF16)

    def layer_step(g_ref, m_ref):
        for tap in range(taps_each):
            apply(0, (0, tap), g_ref[tap * chans : (tap + 1) * chans])

        @pl.when(part == 0)
        def _():
            apply(1, (0,), m_ref[:hid])
            apply(2, (0,), m_ref[hid:].T)

    pl.when(layer == 0)(lambda: layer_step(g0_ref, m0_ref))
    pl.when(layer == 1)(lambda: layer_step(g1_ref, m1_ref))

    @pl.when((layer == 0) & (part == 0))
    def _():
        for i, v_ref in enumerate((v0_ref, v1_ref)):
            for r in range(4):
                wide = hid if r < 3 else chans
                at = (slice(i, i + 1), slice(r * hid, r * hid + wide))
                apply(3, at, v_ref[r : r + 1, :wide])


TAPS_EACH = 3


def update_call(rate, sums, arrays):
    w_enc, w_mid, w_dec, biases = arrays[:4]
    layers, taps, chans, hid = w_enc.shape
    one, _, three, _ = grad_layout(chans, hid)
    steps = taps // TAPS_EACH
    rows = TAPS_EACH * chans
    enc = pl.BlockSpec((1, TAPS_EACH, chans, hid), lambda i, p, info: (i, p, 0, 0))
    mid = pl.BlockSpec((1, hid, hid), lambda i, p, info: (i, 0, 0))
    dec = pl.BlockSpec((1, hid, chans), lambda i, p, info: (i, 0, 0))
    bias = whole(biases.shape)
    specs = [enc, mid, dec, bias]
    shapes = [w_enc.shape, w_mid.shape, w_dec.shape, biases.shape]
    grads = [
        pl.BlockSpec((rows, hid), lambda i, p, info: (jnp.where(i == 0, p, steps - 1), 0)),
        pl.BlockSpec((rows, hid), lambda i, p, info: (jnp.where(i == 0, 0, p), 0)),
        pl.BlockSpec((three - one, hid), lambda i, p, info: (one // (three - one), 0)),
        pl.BlockSpec((three - one, hid), lambda i, p, info: (one // (three - one), 0)),
        pl.BlockSpec((8, hid), lambda i, p, info: (three // 8, 0)),
        pl.BlockSpec((8, hid), lambda i, p, info: (three // 8, 0)),
    ]
    got = pl.pallas_call(
        functools.partial(update_kernel, rate, TAPS_EACH),
        grid_spec=pltpu.PrefetchScalarGridSpec(
            num_scalar_prefetch=1,
            grid=(layers, steps),
            in_specs=grads + specs * 3,
            out_specs=specs * 4,
        ),
        out_shape=[shape_of(s, F32) for s in shapes * 3] + [shape_of(s, BF16) for s in shapes],
        compiler_params=params(),
        cost_estimate=cost(8.0),
        name="update",
    )(jnp.zeros((1,), jnp.int32), sums[0], sums[1], sums[0], sums[1], sums[0], sums[1], *arrays)
    vecs = sums[1][three : three + 8]
    return (jnp.sum(vecs[3, chans:]), vecs[4, 0], *got)


def fits(states, w_mid, lon_n, lat_n):
    pool, lon_t, lat_t, chans = states.shape
    return (
        lat_n == 2
        and lon_n == 16
        and lon_t == 16
        and lat_t == 64
        and pool == 2 * CHUNK
        and chans == 128
        and w_mid.shape[1] == 2 * chans
        and w_mid.shape[0] == 2
    )


def with_halo(block, sides, width, periodic):
    for axis, dim in sides:
        count = lax.axis_size(axis)
        forward = [(i, i + 1) for i in range(count - 1)]
        if periodic:
            forward.append((count - 1, 0))
        backward = [(target, source) for source, target in forward]
        low = lax.ppermute(
            lax.slice_in_dim(block, block.shape[dim] - width, None, axis=dim), axis, forward
        )
        high = lax.ppermute(lax.slice_in_dim(block, 0, width, axis=dim), axis, backward)
        block = jnp.concatenate([low, block, high], axis=dim)
    return block


def tables(nlon, nlat, groups):
    coeffs = jnp.arange(2 * MW)
    wave = jnp.where(coeffs < MW, coeffs, coeffs - MW + 1).astype(jnp.float32)
    places = jnp.arange(nlon).astype(jnp.float32)
    angle = 2.0 * math.pi * wave[:, None] * places[None, :] / nlon
    fourier = jnp.where((coeffs < MW)[:, None], jnp.cos(angle), jnp.sin(angle)) * math.sqrt(
        2.0 / nlon
    )
    phase = ((jnp.arange(nlat).astype(jnp.float32) + 0.5) / nlat - 0.5) * math.pi
    sine = jnp.sin(phase)
    quad = jnp.cos(phase) * math.pi / nlat
    polys = [jnp.ones_like(sine), sine]
    for degree in range(1, NDEG - 1):
        polys.append(((2 * degree + 1) * sine * polys[-1] - degree * polys[-2]) / (degree + 1))
    stacked = jnp.stack(polys[:NDEG])
    degrees = jnp.arange(NDEG).astype(jnp.float32)
    legendre = jnp.sqrt((2 * degrees + 1) / 2)[:, None] * jnp.sqrt(quad)[None, :] * stacked
    damping = 1.5 * (1.0 - 2.0 * degrees * (degrees + 1) / (NDEG * (NDEG + 1)))
    filters = damping[None, :] * (1.0 - 0.5 * wave / MW)[:, None]
    kept = 2 * MW
    slots = (kept + groups - 1) // groups * groups
    fourier = jnp.pad(fourier, ((0, slots - kept), (0, 0)))
    filters = jnp.pad(filters, ((0, slots - kept), (0, 0)))
    return (fourier, legendre, filters)


def spectral(values, tabs):
    fourier, legendre, filters = tabs
    cycles = lax.all_to_all(
        values.astype(jnp.bfloat16), "lon", split_axis=3, concat_axis=1, tiled=True
    ).astype(values.dtype)
    coeff = jnp.einsum("kx,sxjc->skjc", fourier, cycles, precision=HIGH)
    block = fourier.shape[0] // lax.axis_size("lat")
    where = lax.axis_index("lat")
    block_filter = lax.dynamic_slice_in_dim(filters, where * block, block, 0)
    columns = lax.all_to_all(
        coeff.astype(jnp.bfloat16), "lat", split_axis=1, concat_axis=2, tiled=True
    ).astype(coeff.dtype)
    spec = (
        jnp.einsum("nj,skjc->sknc", legendre, columns, precision=HIGH)
        * block_filter[None, :, :, None]
    )
    back = jnp.einsum("nj,sknc->skjc", legendre, spec, precision=HIGH)
    coeff_back = lax.all_to_all(
        back.astype(jnp.bfloat16), "lat", split_axis=2, concat_axis=1, tiled=True
    ).astype(back.dtype)
    grid = jnp.einsum("kx,skjc->sxjc", fourier, coeff_back, precision=HIGH)
    return lax.all_to_all(
        grid.astype(jnp.bfloat16), "lon", split_axis=1, concat_axis=3, tiled=True
    ).astype(grid.dtype)


def extend(field):
    wider = with_halo(field, (("lon", 1),), 1, True)
    return with_halo(wider, (("lat", 2),), 1, False)


def neighbours(padded, flipped, lon_t, lat_t):
    parts = []
    for row_off in range(3):
        for col_off in range(3):
            first = 2 - row_off if flipped else row_off
            second = 2 - col_off if flipped else col_off
            parts.append(padded[:, first : first + lon_t, second : second + lat_t])
    stacked = jnp.stack(parts, axis=3)
    return stacked.reshape(-1, 9 * padded.shape[-1])


def gelu_fn(value):
    return jax.nn.gelu(value, approximate=True)


def gelu_back(value, grad):
    return jax.vjp(gelu_fn, value)[1](grad)[0]


def layer_forward(state, sea, enc, mid, dec, vec, tabs):
    hid = mid.shape[0]
    lon_t, lat_t = (state.shape[1], state.shape[2])
    moved = state + spectral(state, tabs)
    patches = neighbours(extend(moved.astype(jnp.bfloat16)), False, lon_t, lat_t)
    pre1 = jnp.dot(patches, enc, preferred_element_type=jnp.float32)
    pre1 = pre1 + sea.reshape(-1, 1) * vec[hid : 2 * hid] + vec[:hid]
    active1 = gelu_fn(pre1).astype(jnp.bfloat16)
    pre2 = jnp.dot(active1, mid, preferred_element_type=jnp.float32) + vec[2 * hid : 3 * hid]
    active2 = gelu_fn(pre2).astype(jnp.bfloat16)
    output = jnp.dot(active2, dec, preferred_element_type=jnp.float32) + vec[3 * hid :]
    return (moved + output.reshape(state.shape), (patches, pre1, active1, pre2, active2))


def layer_backward(grad_state, sea, enc, mid, dec, saved, tabs):
    patches, pre1, active1, pre2, active2 = saved
    hid = mid.shape[0]
    shape = grad_state.shape
    chans = shape[-1]
    g_out = grad_state.reshape(-1, chans).astype(jnp.bfloat16)
    g_dec = jnp.einsum("rh,rc->hc", active2, g_out, preferred_element_type=jnp.float32)
    g_act2 = jnp.einsum("rc,hc->rh", g_out, dec, preferred_element_type=jnp.float32)
    g_pre2 = gelu_back(pre2, g_act2).astype(jnp.bfloat16)
    g_mid = jnp.einsum("rh,rg->hg", active1, g_pre2, preferred_element_type=jnp.float32)
    g_act1 = jnp.einsum("rg,hg->rh", g_pre2, mid, preferred_element_type=jnp.float32)
    g_pre1 = gelu_back(pre1, g_act1).astype(jnp.bfloat16)
    g_enc = jnp.einsum("rk,rh->kh", patches, g_pre1, preferred_element_type=jnp.float32)
    wide1 = g_pre1.astype(jnp.float32)
    g_vec = jnp.concatenate(
        [
            jnp.sum(wide1, 0),
            jnp.sum(sea.reshape(-1, 1) * wide1, 0),
            jnp.sum(g_pre2.astype(jnp.float32), 0),
            jnp.sum(g_out.astype(jnp.float32), 0),
        ]
    )
    spread = extend(g_pre1.reshape(shape[0], shape[1], shape[2], hid))
    gathered = neighbours(spread, True, shape[1], shape[2]).reshape(-1, 9, hid)
    g_input = jnp.einsum(
        "rkh,kch->rc", gathered, enc.reshape(9, chans, hid), preferred_element_type=jnp.float32
    )
    grad_moved = grad_state + g_input.reshape(shape)
    return (grad_moved + spectral(grad_moved, tabs), (g_enc, g_mid, g_dec, g_vec))


def general_grads(states, targets, sea_temp, ocean, valid, order, w_enc, w_mid, w_dec, biases):
    pool, lon_t, lat_t, chans = states.shape
    layers, hid = (w_mid.shape[0], w_mid.shape[1])
    nlon = lon_t * lax.axis_size("lon")
    nlat = lat_t * lax.axis_size("lat")
    tabs = tables(nlon, nlat, lax.axis_size("lat"))
    lat_glob = (lax.axis_index("lat") * lat_t + jnp.arange(lat_t)).astype(jnp.float32)
    area = jnp.cos(((lat_glob + 0.5) / nlat - 0.5) * math.pi)
    enc_low = w_enc.astype(jnp.bfloat16).reshape(layers, 9 * chans, hid)
    mid_low = w_mid.astype(jnp.bfloat16)
    dec_low = w_dec.astype(jnp.bfloat16)
    snaps = pool // MB
    sums = [
        jnp.zeros((layers, 9 * chans, hid), jnp.float32),
        jnp.zeros_like(w_mid),
        jnp.zeros_like(w_dec),
        jnp.zeros_like(biases),
    ]
    loss = jnp.zeros((), jnp.float32)
    total = jnp.zeros((), jnp.float32)
    for batch_id in range(MB):
        picks = lax.dynamic_slice_in_dim(order, batch_id * snaps, snaps)
        state = jnp.take(states, picks, axis=0).astype(jnp.float32)
        target = jnp.take(targets, picks, axis=0).astype(jnp.float32)
        sea = jnp.take(ocean, picks, axis=0).astype(jnp.float32) * jnp.take(
            sea_temp, picks, axis=0
        ).astype(jnp.float32)
        weight = jnp.take(valid, picks, axis=0).astype(jnp.float32) * area[None, None, :]
        kept = []
        for layer_id in range(layers):
            state, saved = layer_forward(
                state,
                sea,
                enc_low[layer_id],
                mid_low[layer_id],
                dec_low[layer_id],
                biases[layer_id],
                tabs,
            )
            kept.append(saved)
        diff = state - target
        loss = loss + jnp.sum(weight[..., None] * diff * diff)
        total = total + jnp.sum(weight)
        grad_state = 2.0 * weight[..., None] * diff
        for layer_id in reversed(range(layers)):
            grad_state, found = layer_backward(
                grad_state,
                sea,
                enc_low[layer_id],
                mid_low[layer_id],
                dec_low[layer_id],
                kept[layer_id],
                tabs,
            )
            sums = [acc.at[layer_id].add(part) for acc, part in zip(sums, found)]
    g_enc, g_mid, g_dec, g_vec, loss, total = lax.psum(
        (sums[0], sums[1], sums[2], sums[3], loss, total), ("lon", "lat")
    )
    return g_enc.reshape(w_enc.shape), g_mid, g_dec, g_vec, loss, total


def body(
    states,
    targets,
    sea_temp,
    ocean,
    valid,
    order,
    w_enc,
    w_mid,
    w_dec,
    biases,
    mom_enc,
    mom_mid,
    mom_dec,
    mom_bias,
    avg_enc,
    avg_mid,
    avg_dec,
    avg_bias,
):
    pool, lon_t, lat_t = states.shape[:3]
    lon_n, lat_n = lax.axis_size("lon"), lax.axis_size("lat")
    rate = RATE_BASE * math.sqrt(pool * lon_t * lon_n * lat_t * lat_n)
    if fits(states, w_mid, lon_n, lat_n):
        sums = fast_grads(states, targets, sea_temp, ocean, valid, w_enc, w_mid, w_dec, biases)
        arrays = (w_enc, w_mid, w_dec, biases, mom_enc, mom_mid, mom_dec, mom_bias)
        arrays += (avg_enc, avg_mid, avg_dec, avg_bias)
        return update_call(rate, sums, arrays)
    found = general_grads(
        states, targets, sea_temp, ocean, valid, order, w_enc, w_mid, w_dec, biases
    )
    loss, total = found[4:]
    grads = (found[0].reshape(w_enc.shape),) + found[1:4]
    news, moms, avgs, copies = ([], [], [], [])
    for weight_now, grad, mom, avg in zip(
        (w_enc, w_mid, w_dec, biases),
        grads,
        (mom_enc, mom_mid, mom_dec, mom_bias),
        (avg_enc, avg_mid, avg_dec, avg_bias),
    ):
        scaled = grad / total
        mom_new = MOMENTUM * mom + scaled
        fresh = weight_now - rate * (scaled + MOMENTUM * mom_new)
        news.append(fresh)
        moms.append(mom_new)
        avgs.append(AVERAGE * avg + (1.0 - AVERAGE) * fresh)
        copies.append(fresh.astype(jnp.bfloat16))
    return (
        loss,
        total,
        news[0],
        news[1],
        news[2],
        news[3],
        moms[0],
        moms[1],
        moms[2],
        moms[3],
        avgs[0],
        avgs[1],
        avgs[2],
        avgs[3],
        copies[0],
        copies[1],
        copies[2],
        copies[3],
    )


def solution(mesh):
    placed = (
        P(None, "lon", "lat", None),
        P(None, "lon", "lat", None),
        P(None, "lon", "lat"),
        P(None, "lon", "lat"),
        P(None, "lon", "lat"),
        P(),
        P(),
        P(),
        P(),
        P(),
        P(),
        P(),
        P(),
        P(),
        P(),
        P(),
        P(),
        P(),
    )
    return jax.shard_map(
        body,
        mesh=mesh,
        in_specs=placed,
        out_specs=(
            P(),
            P(),
            P(),
            P(),
            P(),
            P(),
            P(),
            P(),
            P(),
            P(),
            P(),
            P(),
            P(),
            P(),
            P(),
            P(),
            P(),
            P(),
        ),
        check_vma=False,
    )
```

```python
import functools
import math

import jax
import jax.numpy as jnp
import numpy as np
from jax import lax
from jax.experimental import pallas as pl
from jax.experimental.pallas import tpu as pltpu
from jax.sharding import PartitionSpec as P

MW = 86
NDEG = 86
MB = 4


HIGH = lax.Precision.HIGHEST
MOMENTUM = 0.9
AVERAGE = 0.99
RATE_BASE = 0.0006

F32 = jnp.float32
BF16 = jnp.bfloat16
CHUNK = 4
VMEM = 56 * 1024 * 1024
GELU_A = math.sqrt(2.0 / math.pi)
GELU_B = 0.044715


def split_table(table):
    table = np.asarray(table, np.float32)
    high = table.astype(BF16)
    low = (table - high.astype(np.float32)).astype(BF16)
    return np.concatenate([high, low], axis=0)


def host_tables(nlon, nlat, deg):
    kept = np.arange(2 * MW)
    wave = np.where(kept < MW, kept, kept - MW + 1).astype(np.float64)
    angle = 2.0 * np.pi * wave[:, None] * np.arange(nlon)[None, :] / nlon
    fourier = np.where((kept < MW)[:, None], np.cos(angle), np.sin(angle)) * np.sqrt(2.0 / nlon)
    zonal = (fourier * (1.0 - 0.5 * wave / MW)[:, None]).T @ fourier
    phase = ((np.arange(nlat) + 0.5) / nlat - 0.5) * np.pi
    sine, area = np.sin(phase), np.cos(phase)
    polys = [np.ones_like(sine), sine]
    for n in range(1, NDEG - 1):
        polys.append(((2 * n + 1) * sine * polys[-1] - n * polys[-2]) / (n + 1))
    degrees = np.arange(NDEG)
    legendre = np.sqrt((2 * degrees + 1) / 2)[:, None] * np.sqrt(area * np.pi / nlat)[None, :]
    legendre = legendre * np.stack(polys)
    damping = 1.5 * (1.0 - 2.0 * degrees * (degrees + 1) / (NDEG * (NDEG + 1)))
    forward = np.zeros((deg, nlat))
    forward[:NDEG] = legendre
    inverse = np.zeros((nlat, -(-deg // 32) * 32))
    inverse[:, :NDEG] = (legendre * damping[:, None]).T
    return split_table(zonal), split_table(forward), split_table(inverse), area


def mm(a, b):
    return jnp.dot(a, b, preferred_element_type=F32)


def mm_rows(a, b):
    return lax.dot_general(a, b, (((0,), (0,)), ((), ())), preferred_element_type=F32)


def whole(shape):
    return pl.BlockSpec(shape, lambda *_: (0,) * len(shape))


def params():
    return pltpu.CompilerParams(vmem_limit_bytes=VMEM)


HALF = CHUNK // 2


def any_spec():
    return pl.BlockSpec(memory_space=pl.ANY)


def shape_of(dims, dtype):
    return jax.ShapeDtypeStruct(dims, dtype)


def grid_of(count, in_specs, out_specs, scratch):
    return pltpu.PrefetchScalarGridSpec(
        num_scalar_prefetch=1,
        grid=(count,),
        in_specs=in_specs,
        out_specs=out_specs,
        scratch_shapes=scratch,
    )


def first_of(chunk, half, info):
    if chunk is None:
        return 0
    return chunk * CHUNK + HALF * (info[0] if half == 0 else 1 - info[0])


def snap_spec(dims, chunk=None, half=0):
    return pl.BlockSpec(
        (1,) + dims, lambda g, info: (first_of(chunk, half, info) + g,) + (0,) * len(dims)
    )


def pick_kernel(info, x_ref, *refs):
    refs[-1][...] = x_ref[...]


def pick_call(info, fields, chunk, half, deps):
    dims = fields.shape[1:]
    return pl.pallas_call(
        pick_kernel,
        grid_spec=grid_of(
            HALF, [snap_spec(dims, chunk, half)] + [any_spec()] * len(deps), snap_spec(dims), []
        ),
        out_shape=shape_of((HALF,) + dims, fields.dtype),
        compiler_params=params(),
        cost_estimate=cost(1.0),
        name="pick",
    )(info, fields, *deps)


def legendre_kernel(
    wide, info, own_ref, other_ref, first_ref, last_ref, l_ref, *refs
):
    o_ref, up_ref, down_ref, rows_ref, tmp = refs[-5:]
    parts, rows, lon_t, chans = o_ref.shape
    lat_t = own_ref.shape[2]
    deg = l_ref.shape[0] // 2
    count = lon_t + 2 if wide else lon_t
    each = deg // parts
    place = lax.broadcasted_iota(jnp.int32, (lat_t, chans), 0)
    south = info[0] == 1
    inner = place == jnp.where(south, 0, lat_t - 1)
    other_inner = place == jnp.where(south, lat_t - 1, 0)

    def column(x):
        own, other = own_ref[0, x], other_ref[0, x]
        if wide:
            to_own = other_ref[0, count, x : x + 1].astype(F32)
            to_other = own_ref[0, count, x : x + 1].astype(F32)
            own = (own.astype(F32) + jnp.where(inner, to_own, 0.0)).astype(BF16)
            other = (other.astype(F32) + jnp.where(other_inner, to_other, 0.0)).astype(BF16)
        else:
            own_f, other_f = own.astype(F32), other.astype(F32)
            ends = [(own_f[:1], own_f[lat_t - 1 :]), (other_f[lat_t - 1 :], other_f[:1])]
            for i, (if_south, if_north) in enumerate(ends):
                rows_ref[0, i, x : x + 1] = jnp.where(south, if_south, if_north)
        return jnp.concatenate([own, other], axis=0)

    for base in range(0, count, 4):
        span = range(base, min(base + 4, count))
        r = mm(l_ref[...], jnp.concatenate([column(x) for x in span], axis=1))
        r = r[:deg] + r[deg:]
        for x in span:
            tmp[:, x, :] = r[:, (x - base) * chans : (x - base + 1) * chans]
    o_ref[:, :each] = tmp[:, :lon_t, :].astype(BF16).reshape(parts, each, lon_t, chans)
    if wide:
        rest = jnp.zeros((lon_t - each, chans), F32)
        for p in range(parts):
            for side in range(2):
                edge = tmp[p * each : (p + 1) * each, lon_t + side, :]
                o_ref[p, each + side] = jnp.concatenate([edge, rest], axis=0).astype(BF16)
        rows_ref[...] = jnp.zeros_like(rows_ref)
    for ref, late_ref, x in ((down_ref, first_ref, 0), (up_ref, last_ref, lon_t - 1)):
        if wide:
            at = lon_t if x == 0 else lon_t + 1
            corner, far = other_ref[0, count, at : at + 1], own_ref[0, count, at : at + 1]
            pieces = [jnp.broadcast_to(v.astype(F32), (8, chans)) for v in (corner, far)]
        else:
            at = x
            pieces = [jnp.broadcast_to(rows_ref[0, 1, x : x + 1], (16, chans))]
        ref[0, 0, :lat_t] = own_ref[0, at]
        ref[0, 0, lat_t:] = jnp.concatenate(pieces, axis=0).astype(BF16)
        ref[0, 1, :lat_t] = late_ref[0, 0]
        ref[0, 1, lat_t:] = jnp.zeros((16, chans), BF16)


def legendre_call(info, own, late, chunk, half, other, table, deps, wide):
    snaps, slabs, lat_t, chans = other.shape
    deg = table.shape[0] // 2
    parts = 8
    lon_t = slabs - 3 if wide else slabs
    rows = deg // parts + (2 if wide else 0)
    message = (2, lat_t + 16, chans)
    sides = (2, lon_t, chans)

    def late_column(x):
        return pl.BlockSpec(
            (1, 1, lat_t, chans), lambda g, info: (first_of(chunk, 1 - half, info) + g, x, 0, 0)
        )

    columns = (lon_t, lon_t + 1) if wide else (0, lon_t - 1)
    return pl.pallas_call(
        functools.partial(legendre_kernel, wide),
        grid_spec=grid_of(
            snaps,
            [
                snap_spec(own.shape[1:], chunk, half),
                snap_spec(other.shape[1:]),
                late_column(columns[0]),
                late_column(columns[1]),
                whole(table.shape),
            ]
            + [any_spec()] * len(deps),
            [
                pl.BlockSpec((parts, rows, lon_t, chans), lambda s, info: (s, 0, 0, 0)),
                snap_spec(message),
                snap_spec(message),
                snap_spec(sides),
            ],
            [pltpu.VMEM((deg, lon_t + 8 if wide else lon_t, chans), F32)],
        ),
        out_shape=[
            shape_of((snaps * parts, rows, lon_t, chans), BF16),
            shape_of((snaps,) + message, BF16),
            shape_of((snaps,) + message, BF16),
            shape_of((snaps,) + sides, F32),
        ],
        compiler_params=params(),
        cost_estimate=cost(3.4),
        name="legendre",
    )(info, own, other, late, late, table, *deps)


def zonal_kernel(wide_in, x_ref, a_ref, *refs):
    o_ref, tmp = refs[-2:]
    groups, _, lon_t, chans = x_ref.shape
    nlon = groups * lon_t
    rows = min(x_ref.shape[1], o_ref.shape[1])
    if wide_in:
        for side in range(2):
            tmp[side * groups : (side + 1) * groups] = x_ref[:, rows + side].astype(F32)
    else:
        tmp[...] = jnp.zeros_like(tmp)
    for base in range(0, rows, 4):
        span = range(base, min(base + 4, rows))
        fields = jnp.concatenate([x_ref[:, n].reshape(nlon, chans) for n in span], axis=1)
        if wide_in:
            edges = jnp.concatenate([tmp[:, n, :] for n in span], axis=1).astype(BF16)
            r = mm(a_ref[:, :nlon], fields) + mm(a_ref[:, nlon:], edges)
            r = r[:nlon] + r[nlon:]
        else:
            r = mm(a_ref[...], fields)
            size = r.shape[0] // 2
            r = r[:size] + r[size:]
        low = r[:nlon].astype(BF16)
        for n in span:
            lanes = slice((n - base) * chans, (n - base + 1) * chans)
            o_ref[:, n] = low[:, lanes].reshape(groups, lon_t, chans)
            if not wide_in:
                tmp[:, n, :] = r[nlon:, lanes]
    if not wide_in:
        for side in range(2):
            o_ref[:, rows + side] = tmp[side * groups : (side + 1) * groups].astype(BF16)


def zonal_call(fields, table, deps, wide_in):
    groups, rows, lon_t, chans = fields.shape
    out = (groups, rows - 2 if wide_in else rows + 2, lon_t, chans)
    return pl.pallas_call(
        functools.partial(zonal_kernel, wide_in),
        in_specs=[pl.BlockSpec(memory_space=pltpu.VMEM)] * 2 + [any_spec()] * len(deps),
        out_specs=pl.BlockSpec(memory_space=pltpu.VMEM),
        out_shape=shape_of(out, BF16),
        scratch_shapes=[pltpu.VMEM((2 * groups, lon_t, chans), F32)],
        compiler_params=params(),
        cost_estimate=cost(2.8),
        name="zonal",
    )(fields, table, *deps)


def synthesis_kernel(wide, info, x_ref, lo_ref, hi_ref, l_ref, *refs):
    rows_refs = refs[: 1 if wide else 2]
    own_ref, send_ref, tmp, side = refs[-4:]
    parts, rows, lon_t, chans = x_ref.shape
    each = rows - 2 if wide else rows
    deg = parts * each
    count = lon_t + 2 if wide else lon_t
    nlat = l_ref.shape[0] // 2
    half = nlat // 2
    south = info[0] == 1
    tmp[:deg, :lon_t, :] = x_ref[:, :each].reshape(deg, lon_t, chans).astype(F32)
    if wide:
        for p in range(parts):
            for e in range(2):
                tmp[p * each : (p + 1) * each, lon_t + e, :] = x_ref[p, each + e, :each].astype(F32)
    tmp[deg:] = jnp.zeros((tmp.shape[0] - deg,) + tmp.shape[1:], F32)
    side[...] = jnp.zeros_like(side)
    low, high = lo_ref[0, 0].astype(F32), hi_ref[0, 0].astype(F32)
    if wide:
        sides_ref = rows_refs[0]
        for i in range(2):
            side[i, :lon_t] = sides_ref[0, 1 - i]
        for at, edge in ((lon_t, low), (lon_t + 1, high)):
            side[0, at : at + 1] = edge[half : half + 1]
            side[1, at : at + 1] = jnp.where(south, edge[:1], edge[half - 1 : half])
    else:
        for i, ref in enumerate(rows_refs[::-1]):
            side[i, :lon_t] = ref[0, 0, :lon_t].astype(F32)
            for at, edge in ((0, low), (lon_t - 1, high)):
                side[i, at : at + 1] += edge[half + 8 * i : half + 8 * i + 1]
    for base in range(0, count, 4):
        span = range(base, min(base + 4, count))
        cols = jnp.concatenate([tmp[:, x, :] for x in span], axis=1).astype(BF16)
        r = mm(l_ref[...], cols)
        r = r[:nlat] + r[nlat:]
        for x in span:
            one = r[:, (x - base) * chans : (x - base + 1) * chans]
            own_ref[0, x] = one[:half].astype(BF16)
            send_ref[0, x] = one[half:].astype(BF16)
            if wide:
                side[0, x : x + 1] += jnp.where(south, one[2 * half - 1 :], one[half : half + 1])
                side[1, x : x + 1] += jnp.where(south, one[:1], one[half - 1 : half])
    rest = jnp.zeros((half - side.shape[1], chans), F32)
    for i, ref in enumerate((own_ref, send_ref)):
        ref[0, count] = jnp.concatenate([side[i], rest], axis=0).astype(BF16)


def synthesis_call(info, coeffs, lo, hi, table, rows_of, snaps, wide, deps):
    total, rows, lon_t, chans = coeffs.shape
    parts = total // snaps
    nlat = table.shape[0] // 2
    slabs = lon_t + 3 if wide else lon_t + 1
    out = snap_spec((slabs, nlat // 2, chans))
    message = pl.BlockSpec((1, 1) + lo.shape[2:], lambda s, info: (s, 0, 0, 0))
    if wide:
        row_specs = [snap_spec(r.shape[1:]) for r in rows_of]
    else:
        last = pl.BlockSpec((1, 1) + rows_of[0].shape[2:], lambda s, info: (s, lon_t + 2, 0, 0))
        row_specs = [last for _ in rows_of]
    return pl.pallas_call(
        functools.partial(synthesis_kernel, wide),
        grid_spec=grid_of(
            snaps,
            [
                pl.BlockSpec((parts, rows, lon_t, chans), lambda s, info: (s, 0, 0, 0)),
                message,
                message,
                whole(table.shape),
            ]
            + row_specs
            + [any_spec()] * len(deps),
            [out, out],
            [
                pltpu.VMEM((table.shape[1], lon_t + 8 if wide else lon_t, chans), F32),
                pltpu.VMEM((2, lon_t + 8, chans), F32),
            ],
        ),
        out_shape=[shape_of((snaps, slabs, nlat // 2, chans), BF16)] * 2,
        compiler_params=params(),
        cost_estimate=cost(3.6),
        name="synthesis",
    )(info, coeffs, lo, hi, table, *rows_of, *deps)


def gelu_of(x):
    t = jnp.tanh(x * (GELU_A + (GELU_A * GELU_B) * (x * x)))
    return 0.5 * x * (1.0 + t)


def gelu_and_slope(x):
    sq = x * x
    t = jnp.tanh(x * (GELU_A + (GELU_A * GELU_B) * sq))
    cdf = 0.5 + 0.5 * t
    slope = cdf + (0.5 * x) * (1.0 - t * t) * (GELU_A + (3.0 * GELU_A * GELU_B) * sq)
    return x * cdf, slope


def fill_patches(patches, slabs, ends, masks):
    lat_t, chans = slabs[0].shape
    lon_t = len(slabs) - 2
    place = lax.broadcasted_iota(jnp.int32, (lat_t, chans), 0)
    for i in range(lon_t + 2):
        low_row, high_row = ends[i] * masks[0:1], ends[i] * masks[1:2]
        down = jnp.where(place == 0, low_row, pltpu.roll(slabs[i], 1, 0)).astype(BF16)
        up = jnp.where(place == lat_t - 1, high_row, pltpu.roll(slabs[i], lat_t - 1, 0)).astype(BF16)
        mid = slabs[i].astype(BF16)
        for a in range(3):
            x = i - a
            if 0 <= x < lon_t:
                for b, piece in enumerate((down, mid, up)):
                    k = 3 * a + b
                    patches[x * lat_t : (x + 1) * lat_t, k * chans : (k + 1) * chans] = piece


def assemble(patches, field_refs, moved):
    state_ref, s_ref, lo_ref, hi_ref, extra_ref, masks_ref = field_refs
    lon_t, lat_t, chans = moved.shape
    moved[...] = state_ref[0].astype(F32) + s_ref[0, :lon_t].astype(F32)
    rows = s_ref[0, lon_t + 2].astype(F32)
    slabs = [lo_ref[0, 0, :lat_t].astype(F32) + s_ref[0, lon_t].astype(F32)]
    slabs += [moved[i] for i in range(lon_t)]
    slabs += [hi_ref[0, 0, :lat_t].astype(F32) + s_ref[0, lon_t + 1].astype(F32)]
    ends = [rows[i : i + 1] for i in [lon_t] + list(range(lon_t)) + [lon_t + 1]]
    fill_patches(patches, slabs, ends, masks_ref[...])
    patches[:, 9 * chans :] = extra_ref[0]


def forward_kernel(info, *refs):
    field_refs, (w1_ref, mid_ref, dec_ref, bias_ref) = refs[:6], refs[6:10]
    state_out, low_out, pre1_out, pre2_out, patches, moved = refs[-6:]
    lon_t, lat_t, chans = moved.shape
    hid = mid_ref.shape[0]
    assemble(patches, field_refs, moved)
    pre1 = mm(patches[...], w1_ref[...])
    pre1_out[0] = pre1
    active1 = gelu_of(pre1).astype(BF16)
    pre2 = mm(active1, mid_ref[...]) + bias_ref[0:1, :hid]
    pre2_out[0] = pre2
    active2 = gelu_of(pre2).astype(BF16)
    out = mm(active2, dec_ref[...]) + bias_ref[1:2, :chans]
    state_out[0] = moved[...] + out.reshape(lon_t, lat_t, chans)
    low_out[0] = state_out[0].astype(BF16)


GRAD_PAD = 128


def grad_layout(chans, hid):
    one, two, three = 9 * chans, 9 * chans + hid, 9 * chans + hid + chans
    return (one, two, three, -(-(three + 8) // GRAD_PAD) * GRAD_PAD)


def add_grads(first, out, before, patches, active1, active2, g_out, g_pre2, g_pre1, ends):
    chans, hid = g_out.shape[1], g_pre1.shape[1]
    one, two, three, _ = grad_layout(chans, hid)
    enc = mm_rows(patches[...], g_pre1[...])
    pieces = [
        (0, one, enc[:one]),
        (one, two, mm_rows(active1[...], g_pre2[...])),
        (two, three, mm_rows(g_out[...], active2[...])),
    ]

    @pl.when(first)
    def _():
        ends[...] = enc[one : one + 8]
        for start, stop, piece in pieces:
            out[start:stop] = piece if before is None else before[start:stop] + piece

    @pl.when(jnp.logical_not(first))
    def _():
        ends[...] += enc[one : one + 8]
        for start, stop, piece in pieces:
            out[start:stop] += piece


def pack_grads(out, before, chans, hid, ends, vecs):
    _, _, three, rows = grad_layout(chans, hid)
    tail = jnp.concatenate([vecs[2:3, :chans], vecs[1:2, :chans]], axis=1)
    out[three:] = jnp.zeros((rows - three, hid), F32)
    for row, piece in enumerate((ends[3:4], ends[0:1], vecs[0:1], tail, vecs[3:4])):
        at = slice(three + row, three + row + 1)
        out[at] = piece if before is None else before[at] + piece


def turn_kernel(more, info, *refs):
    field_refs, (w1_ref, mid_ref, dec_ref, bias_ref) = refs[:6], refs[6:10]
    extra_ref, masks_ref = field_refs[4:]
    target_ref, area_ref, w1t_ref, midt_ref, dect_ref = refs[10:15]
    before = refs[15] if more else None
    (
        gm_out, low_out, grads_out,
        patches, moved, active1, active2, slope1, slope2, g_out, g_pre2, g_pre1, spread,
        ends, vecs, side,
    ) = refs[-16:]
    lon_t, lat_t, chans = moved.shape
    hid = mid_ref.shape[0]
    first = pl.program_id(0) == 0
    assemble(patches, field_refs, moved)
    spread[...] = jnp.zeros_like(spread)

    @pl.when(first)
    def _():
        vecs[...] = jnp.zeros_like(vecs)
        side[...] = jnp.zeros_like(side)

    step = 8
    for x in range(0, lon_t, step):
        rows = slice(x * lat_t, (x + step) * lat_t)
        pre1 = mm(patches[rows], w1_ref[...])
        a1, d1 = gelu_and_slope(pre1)
        active1[rows] = a1.astype(BF16)
        slope1[rows] = d1
        pre2 = mm(active1[rows], mid_ref[...]) + bias_ref[0:1, :hid]
        a2, d2 = gelu_and_slope(pre2)
        active2[rows] = a2.astype(BF16)
        slope2[rows] = d2
        out = mm(active2[rows], dec_ref[...]) + bias_ref[1:2, :chans]
        fresh = moved[x : x + step] + out.reshape(step, lat_t, chans)
        diff = fresh - target_ref[0, x : x + step].astype(F32)
        valid = jnp.broadcast_to(extra_ref[0, rows, 6:7].astype(F32), (step * lat_t, chans))
        weight = valid.reshape(step, lat_t, chans) * area_ref[...][None]
        vecs[3:4, :chans] += jnp.sum(weight.reshape(step * lat_t, chans), 0, keepdims=True)
        weighted = weight * diff
        vecs[1:2, :chans] += jnp.sum((weighted * diff).reshape(step * lat_t, chans), 0, keepdims=True)
        grad = 2.0 * weighted
        moved[x : x + step] = grad
        low = grad.reshape(step * lat_t, chans).astype(BF16)
        g_out[rows] = low
        vecs[2:3, :chans] += jnp.sum(low.astype(F32), 0, keepdims=True)
        gp2 = (mm(low, dect_ref[...]) * slope2[rows]).astype(BF16)
        g_pre2[rows] = gp2
        vecs[0:1] += jnp.sum(gp2.astype(F32), 0, keepdims=True)
        gp1 = (mm(gp2, midt_ref[...]) * slope1[rows]).astype(BF16)
        g_pre1[rows] = gp1
        taps = mm(gp1, w1t_ref[...])
        for a in range(3):
            for b in range(3):
                k = 3 * a + b
                spread[b, x + a : x + a + step] += taps[:, k * chans : (k + 1) * chans].reshape(
                    step, lat_t, chans
                )
    place = lax.broadcasted_iota(jnp.int32, (lat_t, chans), 0)
    masks = masks_ref[...]
    for i in range(lon_t + 2):
        down, here, up = spread[0, i], spread[1, i], spread[2, i]
        got = here + jnp.where(place == lat_t - 1, 0.0, pltpu.roll(down, lat_t - 1, 0))
        got = got + jnp.where(place == 0, 0.0, pltpu.roll(up, 1, 0))
        beyond = down[0:1] * masks[0:1] + up[lat_t - 1 : lat_t] * masks[1:2]
        if i in (0, lon_t + 1):
            at = lon_t if i == 0 else lon_t + 1
            low_out[0, at] = got.astype(BF16)
        else:
            at = i - 1
            total = got + moved[at]
            gm_out[0, at] = total
            low_out[0, at] = total.astype(BF16)
        side[at : at + 1] = beyond
    rest = jnp.zeros((lat_t - side.shape[0], chans), F32)
    low_out[0, lon_t + 2] = jnp.concatenate([side[...], rest], axis=0).astype(BF16)
    add_grads(first, grads_out, before, patches, active1, active2, g_out, g_pre2, g_pre1, ends)

    @pl.when(pl.program_id(0) == pl.num_programs(0) - 1)
    def _():
        pack_grads(grads_out, before, chans, hid, ends, vecs)


def bottom_kernel(more, info, *refs):
    field_refs = refs[:6]
    pre1_ref, pre2_ref, gm_ref, glo_ref, ghi_ref, gs_ref, midt_ref, dect_ref = refs[6:14]
    before = refs[14] if more else None
    (
        grads_out, patches, moved, active1, active2, g_out, g_pre2, g_pre1, ends, vecs,
    ) = refs[-10:]
    lon_t, lat_t, chans = moved.shape
    hid = midt_ref.shape[0]
    first = pl.program_id(0) == 0
    assemble(patches, field_refs, moved)

    moved[...] = gm_ref[0] + gs_ref[0, :lon_t].astype(F32)
    moved[0] += glo_ref[0, 0, :lat_t].astype(F32)
    moved[lon_t - 1] += ghi_ref[0, 0, :lat_t].astype(F32)
    place = lax.broadcasted_iota(jnp.int32, (lat_t, chans), 0)
    inner = place == jnp.where(info[0] == 1, 0, lat_t - 1)
    for x in range(lon_t):
        moved[x] += jnp.where(inner, gs_ref[0, lon_t, x : x + 1].astype(F32), 0.0)

    @pl.when(first)
    def _():
        vecs[...] = jnp.zeros_like(vecs)

    step = 8
    for x in range(0, lon_t, step):
        rows = slice(x * lat_t, (x + step) * lat_t)
        a1, d1 = gelu_and_slope(pre1_ref[0, rows])
        active1[rows] = a1.astype(BF16)
        a2, d2 = gelu_and_slope(pre2_ref[0, rows])
        active2[rows] = a2.astype(BF16)
        low = moved[x : x + step].reshape(step * lat_t, chans).astype(BF16)
        g_out[rows] = low
        vecs[2:3, :chans] += jnp.sum(low.astype(F32), 0, keepdims=True)
        gp2 = (mm(low, dect_ref[...]) * d2).astype(BF16)
        g_pre2[rows] = gp2
        vecs[0:1] += jnp.sum(gp2.astype(F32), 0, keepdims=True)
        g_pre1[rows] = (mm(gp2, midt_ref[...]) * d1).astype(BF16)
    add_grads(first, grads_out, before, patches, active1, active2, g_out, g_pre2, g_pre1, ends)

    @pl.when(pl.program_id(0) == pl.num_programs(0) - 1)
    def _():
        pack_grads(grads_out, before, chans, hid, ends, vecs)


def message_spec(dims, late):
    return pl.BlockSpec((1, 1) + dims, lambda g, info: (g, late, 0, 0))


def field_specs(field, chunk, half, late, pool_state):
    state, s_ext, lo, hi, extra, masks = field
    return [
        snap_spec(state.shape[1:], chunk if pool_state else None, half),
        snap_spec(s_ext.shape[1:]),
        message_spec(lo.shape[2:], late),
        message_spec(hi.shape[2:], late),
        snap_spec(extra.shape[1:], chunk, half),
        whole(masks.shape),
    ]


def cost(micros):
    return pl.CostEstimate(flops=int(micros * 3e10), bytes_accessed=int(micros * 1e8), transcendentals=0)


def forward_call(info, chunk, half, late, field, weights, deps):
    dims = field[0].shape[1:]
    lon_t, lat_t, chans = dims
    cells = lon_t * lat_t
    hid = weights["mid"].shape[0]
    ws = [weights[k] for k in ("w1", "mid", "dec", "bias")]
    outs = [(dims, F32), (dims, BF16), ((cells, hid), F32), ((cells, hid), F32)]
    return pl.pallas_call(
        forward_kernel,
        grid_spec=grid_of(
            HALF,
            field_specs(field, chunk, half, late, True) + [whole(w.shape) for w in ws] + [any_spec()] * len(deps),
            [snap_spec(d) for d, _ in outs],
            [pltpu.VMEM((cells, 10 * chans), BF16), pltpu.VMEM(dims, F32)],
        ),
        out_shape=[shape_of((HALF,) + d, t) for d, t in outs],
        compiler_params=params(),
        cost_estimate=cost(6.5),
        name="forward",
    )(info, *field, *ws, *deps)


def back_scratch(dims, hid):
    lon_t, lat_t, chans = dims
    cells = lon_t * lat_t
    return [
        pltpu.VMEM((cells, chans), BF16),
        pltpu.VMEM((cells, hid), BF16),
        pltpu.VMEM((cells, hid), BF16),
    ], [
        pltpu.VMEM((8, hid), F32),
        pltpu.VMEM((8, hid), F32),
    ]


def turn_call(info, chunk, half, late, field, weights, targets, area, deps, before):
    dims = field[0].shape[1:]
    lon_t, lat_t, chans = dims
    cells = lon_t * lat_t
    hid = weights["mid"].shape[0]
    ws = [weights[k] for k in ("w1", "mid", "dec", "bias")]
    wt = [weights[k] for k in ("w1t", "midt", "dect")]
    grad_rows = grad_layout(chans, hid)[-1]
    more = before is not None
    last = [before] if more else []
    outs = [(dims, F32), ((lon_t + 3, lat_t, chans), BF16)]
    grads, sums = back_scratch(dims, hid)
    return pl.pallas_call(
        functools.partial(turn_kernel, more),
        grid_spec=grid_of(
            HALF,
            field_specs(field, chunk, half, late, False)
            + [whole(w.shape) for w in ws]
            + [snap_spec(dims, chunk, half), whole(area.shape)]
            + [whole(w.shape) for w in wt + last]
            + [any_spec()] * len(deps),
            [snap_spec(d) for d, _ in outs] + [whole((grad_rows, hid))],
            [
                pltpu.VMEM((cells, 10 * chans), BF16),
                pltpu.VMEM(dims, F32),
                pltpu.VMEM((cells, hid), BF16),
                pltpu.VMEM((cells, hid), BF16),
                pltpu.VMEM((cells, hid), F32),
                pltpu.VMEM((cells, hid), F32),
            ]
            + grads
            + [pltpu.VMEM((3, lon_t + 2, lat_t, chans), F32)]
            + sums
            + [pltpu.VMEM((lon_t + 8, chans), F32)],
        ),
        out_shape=[shape_of((HALF,) + d, t) for d, t in outs] + [shape_of((grad_rows, hid), F32)],
        compiler_params=params(),
        cost_estimate=cost(13.0),
        name="turn",
    )(info, *field, *ws, targets, area, *wt, *last, *deps)


def bottom_call(info, chunk, half, late, field, weights, pre, gm, glo, ghi, glate, gs, deps, before):
    dims = field[0].shape[1:]
    lon_t, lat_t, chans = dims
    cells = lon_t * lat_t
    hid = weights["mid"].shape[0]
    wt = [weights[k] for k in ("midt", "dect")]
    grad_rows = grad_layout(chans, hid)[-1]
    more = before is not None
    last = [before] if more else []
    grads, sums = back_scratch(dims, hid)
    return pl.pallas_call(
        functools.partial(bottom_kernel, more),
        grid_spec=grid_of(
            HALF,
            field_specs(field, chunk, half, late, True)
            + [snap_spec(v.shape[1:]) for v in (*pre, gm)]
            + [message_spec(glo.shape[2:], glate)] * 2
            + [snap_spec(gs.shape[1:])]
            + [whole(w.shape) for w in wt + last]
            + [any_spec()] * len(deps),
            whole((grad_rows, hid)),
            [
                pltpu.VMEM((cells, 10 * chans), BF16),
                pltpu.VMEM(dims, F32),
                pltpu.VMEM((cells, hid), BF16),
                pltpu.VMEM((cells, hid), BF16),
            ]
            + grads
            + sums,
        ),
        out_shape=shape_of((grad_rows, hid), F32),
        compiler_params=params(),
        cost_estimate=cost(8.0),
        name="bottom",
    )(info, *field, *pre, gm, glo, ghi, gs, *wt, *last, *deps)


def three_parts(vec):
    high = lax.reduce_precision(vec, 8, 7)
    rest = vec - high
    mid = lax.reduce_precision(rest, 8, 7)
    low = lax.reduce_precision(rest - mid, 8, 7)
    return jnp.stack([high, mid, low], axis=-2)


def layer_weights(enc, mid, dec, vec):
    taps, chans, hid = enc.shape
    parts = jnp.concatenate([three_parts(vec[hid : 2 * hid]), three_parts(vec[:hid])], axis=0)
    parts = jnp.pad(parts, ((0, chans - 6), (0, 0)))
    w1 = jnp.concatenate([enc.reshape(taps * chans, hid), parts], axis=0).astype(BF16)
    pad = jnp.zeros((hid - chans,), F32)
    bias = jnp.stack([vec[2 * hid : 3 * hid], jnp.concatenate([vec[3 * hid :], pad])])
    return {
        "w1": w1,
        "mid": mid.astype(BF16),
        "dec": dec.astype(BF16),
        "bias": bias,
        "w1t": jnp.transpose(enc, (2, 0, 1)).reshape(hid, taps * chans).astype(BF16),
        "midt": mid.T.astype(BF16),
        "dect": dec.T.astype(BF16),
    }


def reduce_steps(part, order):
    lon_n = lax.axis_size("lon")
    me = lax.axis_index("lon")

    def over(stride):
        return "lon", (me // stride) % 2, [(i, i ^ stride) for i in range(lon_n)]

    links = {"core": over(1), "x": over(2), "y": ("lat", lax.axis_index("lat"), [(0, 1), (1, 0)]), "z": over(8)}
    stages = [links[name] for name in order]

    def after(x, hold):
        return x if hold is None else lax.optimization_barrier((x, hold))[0]

    hold = None
    for axis, bit, perm in stages:
        half = part.shape[0] // 2
        give = lax.dynamic_slice_in_dim(part, (1 - bit) * half, half)
        mine = lax.dynamic_slice_in_dim(part, bit * half, half)
        part = after(mine, hold) + lax.ppermute(give, axis, perm)
        hold = yield part
    axis, _, perm = over(4)
    part = after(part, hold) + lax.ppermute(part, axis, perm)
    hold = yield part
    for axis, bit, perm in reversed(stages):
        got = lax.ppermute(part, axis, perm)
        part = after(part, hold)
        part = jnp.concatenate([jnp.where(bit == 0, part, got), jnp.where(bit == 0, got, part)])
        hold = yield part


def fast_grads(states, targets, sea_temp, ocean, valid, w_enc, w_mid, w_dec, biases):
    pool, lon_t, lat_t, chans = states.shape
    lon_n, lat_n = lax.axis_size("lon"), lax.axis_size("lat")
    nlon, nlat = lon_t * lon_n, lat_t * lat_n
    zonal, forward, inverse, area_all = host_tables(nlon, nlat, 88)
    hemi = lax.axis_index("lat")
    info = hemi[None].astype(jnp.int32)
    flip = np.concatenate([np.arange(lat_t, nlat), np.arange(lat_t)])
    flip2 = np.concatenate([flip, nlat + flip])
    ends = (np.arange(0, nlon, lon_t)[None, :] + np.array([[-1], [lon_t]])).reshape(-1) % nlon
    zonal_in = jnp.asarray(np.concatenate([zonal, zonal[:, ends]], axis=1))
    zonal_out = jnp.asarray(
        np.concatenate([zonal[:nlon], zonal[:nlon][ends], zonal[nlon:], zonal[nlon:][ends]], axis=0)
    )
    forward = jnp.where(hemi == 0, jnp.asarray(forward), jnp.asarray(forward[:, flip]))
    inverse = jnp.where(hemi == 0, jnp.asarray(inverse), jnp.asarray(inverse[flip2]))
    side = jnp.stack([hemi == 1, hemi == 0]).astype(F32)
    masks = jnp.broadcast_to(side[:, None], (2, chans))
    area = lax.dynamic_slice_in_dim(jnp.asarray(area_all, F32), hemi * lat_t, lat_t)
    area_wide = jnp.broadcast_to(area[:, None], (lat_t, chans))
    up = [(i, (i + 1) % lon_n) for i in range(lon_n)]
    down = [(t, s) for s, t in up]
    swap = [(0, 1), (1, 0)]
    chunks = range(pool // CHUNK)

    first_traded = lax.ppermute(pick_call(info, states, 0, 1, []), "lat", swap)
    held = lax.optimization_barrier((first_traded, w_enc, w_mid, w_dec, biases))
    _, w_enc, w_mid, w_dec, biases = held
    layers = [layer_weights(w_enc[i], w_mid[i], w_dec[i], biases[i]) for i in range(2)]

    last = [forward]

    def then(result, pick=None):
        last[:] = [result if pick is None else result[pick]]
        return result

    def over_lon(spec):
        return lax.all_to_all(spec, "lon", split_axis=0, concat_axis=0, tiled=True)

    class Chunk:
        def __init__(self, c):
            self.c = c
            self.early = 0
            self.round = 0
            self.other = first_traded
            self.field0, self.pres = [None, None], [None, None]
            self.fresh, self.low, self.s_ext, self.gm = ([None, None] for _ in range(4))

        def legendre(self):
            half = self.early
            own, late = (states, states) if self.round == 0 else (self.low[half], self.low[1 - half])
            there = self.c if self.round == 0 else None
            wide = self.round == 2
            got = legendre_call(info, own, late, there, half, self.other, forward, last, wide)
            spec, to_up, to_down, sides = then(got, 0)
            self.spec = over_lon(spec)
            self.lo, self.hi = lax.ppermute(to_up, "lon", up), lax.ppermute(to_down, "lon", down)
            self.rows_of = (own, self.other) if wide else (sides,)

        def zonal(self):
            table = zonal_in if self.round == 2 else zonal_out
            self.spec = over_lon(then(zonal_call(self.spec, table, last, self.round == 2)))

        def synthesis(self):
            got = synthesis_call(
                info, self.spec, self.lo, self.hi, inverse, self.rows_of, HALF, self.round < 2, last
            )
            own, send = then(got, 0)
            self.s_ext[self.early] = own
            self.s_ext[1 - self.early] = lax.ppermute(send, "lat", swap)

        def forward(self, late):
            half = self.early ^ late
            field = (states, self.s_ext[half], self.lo, self.hi, extra, masks)
            self.field0[half] = field
            got = forward_call(info, self.c, half, late, field, layers[0], last)
            self.fresh[half], self.low[half], *pre = then(got, 1)
            self.pres[half] = pre
            self.send(half, late)

        def turn(self, late, before):
            half = self.early ^ late
            field = (self.fresh[half], self.s_ext[half], self.lo, self.hi, extra, masks)
            got = turn_call(
                info, self.c, half, late, field, layers[1], targets, area_wide, last, before
            )
            self.gm[half], self.low[half], before = then(got, 1)
            self.send(half, late)
            return before

        def send(self, half, late):
            if not late:
                self.other = lax.ppermute(self.low[half], "lat", swap)

        def flip(self):
            self.early = 1 - self.early
            self.round += 1

        def bottom(self, late, before):
            half = self.early ^ late
            got = bottom_call(
                info, self.c, half, late, self.field0[half], layers[0], self.pres[half],
                self.gm[half], self.lo, self.hi, late, self.s_ext[half], last, before,
            )
            return then(got)

    a, b = (Chunk(c) for c in chunks)
    top, low = None, None
    a.legendre()
    b.other = lax.ppermute(then(pick_call(info, states, 1, 1, last)), "lat", swap)
    a.zonal()
    _, ocean, sea_temp, valid = lax.optimization_barrier((last[0], ocean, sea_temp, valid))
    sea = ocean.astype(F32) * sea_temp.astype(F32)
    cells = lon_t * lat_t
    lane = jnp.arange(chans)
    wide_sea = sea.reshape(pool, cells, 1).astype(BF16)
    wide_valid = valid.reshape(pool, cells, 1).astype(BF16)
    extra = jnp.where(lane < 3, wide_sea, jnp.where(lane < 6, jnp.ones((), BF16), wide_valid))
    extra = jnp.where(lane < 7, extra, jnp.zeros((), BF16))
    b.legendre()
    for one, two in ((a, b), (b, a)):
        one.synthesis()
        one.forward(0)
        two.zonal()
        one.forward(1)
        one.flip()
        one.legendre()
    for one, two in ((a, b), (b, a)):
        one.synthesis()
        top = one.turn(0, top)
        two.zonal()
        top = one.turn(1, top)
        one.flip()
        one.legendre()
    a.synthesis()
    top, _ = lax.optimization_barrier((top, last[0]))
    upper = reduce_steps(top, ("core", "y", "x", "z"))
    low = a.bottom(0, low)
    b.zonal()
    last.append(next(upper))
    low = a.bottom(1, low)
    last.append(next(upper))
    b.synthesis()
    last.append(next(upper))
    low = b.bottom(0, low)
    last.append(next(upper))
    low = b.bottom(1, low)
    lower = reduce_steps(low, ("core", "x", "y", "z"))
    *_, high = upper
    *_, low = lower
    return low, high


def update_kernel(rate, taps_each, info, g0_ref, g1_ref, m0_ref, m1_ref, v0_ref, v1_ref, *refs):
    ins, outs = refs[:12], refs[12:]
    layer, part = pl.program_id(0), pl.program_id(1)
    chans, hid = ins[0].shape[2:]
    scale = 1.0 / v1_ref[4:5, 0:1]

    def apply(group, at, grad):
        w_ref, m_ref, a_ref = (ins[4 * i + group] for i in range(3))
        new_ref, mom_ref, avg_ref, copy_ref = (outs[4 * i + group] for i in range(4))
        scaled = grad * scale
        mom = MOMENTUM * m_ref[at] + scaled
        fresh = w_ref[at] - rate * (scaled + MOMENTUM * mom)
        new_ref[at] = fresh
        mom_ref[at] = mom
        avg_ref[at] = AVERAGE * a_ref[at] + (1.0 - AVERAGE) * fresh
        copy_ref[at] = fresh.astype(BF16)

    def layer_step(g_ref, m_ref):
        for tap in range(taps_each):
            apply(0, (0, tap), g_ref[tap * chans : (tap + 1) * chans])

        @pl.when(part == 0)
        def _():
            apply(1, (0,), m_ref[:hid])
            apply(2, (0,), m_ref[hid:].T)

    pl.when(layer == 0)(lambda: layer_step(g0_ref, m0_ref))
    pl.when(layer == 1)(lambda: layer_step(g1_ref, m1_ref))

    @pl.when((layer == 0) & (part == 0))
    def _():
        for i, v_ref in enumerate((v0_ref, v1_ref)):
            for r in range(4):
                wide = hid if r < 3 else chans
                at = (slice(i, i + 1), slice(r * hid, r * hid + wide))
                apply(3, at, v_ref[r : r + 1, :wide])


TAPS_EACH = 9


def update_call(rate, sums, arrays):
    w_enc, w_mid, w_dec, biases = arrays[:4]
    layers, taps, chans, hid = w_enc.shape
    one, _, three, _ = grad_layout(chans, hid)
    steps = taps // TAPS_EACH
    rows = TAPS_EACH * chans
    enc = pl.BlockSpec((1, TAPS_EACH, chans, hid), lambda i, p, info: (i, p, 0, 0))
    mid = pl.BlockSpec((1, hid, hid), lambda i, p, info: (i, 0, 0))
    dec = pl.BlockSpec((1, hid, chans), lambda i, p, info: (i, 0, 0))
    bias = whole(biases.shape)
    specs = [enc, mid, dec, bias]
    shapes = [w_enc.shape, w_mid.shape, w_dec.shape, biases.shape]
    grads = [
        pl.BlockSpec((rows, hid), lambda i, p, info: (jnp.where(i == 0, p, steps - 1), 0)),
        pl.BlockSpec((rows, hid), lambda i, p, info: (jnp.where(i == 0, 0, p), 0)),
        pl.BlockSpec((three - one, hid), lambda i, p, info: (one // (three - one), 0)),
        pl.BlockSpec((three - one, hid), lambda i, p, info: (one // (three - one), 0)),
        pl.BlockSpec((8, hid), lambda i, p, info: (three // 8, 0)),
        pl.BlockSpec((8, hid), lambda i, p, info: (three // 8, 0)),
    ]
    got = pl.pallas_call(
        functools.partial(update_kernel, rate, TAPS_EACH),
        grid_spec=pltpu.PrefetchScalarGridSpec(
            num_scalar_prefetch=1,
            grid=(layers, steps),
            in_specs=grads + specs * 3,
            out_specs=specs * 4,
        ),
        out_shape=[shape_of(s, F32) for s in shapes * 3] + [shape_of(s, BF16) for s in shapes],
        compiler_params=params(),
        cost_estimate=cost(8.0),
        name="update",
    )(jnp.zeros((1,), jnp.int32), sums[0], sums[1], sums[0], sums[1], sums[0], sums[1], *arrays)
    vecs = sums[1][three : three + 8]
    return (jnp.sum(vecs[3, chans:]), vecs[4, 0], *got)


def fits(states, w_mid, lon_n, lat_n):
    pool, lon_t, lat_t, chans = states.shape
    return (
        lat_n == 2
        and lon_n == 16
        and lon_t == 16
        and lat_t == 64
        and pool == 2 * CHUNK
        and chans == 128
        and w_mid.shape[1] == 2 * chans
        and w_mid.shape[0] == 2
    )


def with_halo(block, sides, width, periodic):
    for axis, dim in sides:
        count = lax.axis_size(axis)
        forward = [(i, i + 1) for i in range(count - 1)]
        if periodic:
            forward.append((count - 1, 0))
        backward = [(target, source) for source, target in forward]
        low = lax.ppermute(
            lax.slice_in_dim(block, block.shape[dim] - width, None, axis=dim), axis, forward
        )
        high = lax.ppermute(lax.slice_in_dim(block, 0, width, axis=dim), axis, backward)
        block = jnp.concatenate([low, block, high], axis=dim)
    return block


def tables(nlon, nlat, groups):
    coeffs = jnp.arange(2 * MW)
    wave = jnp.where(coeffs < MW, coeffs, coeffs - MW + 1).astype(jnp.float32)
    places = jnp.arange(nlon).astype(jnp.float32)
    angle = 2.0 * math.pi * wave[:, None] * places[None, :] / nlon
    fourier = jnp.where((coeffs < MW)[:, None], jnp.cos(angle), jnp.sin(angle)) * math.sqrt(
        2.0 / nlon
    )
    phase = ((jnp.arange(nlat).astype(jnp.float32) + 0.5) / nlat - 0.5) * math.pi
    sine = jnp.sin(phase)
    quad = jnp.cos(phase) * math.pi / nlat
    polys = [jnp.ones_like(sine), sine]
    for degree in range(1, NDEG - 1):
        polys.append(((2 * degree + 1) * sine * polys[-1] - degree * polys[-2]) / (degree + 1))
    stacked = jnp.stack(polys[:NDEG])
    degrees = jnp.arange(NDEG).astype(jnp.float32)
    legendre = jnp.sqrt((2 * degrees + 1) / 2)[:, None] * jnp.sqrt(quad)[None, :] * stacked
    damping = 1.5 * (1.0 - 2.0 * degrees * (degrees + 1) / (NDEG * (NDEG + 1)))
    filters = damping[None, :] * (1.0 - 0.5 * wave / MW)[:, None]
    kept = 2 * MW
    slots = (kept + groups - 1) // groups * groups
    fourier = jnp.pad(fourier, ((0, slots - kept), (0, 0)))
    filters = jnp.pad(filters, ((0, slots - kept), (0, 0)))
    return (fourier, legendre, filters)


def spectral(values, tabs):
    fourier, legendre, filters = tabs
    cycles = lax.all_to_all(
        values.astype(jnp.bfloat16), "lon", split_axis=3, concat_axis=1, tiled=True
    ).astype(values.dtype)
    coeff = jnp.einsum("kx,sxjc->skjc", fourier, cycles, precision=HIGH)
    block = fourier.shape[0] // lax.axis_size("lat")
    where = lax.axis_index("lat")
    block_filter = lax.dynamic_slice_in_dim(filters, where * block, block, 0)
    columns = lax.all_to_all(
        coeff.astype(jnp.bfloat16), "lat", split_axis=1, concat_axis=2, tiled=True
    ).astype(coeff.dtype)
    spec = (
        jnp.einsum("nj,skjc->sknc", legendre, columns, precision=HIGH)
        * block_filter[None, :, :, None]
    )
    back = jnp.einsum("nj,sknc->skjc", legendre, spec, precision=HIGH)
    coeff_back = lax.all_to_all(
        back.astype(jnp.bfloat16), "lat", split_axis=2, concat_axis=1, tiled=True
    ).astype(back.dtype)
    grid = jnp.einsum("kx,skjc->sxjc", fourier, coeff_back, precision=HIGH)
    return lax.all_to_all(
        grid.astype(jnp.bfloat16), "lon", split_axis=1, concat_axis=3, tiled=True
    ).astype(grid.dtype)


def extend(field):
    wider = with_halo(field, (("lon", 1),), 1, True)
    return with_halo(wider, (("lat", 2),), 1, False)


def neighbours(padded, flipped, lon_t, lat_t):
    parts = []
    for row_off in range(3):
        for col_off in range(3):
            first = 2 - row_off if flipped else row_off
            second = 2 - col_off if flipped else col_off
            parts.append(padded[:, first : first + lon_t, second : second + lat_t])
    stacked = jnp.stack(parts, axis=3)
    return stacked.reshape(-1, 9 * padded.shape[-1])


def gelu_fn(value):
    return jax.nn.gelu(value, approximate=True)


def gelu_back(value, grad):
    return jax.vjp(gelu_fn, value)[1](grad)[0]


def layer_forward(state, sea, enc, mid, dec, vec, tabs):
    hid = mid.shape[0]
    lon_t, lat_t = (state.shape[1], state.shape[2])
    moved = state + spectral(state, tabs)
    patches = neighbours(extend(moved.astype(jnp.bfloat16)), False, lon_t, lat_t)
    pre1 = jnp.dot(patches, enc, preferred_element_type=jnp.float32)
    pre1 = pre1 + sea.reshape(-1, 1) * vec[hid : 2 * hid] + vec[:hid]
    active1 = gelu_fn(pre1).astype(jnp.bfloat16)
    pre2 = jnp.dot(active1, mid, preferred_element_type=jnp.float32) + vec[2 * hid : 3 * hid]
    active2 = gelu_fn(pre2).astype(jnp.bfloat16)
    output = jnp.dot(active2, dec, preferred_element_type=jnp.float32) + vec[3 * hid :]
    return (moved + output.reshape(state.shape), (patches, pre1, active1, pre2, active2))


def layer_backward(grad_state, sea, enc, mid, dec, saved, tabs):
    patches, pre1, active1, pre2, active2 = saved
    hid = mid.shape[0]
    shape = grad_state.shape
    chans = shape[-1]
    g_out = grad_state.reshape(-1, chans).astype(jnp.bfloat16)
    g_dec = jnp.einsum("rh,rc->hc", active2, g_out, preferred_element_type=jnp.float32)
    g_act2 = jnp.einsum("rc,hc->rh", g_out, dec, preferred_element_type=jnp.float32)
    g_pre2 = gelu_back(pre2, g_act2).astype(jnp.bfloat16)
    g_mid = jnp.einsum("rh,rg->hg", active1, g_pre2, preferred_element_type=jnp.float32)
    g_act1 = jnp.einsum("rg,hg->rh", g_pre2, mid, preferred_element_type=jnp.float32)
    g_pre1 = gelu_back(pre1, g_act1).astype(jnp.bfloat16)
    g_enc = jnp.einsum("rk,rh->kh", patches, g_pre1, preferred_element_type=jnp.float32)
    wide1 = g_pre1.astype(jnp.float32)
    g_vec = jnp.concatenate(
        [
            jnp.sum(wide1, 0),
            jnp.sum(sea.reshape(-1, 1) * wide1, 0),
            jnp.sum(g_pre2.astype(jnp.float32), 0),
            jnp.sum(g_out.astype(jnp.float32), 0),
        ]
    )
    spread = extend(g_pre1.reshape(shape[0], shape[1], shape[2], hid))
    gathered = neighbours(spread, True, shape[1], shape[2]).reshape(-1, 9, hid)
    g_input = jnp.einsum(
        "rkh,kch->rc", gathered, enc.reshape(9, chans, hid), preferred_element_type=jnp.float32
    )
    grad_moved = grad_state + g_input.reshape(shape)
    return (grad_moved + spectral(grad_moved, tabs), (g_enc, g_mid, g_dec, g_vec))


def general_grads(states, targets, sea_temp, ocean, valid, order, w_enc, w_mid, w_dec, biases):
    pool, lon_t, lat_t, chans = states.shape
    layers, hid = (w_mid.shape[0], w_mid.shape[1])
    nlon = lon_t * lax.axis_size("lon")
    nlat = lat_t * lax.axis_size("lat")
    tabs = tables(nlon, nlat, lax.axis_size("lat"))
    lat_glob = (lax.axis_index("lat") * lat_t + jnp.arange(lat_t)).astype(jnp.float32)
    area = jnp.cos(((lat_glob + 0.5) / nlat - 0.5) * math.pi)
    enc_low = w_enc.astype(jnp.bfloat16).reshape(layers, 9 * chans, hid)
    mid_low = w_mid.astype(jnp.bfloat16)
    dec_low = w_dec.astype(jnp.bfloat16)
    snaps = pool // MB
    sums = [
        jnp.zeros((layers, 9 * chans, hid), jnp.float32),
        jnp.zeros_like(w_mid),
        jnp.zeros_like(w_dec),
        jnp.zeros_like(biases),
    ]
    loss = jnp.zeros((), jnp.float32)
    total = jnp.zeros((), jnp.float32)
    for batch_id in range(MB):
        picks = lax.dynamic_slice_in_dim(order, batch_id * snaps, snaps)
        state = jnp.take(states, picks, axis=0).astype(jnp.float32)
        target = jnp.take(targets, picks, axis=0).astype(jnp.float32)
        sea = jnp.take(ocean, picks, axis=0).astype(jnp.float32) * jnp.take(
            sea_temp, picks, axis=0
        ).astype(jnp.float32)
        weight = jnp.take(valid, picks, axis=0).astype(jnp.float32) * area[None, None, :]
        kept = []
        for layer_id in range(layers):
            state, saved = layer_forward(
                state,
                sea,
                enc_low[layer_id],
                mid_low[layer_id],
                dec_low[layer_id],
                biases[layer_id],
                tabs,
            )
            kept.append(saved)
        diff = state - target
        loss = loss + jnp.sum(weight[..., None] * diff * diff)
        total = total + jnp.sum(weight)
        grad_state = 2.0 * weight[..., None] * diff
        for layer_id in reversed(range(layers)):
            grad_state, found = layer_backward(
                grad_state,
                sea,
                enc_low[layer_id],
                mid_low[layer_id],
                dec_low[layer_id],
                kept[layer_id],
                tabs,
            )
            sums = [acc.at[layer_id].add(part) for acc, part in zip(sums, found)]
    g_enc, g_mid, g_dec, g_vec, loss, total = lax.psum(
        (sums[0], sums[1], sums[2], sums[3], loss, total), ("lon", "lat")
    )
    return g_enc.reshape(w_enc.shape), g_mid, g_dec, g_vec, loss, total


def body(
    states,
    targets,
    sea_temp,
    ocean,
    valid,
    order,
    w_enc,
    w_mid,
    w_dec,
    biases,
    mom_enc,
    mom_mid,
    mom_dec,
    mom_bias,
    avg_enc,
    avg_mid,
    avg_dec,
    avg_bias,
):
    pool, lon_t, lat_t = states.shape[:3]
    lon_n, lat_n = lax.axis_size("lon"), lax.axis_size("lat")
    rate = RATE_BASE * math.sqrt(pool * lon_t * lon_n * lat_t * lat_n)
    if fits(states, w_mid, lon_n, lat_n):
        sums = fast_grads(states, targets, sea_temp, ocean, valid, w_enc, w_mid, w_dec, biases)
        arrays = (w_enc, w_mid, w_dec, biases, mom_enc, mom_mid, mom_dec, mom_bias)
        arrays += (avg_enc, avg_mid, avg_dec, avg_bias)
        return update_call(rate, sums, arrays)
    found = general_grads(
        states, targets, sea_temp, ocean, valid, order, w_enc, w_mid, w_dec, biases
    )
    loss, total = found[4:]
    grads = (found[0].reshape(w_enc.shape),) + found[1:4]
    news, moms, avgs, copies = ([], [], [], [])
    for weight_now, grad, mom, avg in zip(
        (w_enc, w_mid, w_dec, biases),
        grads,
        (mom_enc, mom_mid, mom_dec, mom_bias),
        (avg_enc, avg_mid, avg_dec, avg_bias),
    ):
        scaled = grad / total
        mom_new = MOMENTUM * mom + scaled
        fresh = weight_now - rate * (scaled + MOMENTUM * mom_new)
        news.append(fresh)
        moms.append(mom_new)
        avgs.append(AVERAGE * avg + (1.0 - AVERAGE) * fresh)
        copies.append(fresh.astype(jnp.bfloat16))
    return (
        loss,
        total,
        news[0],
        news[1],
        news[2],
        news[3],
        moms[0],
        moms[1],
        moms[2],
        moms[3],
        avgs[0],
        avgs[1],
        avgs[2],
        avgs[3],
        copies[0],
        copies[1],
        copies[2],
        copies[3],
    )


def solution(mesh):
    placed = (
        P(None, "lon", "lat", None),
        P(None, "lon", "lat", None),
        P(None, "lon", "lat"),
        P(None, "lon", "lat"),
        P(None, "lon", "lat"),
        P(),
        P(),
        P(),
        P(),
        P(),
        P(),
        P(),
        P(),
        P(),
        P(),
        P(),
        P(),
        P(),
    )
    return jax.shard_map(
        body,
        mesh=mesh,
        in_specs=placed,
        out_specs=(
            P(),
            P(),
            P(),
            P(),
            P(),
            P(),
            P(),
            P(),
            P(),
            P(),
            P(),
            P(),
            P(),
            P(),
            P(),
            P(),
            P(),
            P(),
        ),
        check_vma=False,
    )
```

```python
import functools
import math

import jax
import jax.numpy as jnp
import numpy as np
from jax import lax
from jax.experimental import pallas as pl
from jax.experimental.pallas import tpu as pltpu
from jax.sharding import PartitionSpec as P

MW = 86
NDEG = 86
MB = 4


HIGH = lax.Precision.HIGHEST
MOMENTUM = 0.9
AVERAGE = 0.99
RATE_BASE = 0.0006

F32 = jnp.float32
BF16 = jnp.bfloat16
CHUNK = 4
VMEM = 56 * 1024 * 1024
GELU_A = math.sqrt(2.0 / math.pi)
GELU_B = 0.044715


def split_table(table):
    table = np.asarray(table, np.float32)
    high = table.astype(BF16)
    low = (table - high.astype(np.float32)).astype(BF16)
    return np.concatenate([high, low], axis=0)


def host_tables(nlon, nlat, deg):
    kept = np.arange(2 * MW)
    wave = np.where(kept < MW, kept, kept - MW + 1).astype(np.float64)
    angle = 2.0 * np.pi * wave[:, None] * np.arange(nlon)[None, :] / nlon
    fourier = np.where((kept < MW)[:, None], np.cos(angle), np.sin(angle)) * np.sqrt(2.0 / nlon)
    zonal = (fourier * (1.0 - 0.5 * wave / MW)[:, None]).T @ fourier
    phase = ((np.arange(nlat) + 0.5) / nlat - 0.5) * np.pi
    sine, area = np.sin(phase), np.cos(phase)
    polys = [np.ones_like(sine), sine]
    for n in range(1, NDEG - 1):
        polys.append(((2 * n + 1) * sine * polys[-1] - n * polys[-2]) / (n + 1))
    degrees = np.arange(NDEG)
    legendre = np.sqrt((2 * degrees + 1) / 2)[:, None] * np.sqrt(area * np.pi / nlat)[None, :]
    legendre = legendre * np.stack(polys)
    damping = 1.5 * (1.0 - 2.0 * degrees * (degrees + 1) / (NDEG * (NDEG + 1)))
    forward = np.zeros((deg, nlat))
    forward[:NDEG] = legendre
    inverse = np.zeros((nlat, -(-deg // 32) * 32))
    inverse[:, :NDEG] = (legendre * damping[:, None]).T
    return split_table(zonal), split_table(forward), split_table(inverse), area


def mm(a, b):
    return jnp.dot(a, b, preferred_element_type=F32)


def mm_rows(a, b):
    return lax.dot_general(a, b, (((0,), (0,)), ((), ())), preferred_element_type=F32)


def whole(shape):
    return pl.BlockSpec(shape, lambda *_: (0,) * len(shape))


def params():
    return pltpu.CompilerParams(vmem_limit_bytes=VMEM)


HALF = CHUNK // 2


def any_spec():
    return pl.BlockSpec(memory_space=pl.ANY)


def shape_of(dims, dtype):
    return jax.ShapeDtypeStruct(dims, dtype)


def grid_of(count, in_specs, out_specs, scratch):
    return pltpu.PrefetchScalarGridSpec(
        num_scalar_prefetch=1,
        grid=(count,),
        in_specs=in_specs,
        out_specs=out_specs,
        scratch_shapes=scratch,
    )


def first_of(chunk, half, info):
    if chunk is None:
        return 0
    return chunk * CHUNK + HALF * (info[0] if half == 0 else 1 - info[0])


def snap_spec(dims, chunk=None, half=0):
    return pl.BlockSpec(
        (1,) + dims, lambda g, info: (first_of(chunk, half, info) + g,) + (0,) * len(dims)
    )


def pick_kernel(info, x_ref, *refs):
    refs[-1][...] = x_ref[...]


def pick_call(info, fields, chunk, half, deps):
    dims = fields.shape[1:]
    return pl.pallas_call(
        pick_kernel,
        grid_spec=grid_of(
            HALF, [snap_spec(dims, chunk, half)] + [any_spec()] * len(deps), snap_spec(dims), []
        ),
        out_shape=shape_of((HALF,) + dims, fields.dtype),
        compiler_params=params(),
        cost_estimate=cost(1.0),
        name="pick",
    )(info, fields, *deps)


def legendre_kernel(
    wide, info, own_ref, other_ref, first_ref, last_ref, l_ref, *refs
):
    o_ref, up_ref, down_ref, rows_ref, tmp = refs[-5:]
    parts, rows, lon_t, chans = o_ref.shape
    lat_t = own_ref.shape[2]
    deg = l_ref.shape[0] // 2
    count = lon_t + 2 if wide else lon_t
    each = deg // parts
    place = lax.broadcasted_iota(jnp.int32, (lat_t, chans), 0)
    south = info[0] == 1
    inner = place == jnp.where(south, 0, lat_t - 1)
    other_inner = place == jnp.where(south, lat_t - 1, 0)

    def column(x):
        own, other = own_ref[0, x], other_ref[0, x]
        if wide:
            to_own = other_ref[0, count, x : x + 1].astype(F32)
            to_other = own_ref[0, count, x : x + 1].astype(F32)
            own = (own.astype(F32) + jnp.where(inner, to_own, 0.0)).astype(BF16)
            other = (other.astype(F32) + jnp.where(other_inner, to_other, 0.0)).astype(BF16)
        else:
            own_f, other_f = own.astype(F32), other.astype(F32)
            ends = [(own_f[:1], own_f[lat_t - 1 :]), (other_f[lat_t - 1 :], other_f[:1])]
            for i, (if_south, if_north) in enumerate(ends):
                rows_ref[0, i, x : x + 1] = jnp.where(south, if_south, if_north)
        return jnp.concatenate([own, other], axis=0)

    for base in range(0, count, 4):
        span = range(base, min(base + 4, count))
        r = mm(l_ref[...], jnp.concatenate([column(x) for x in span], axis=1))
        r = r[:deg] + r[deg:]
        for x in span:
            tmp[:deg, x, :] = r[:, (x - base) * chans : (x - base + 1) * chans]
    o_ref[:, :each] = tmp[:deg, :lon_t, :].astype(BF16).reshape(parts, each, lon_t, chans)
    if wide:
        rest = jnp.zeros((lon_t - each, chans), F32)
        for p in range(parts):
            for side in range(2):
                edge = tmp[p * each : (p + 1) * each, lon_t + side, :]
                o_ref[p, each + side] = jnp.concatenate([edge, rest], axis=0).astype(BF16)
        rows_ref[...] = jnp.zeros_like(rows_ref)
    for ref, late_ref, x in ((down_ref, first_ref, 0), (up_ref, last_ref, lon_t - 1)):
        if wide:
            at = lon_t if x == 0 else lon_t + 1
            corner, far = other_ref[0, count, at : at + 1], own_ref[0, count, at : at + 1]
            pieces = [jnp.broadcast_to(v.astype(F32), (8, chans)) for v in (corner, far)]
        else:
            at = x
            pieces = [jnp.broadcast_to(rows_ref[0, 1, x : x + 1], (16, chans))]
        ref[0, 0, :lat_t] = own_ref[0, at]
        ref[0, 0, lat_t:] = jnp.concatenate(pieces, axis=0).astype(BF16)
        ref[0, 1, :lat_t] = late_ref[0, 0]
        ref[0, 1, lat_t:] = jnp.zeros((16, chans), BF16)


def legendre_call(info, own, late, chunk, half, other, table, deps, wide):
    snaps, slabs, lat_t, chans = other.shape
    deg = table.shape[0] // 2
    parts = 8
    lon_t = slabs - 3 if wide else slabs
    rows = deg // parts + (2 if wide else 0)
    message = (2, lat_t + 16, chans)
    sides = (2, lon_t, chans)

    def late_column(x):
        return pl.BlockSpec(
            (1, 1, lat_t, chans), lambda g, info: (first_of(chunk, 1 - half, info) + g, x, 0, 0)
        )

    columns = (lon_t, lon_t + 1) if wide else (0, lon_t - 1)
    return pl.pallas_call(
        functools.partial(legendre_kernel, wide),
        grid_spec=grid_of(
            snaps,
            [
                snap_spec(own.shape[1:], chunk, half),
                snap_spec(other.shape[1:]),
                late_column(columns[0]),
                late_column(columns[1]),
                whole(table.shape),
            ]
            + [any_spec()] * len(deps),
            [
                pl.BlockSpec((parts, rows, lon_t, chans), lambda s, info: (s, 0, 0, 0)),
                snap_spec(message),
                snap_spec(message),
                snap_spec(sides),
            ],
            [pltpu.VMEM((-(-deg // 32) * 32, lon_t + 8 if wide else lon_t, chans), F32)],
        ),
        out_shape=[
            shape_of((snaps * parts, rows, lon_t, chans), BF16),
            shape_of((snaps,) + message, BF16),
            shape_of((snaps,) + message, BF16),
            shape_of((snaps,) + sides, F32),
        ],
        compiler_params=params(),
        cost_estimate=cost(3.4),
        name="legendre",
    )(info, own, other, late, late, table, *deps)


def zonal_kernel(wide_in, x_ref, a_ref, *refs):
    o_ref, tmp = refs[-2:]
    groups, _, lon_t, chans = x_ref.shape
    nlon = groups * lon_t
    rows = min(x_ref.shape[1], o_ref.shape[1])
    if wide_in:
        for side in range(2):
            tmp[side * groups : (side + 1) * groups] = x_ref[:, rows + side].astype(F32)
    else:
        tmp[...] = jnp.zeros_like(tmp)
    for base in range(0, rows, 4):
        span = range(base, min(base + 4, rows))
        fields = jnp.concatenate([x_ref[:, n].reshape(nlon, chans) for n in span], axis=1)
        if wide_in:
            edges = jnp.concatenate([tmp[:, n, :] for n in span], axis=1).astype(BF16)
            r = mm(a_ref[:, :nlon], fields) + mm(a_ref[:, nlon:], edges)
            r = r[:nlon] + r[nlon:]
        else:
            r = mm(a_ref[...], fields)
            size = r.shape[0] // 2
            r = r[:size] + r[size:]
        low = r[:nlon].astype(BF16)
        for n in span:
            lanes = slice((n - base) * chans, (n - base + 1) * chans)
            o_ref[:, n] = low[:, lanes].reshape(groups, lon_t, chans)
            if not wide_in:
                tmp[:, n, :] = r[nlon:, lanes]
    if not wide_in:
        for side in range(2):
            o_ref[:, rows + side] = tmp[side * groups : (side + 1) * groups].astype(BF16)


def zonal_call(fields, table, deps, wide_in):
    groups, rows, lon_t, chans = fields.shape
    out = (groups, rows - 2 if wide_in else rows + 2, lon_t, chans)
    return pl.pallas_call(
        functools.partial(zonal_kernel, wide_in),
        in_specs=[pl.BlockSpec(memory_space=pltpu.VMEM)] * 2 + [any_spec()] * len(deps),
        out_specs=pl.BlockSpec(memory_space=pltpu.VMEM),
        out_shape=shape_of(out, BF16),
        scratch_shapes=[pltpu.VMEM((2 * groups, lon_t, chans), F32)],
        compiler_params=params(),
        cost_estimate=cost(2.8),
        name="zonal",
    )(fields, table, *deps)


def synthesis_kernel(wide, info, x_ref, lo_ref, hi_ref, l_ref, *refs):
    rows_refs = refs[: 1 if wide else 2]
    own_ref, send_ref, tmp, side = refs[-4:]
    parts, rows, lon_t, chans = x_ref.shape
    each = rows - 2 if wide else rows
    deg = parts * each
    count = lon_t + 2 if wide else lon_t
    nlat = l_ref.shape[0] // 2
    half = nlat // 2
    south = info[0] == 1
    tmp[:deg, :lon_t, :] = x_ref[:, :each].reshape(deg, lon_t, chans).astype(F32)
    if wide:
        for p in range(parts):
            for e in range(2):
                tmp[p * each : (p + 1) * each, lon_t + e, :] = x_ref[p, each + e, :each].astype(F32)
    tmp[deg:] = jnp.zeros((tmp.shape[0] - deg,) + tmp.shape[1:], F32)
    side[...] = jnp.zeros_like(side)
    low, high = lo_ref[0, 0].astype(F32), hi_ref[0, 0].astype(F32)
    if wide:
        sides_ref = rows_refs[0]
        for i in range(2):
            side[i, :lon_t] = sides_ref[0, 1 - i]
        for at, edge in ((lon_t, low), (lon_t + 1, high)):
            side[0, at : at + 1] = edge[half : half + 1]
            side[1, at : at + 1] = jnp.where(south, edge[:1], edge[half - 1 : half])
    else:
        for i, ref in enumerate(rows_refs[::-1]):
            side[i, :lon_t] = ref[0, 0, :lon_t].astype(F32)
            for at, edge in ((0, low), (lon_t - 1, high)):
                side[i, at : at + 1] += edge[half + 8 * i : half + 8 * i + 1]
    for base in range(0, count, 4):
        span = range(base, min(base + 4, count))
        cols = jnp.concatenate([tmp[:, x, :] for x in span], axis=1).astype(BF16)
        r = mm(l_ref[...], cols)
        r = r[:nlat] + r[nlat:]
        for x in span:
            one = r[:, (x - base) * chans : (x - base + 1) * chans]
            own_ref[0, x] = one[:half].astype(BF16)
            send_ref[0, x] = one[half:].astype(BF16)
            if wide:
                side[0, x : x + 1] += jnp.where(south, one[2 * half - 1 :], one[half : half + 1])
                side[1, x : x + 1] += jnp.where(south, one[:1], one[half - 1 : half])
    rest = jnp.zeros((half - side.shape[1], chans), F32)
    for i, ref in enumerate((own_ref, send_ref)):
        ref[0, count] = jnp.concatenate([side[i], rest], axis=0).astype(BF16)


def synthesis_call(info, coeffs, lo, hi, table, rows_of, snaps, wide, deps):
    total, rows, lon_t, chans = coeffs.shape
    parts = total // snaps
    nlat = table.shape[0] // 2
    slabs = lon_t + 3 if wide else lon_t + 1
    out = snap_spec((slabs, nlat // 2, chans))
    message = pl.BlockSpec((1, 1) + lo.shape[2:], lambda s, info: (s, 0, 0, 0))
    if wide:
        row_specs = [snap_spec(r.shape[1:]) for r in rows_of]
    else:
        last = pl.BlockSpec((1, 1) + rows_of[0].shape[2:], lambda s, info: (s, lon_t + 2, 0, 0))
        row_specs = [last for _ in rows_of]
    return pl.pallas_call(
        functools.partial(synthesis_kernel, wide),
        grid_spec=grid_of(
            snaps,
            [
                pl.BlockSpec((parts, rows, lon_t, chans), lambda s, info: (s, 0, 0, 0)),
                message,
                message,
                whole(table.shape),
            ]
            + row_specs
            + [any_spec()] * len(deps),
            [out, out],
            [
                pltpu.VMEM((table.shape[1], lon_t + 8 if wide else lon_t, chans), F32),
                pltpu.VMEM((2, lon_t + 8, chans), F32),
            ],
        ),
        out_shape=[shape_of((snaps, slabs, nlat // 2, chans), BF16)] * 2,
        compiler_params=params(),
        cost_estimate=cost(3.6),
        name="synthesis",
    )(info, coeffs, lo, hi, table, *rows_of, *deps)


def gelu_of(x):
    t = jnp.tanh(x * (GELU_A + (GELU_A * GELU_B) * (x * x)))
    return 0.5 * x * (1.0 + t)


def gelu_and_slope(x):
    sq = x * x
    t = jnp.tanh(x * (GELU_A + (GELU_A * GELU_B) * sq))
    cdf = 0.5 + 0.5 * t
    slope = cdf + (0.5 * x) * (1.0 - t * t) * (GELU_A + (3.0 * GELU_A * GELU_B) * sq)
    return x * cdf, slope


def fill_patches(patches, slabs, ends, masks):
    lat_t, chans = slabs[0].shape
    lon_t = len(slabs) - 2
    place = lax.broadcasted_iota(jnp.int32, (lat_t, chans), 0)
    for i in range(lon_t + 2):
        low_row, high_row = ends[i] * masks[0:1], ends[i] * masks[1:2]
        down = jnp.where(place == 0, low_row, pltpu.roll(slabs[i], 1, 0)).astype(BF16)
        up = jnp.where(place == lat_t - 1, high_row, pltpu.roll(slabs[i], lat_t - 1, 0)).astype(BF16)
        mid = slabs[i].astype(BF16)
        for a in range(3):
            x = i - a
            if 0 <= x < lon_t:
                for b, piece in enumerate((down, mid, up)):
                    k = 3 * a + b
                    patches[x * lat_t : (x + 1) * lat_t, k * chans : (k + 1) * chans] = piece


def assemble(patches, field_refs, moved):
    state_ref, s_ref, lo_ref, hi_ref, extra_ref, masks_ref = field_refs
    lon_t, lat_t, chans = moved.shape
    moved[...] = state_ref[0].astype(F32) + s_ref[0, :lon_t].astype(F32)
    rows = s_ref[0, lon_t + 2].astype(F32)
    slabs = [lo_ref[0, 0, :lat_t].astype(F32) + s_ref[0, lon_t].astype(F32)]
    slabs += [moved[i] for i in range(lon_t)]
    slabs += [hi_ref[0, 0, :lat_t].astype(F32) + s_ref[0, lon_t + 1].astype(F32)]
    ends = [rows[i : i + 1] for i in [lon_t] + list(range(lon_t)) + [lon_t + 1]]
    fill_patches(patches, slabs, ends, masks_ref[...])
    patches[:, 9 * chans :] = extra_ref[0]


def forward_kernel(info, *refs):
    field_refs, (w1_ref, mid_ref, dec_ref, bias_ref) = refs[:6], refs[6:10]
    state_out, low_out, pre1_out, pre2_out, patches, moved = refs[-6:]
    lon_t, lat_t, chans = moved.shape
    hid = mid_ref.shape[0]
    assemble(patches, field_refs, moved)
    pre1 = mm(patches[...], w1_ref[...])
    pre1_out[0] = pre1
    active1 = gelu_of(pre1).astype(BF16)
    pre2 = mm(active1, mid_ref[...]) + bias_ref[0:1, :hid]
    pre2_out[0] = pre2
    active2 = gelu_of(pre2).astype(BF16)
    out = mm(active2, dec_ref[...]) + bias_ref[1:2, :chans]
    state_out[0] = moved[...] + out.reshape(lon_t, lat_t, chans)
    low_out[0] = state_out[0].astype(BF16)


GRAD_PAD = 128


def grad_layout(chans, hid):
    one, two, three = 9 * chans, 9 * chans + hid, 9 * chans + hid + chans
    return (one, two, three, -(-(three + 8) // GRAD_PAD) * GRAD_PAD)


def add_grads(first, out, before, patches, active1, active2, g_out, g_pre2, g_pre1, ends):
    chans, hid = g_out.shape[1], g_pre1.shape[1]
    one, two, three, _ = grad_layout(chans, hid)
    enc = mm_rows(patches[...], g_pre1[...])
    pieces = [
        (0, one, enc[:one]),
        (one, two, mm_rows(active1[...], g_pre2[...])),
        (two, three, mm_rows(g_out[...], active2[...])),
    ]

    @pl.when(first)
    def _():
        ends[...] = enc[one : one + 8]
        for start, stop, piece in pieces:
            out[start:stop] = piece if before is None else before[start:stop] + piece

    @pl.when(jnp.logical_not(first))
    def _():
        ends[...] += enc[one : one + 8]
        for start, stop, piece in pieces:
            out[start:stop] += piece


def pack_grads(out, before, chans, hid, ends, vecs):
    _, _, three, rows = grad_layout(chans, hid)
    tail = jnp.concatenate([vecs[2:3, :chans], vecs[1:2, :chans]], axis=1)
    out[three:] = jnp.zeros((rows - three, hid), F32)
    for row, piece in enumerate((ends[3:4], ends[0:1], vecs[0:1], tail, vecs[3:4])):
        at = slice(three + row, three + row + 1)
        out[at] = piece if before is None else before[at] + piece


def turn_kernel(more, info, *refs):
    field_refs, (w1_ref, mid_ref, dec_ref, bias_ref) = refs[:6], refs[6:10]
    extra_ref, masks_ref = field_refs[4:]
    target_ref, area_ref, w1t_ref, midt_ref, dect_ref = refs[10:15]
    before = refs[15] if more else None
    (
        gm_out, low_out, grads_out,
        patches, moved, active1, active2, slope1, slope2, g_out, g_pre2, g_pre1, spread,
        ends, vecs, side,
    ) = refs[-16:]
    lon_t, lat_t, chans = moved.shape
    hid = mid_ref.shape[0]
    first = pl.program_id(0) == 0
    assemble(patches, field_refs, moved)
    spread[...] = jnp.zeros_like(spread)

    @pl.when(first)
    def _():
        vecs[...] = jnp.zeros_like(vecs)
        side[...] = jnp.zeros_like(side)

    step = 8
    for x in range(0, lon_t, step):
        rows = slice(x * lat_t, (x + step) * lat_t)
        pre1 = mm(patches[rows], w1_ref[...])
        a1, d1 = gelu_and_slope(pre1)
        active1[rows] = a1.astype(BF16)
        slope1[rows] = d1
        pre2 = mm(active1[rows], mid_ref[...]) + bias_ref[0:1, :hid]
        a2, d2 = gelu_and_slope(pre2)
        active2[rows] = a2.astype(BF16)
        slope2[rows] = d2
        out = mm(active2[rows], dec_ref[...]) + bias_ref[1:2, :chans]
        fresh = moved[x : x + step] + out.reshape(step, lat_t, chans)
        diff = fresh - target_ref[0, x : x + step].astype(F32)
        valid = jnp.broadcast_to(extra_ref[0, rows, 6:7].astype(F32), (step * lat_t, chans))
        weight = valid.reshape(step, lat_t, chans) * area_ref[...][None]
        vecs[3:4, :chans] += jnp.sum(weight.reshape(step * lat_t, chans), 0, keepdims=True)
        weighted = weight * diff
        vecs[1:2, :chans] += jnp.sum((weighted * diff).reshape(step * lat_t, chans), 0, keepdims=True)
        grad = 2.0 * weighted
        moved[x : x + step] = grad
        low = grad.reshape(step * lat_t, chans).astype(BF16)
        g_out[rows] = low
        vecs[2:3, :chans] += jnp.sum(low.astype(F32), 0, keepdims=True)
        gp2 = (mm(low, dect_ref[...]) * slope2[rows]).astype(BF16)
        g_pre2[rows] = gp2
        vecs[0:1] += jnp.sum(gp2.astype(F32), 0, keepdims=True)
        gp1 = (mm(gp2, midt_ref[...]) * slope1[rows]).astype(BF16)
        g_pre1[rows] = gp1
        taps = mm(gp1, w1t_ref[...])
        for a in range(3):
            for b in range(3):
                k = 3 * a + b
                spread[b, x + a : x + a + step] += taps[:, k * chans : (k + 1) * chans].reshape(
                    step, lat_t, chans
                )
    place = lax.broadcasted_iota(jnp.int32, (lat_t, chans), 0)
    masks = masks_ref[...]
    for i in range(lon_t + 2):
        down, here, up = spread[0, i], spread[1, i], spread[2, i]
        got = here + jnp.where(place == lat_t - 1, 0.0, pltpu.roll(down, lat_t - 1, 0))
        got = got + jnp.where(place == 0, 0.0, pltpu.roll(up, 1, 0))
        beyond = down[0:1] * masks[0:1] + up[lat_t - 1 : lat_t] * masks[1:2]
        if i in (0, lon_t + 1):
            at = lon_t if i == 0 else lon_t + 1
            low_out[0, at] = got.astype(BF16)
        else:
            at = i - 1
            total = got + moved[at]
            gm_out[0, at] = total
            low_out[0, at] = total.astype(BF16)
        side[at : at + 1] = beyond
    rest = jnp.zeros((lat_t - side.shape[0], chans), F32)
    low_out[0, lon_t + 2] = jnp.concatenate([side[...], rest], axis=0).astype(BF16)
    add_grads(first, grads_out, before, patches, active1, active2, g_out, g_pre2, g_pre1, ends)

    @pl.when(pl.program_id(0) == pl.num_programs(0) - 1)
    def _():
        pack_grads(grads_out, before, chans, hid, ends, vecs)


def bottom_kernel(more, info, *refs):
    field_refs = refs[:6]
    pre1_ref, pre2_ref, gm_ref, glo_ref, ghi_ref, gs_ref, midt_ref, dect_ref = refs[6:14]
    before = refs[14] if more else None
    (
        grads_out, patches, moved, active1, active2, g_out, g_pre2, g_pre1, ends, vecs,
    ) = refs[-10:]
    lon_t, lat_t, chans = moved.shape
    hid = midt_ref.shape[0]
    first = pl.program_id(0) == 0
    assemble(patches, field_refs, moved)

    moved[...] = gm_ref[0] + gs_ref[0, :lon_t].astype(F32)
    moved[0] += glo_ref[0, 0, :lat_t].astype(F32)
    moved[lon_t - 1] += ghi_ref[0, 0, :lat_t].astype(F32)
    place = lax.broadcasted_iota(jnp.int32, (lat_t, chans), 0)
    inner = place == jnp.where(info[0] == 1, 0, lat_t - 1)
    for x in range(lon_t):
        moved[x] += jnp.where(inner, gs_ref[0, lon_t, x : x + 1].astype(F32), 0.0)

    @pl.when(first)
    def _():
        vecs[...] = jnp.zeros_like(vecs)

    step = 8
    for x in range(0, lon_t, step):
        rows = slice(x * lat_t, (x + step) * lat_t)
        a1, d1 = gelu_and_slope(pre1_ref[0, rows])
        active1[rows] = a1.astype(BF16)
        a2, d2 = gelu_and_slope(pre2_ref[0, rows])
        active2[rows] = a2.astype(BF16)
        low = moved[x : x + step].reshape(step * lat_t, chans).astype(BF16)
        g_out[rows] = low
        vecs[2:3, :chans] += jnp.sum(low.astype(F32), 0, keepdims=True)
        gp2 = (mm(low, dect_ref[...]) * d2).astype(BF16)
        g_pre2[rows] = gp2
        vecs[0:1] += jnp.sum(gp2.astype(F32), 0, keepdims=True)
        g_pre1[rows] = (mm(gp2, midt_ref[...]) * d1).astype(BF16)
    add_grads(first, grads_out, before, patches, active1, active2, g_out, g_pre2, g_pre1, ends)

    @pl.when(pl.program_id(0) == pl.num_programs(0) - 1)
    def _():
        pack_grads(grads_out, before, chans, hid, ends, vecs)


def message_spec(dims, late):
    return pl.BlockSpec((1, 1) + dims, lambda g, info: (g, late, 0, 0))


def field_specs(field, chunk, half, late, pool_state):
    state, s_ext, lo, hi, extra, masks = field
    return [
        snap_spec(state.shape[1:], chunk if pool_state else None, half),
        snap_spec(s_ext.shape[1:]),
        message_spec(lo.shape[2:], late),
        message_spec(hi.shape[2:], late),
        snap_spec(extra.shape[1:], chunk, half),
        whole(masks.shape),
    ]


def cost(micros):
    return pl.CostEstimate(flops=int(micros * 3e10), bytes_accessed=int(micros * 1e8), transcendentals=0)


def forward_call(info, chunk, half, late, field, weights, deps):
    dims = field[0].shape[1:]
    lon_t, lat_t, chans = dims
    cells = lon_t * lat_t
    hid = weights["mid"].shape[0]
    ws = [weights[k] for k in ("w1", "mid", "dec", "bias")]
    outs = [(dims, F32), (dims, BF16), ((cells, hid), F32), ((cells, hid), F32)]
    return pl.pallas_call(
        forward_kernel,
        grid_spec=grid_of(
            HALF,
            field_specs(field, chunk, half, late, True) + [whole(w.shape) for w in ws] + [any_spec()] * len(deps),
            [snap_spec(d) for d, _ in outs],
            [pltpu.VMEM((cells, 10 * chans), BF16), pltpu.VMEM(dims, F32)],
        ),
        out_shape=[shape_of((HALF,) + d, t) for d, t in outs],
        compiler_params=params(),
        cost_estimate=cost(6.5),
        name="forward",
    )(info, *field, *ws, *deps)


def back_scratch(dims, hid):
    lon_t, lat_t, chans = dims
    cells = lon_t * lat_t
    return [
        pltpu.VMEM((cells, chans), BF16),
        pltpu.VMEM((cells, hid), BF16),
        pltpu.VMEM((cells, hid), BF16),
    ], [
        pltpu.VMEM((8, hid), F32),
        pltpu.VMEM((8, hid), F32),
    ]


def turn_call(info, chunk, half, late, field, weights, targets, area, deps, before):
    dims = field[0].shape[1:]
    lon_t, lat_t, chans = dims
    cells = lon_t * lat_t
    hid = weights["mid"].shape[0]
    ws = [weights[k] for k in ("w1", "mid", "dec", "bias")]
    wt = [weights[k] for k in ("w1t", "midt", "dect")]
    grad_rows = grad_layout(chans, hid)[-1]
    more = before is not None
    last = [before] if more else []
    outs = [(dims, F32), ((lon_t + 3, lat_t, chans), BF16)]
    grads, sums = back_scratch(dims, hid)
    return pl.pallas_call(
        functools.partial(turn_kernel, more),
        grid_spec=grid_of(
            HALF,
            field_specs(field, chunk, half, late, False)
            + [whole(w.shape) for w in ws]
            + [snap_spec(dims, chunk, half), whole(area.shape)]
            + [whole(w.shape) for w in wt + last]
            + [any_spec()] * len(deps),
            [snap_spec(d) for d, _ in outs] + [whole((grad_rows, hid))],
            [
                pltpu.VMEM((cells, 10 * chans), BF16),
                pltpu.VMEM(dims, F32),
                pltpu.VMEM((cells, hid), BF16),
                pltpu.VMEM((cells, hid), BF16),
                pltpu.VMEM((cells, hid), F32),
                pltpu.VMEM((cells, hid), F32),
            ]
            + grads
            + [pltpu.VMEM((3, lon_t + 2, lat_t, chans), F32)]
            + sums
            + [pltpu.VMEM((lon_t + 8, chans), F32)],
        ),
        out_shape=[shape_of((HALF,) + d, t) for d, t in outs] + [shape_of((grad_rows, hid), F32)],
        compiler_params=params(),
        cost_estimate=cost(13.0),
        name="turn",
    )(info, *field, *ws, targets, area, *wt, *last, *deps)


def bottom_call(info, chunk, half, late, field, weights, pre, gm, glo, ghi, glate, gs, deps, before):
    dims = field[0].shape[1:]
    lon_t, lat_t, chans = dims
    cells = lon_t * lat_t
    hid = weights["mid"].shape[0]
    wt = [weights[k] for k in ("midt", "dect")]
    grad_rows = grad_layout(chans, hid)[-1]
    more = before is not None
    last = [before] if more else []
    grads, sums = back_scratch(dims, hid)
    return pl.pallas_call(
        functools.partial(bottom_kernel, more),
        grid_spec=grid_of(
            HALF,
            field_specs(field, chunk, half, late, True)
            + [snap_spec(v.shape[1:]) for v in (*pre, gm)]
            + [message_spec(glo.shape[2:], glate)] * 2
            + [snap_spec(gs.shape[1:])]
            + [whole(w.shape) for w in wt + last]
            + [any_spec()] * len(deps),
            whole((grad_rows, hid)),
            [
                pltpu.VMEM((cells, 10 * chans), BF16),
                pltpu.VMEM(dims, F32),
                pltpu.VMEM((cells, hid), BF16),
                pltpu.VMEM((cells, hid), BF16),
            ]
            + grads
            + sums,
        ),
        out_shape=shape_of((grad_rows, hid), F32),
        compiler_params=params(),
        cost_estimate=cost(8.0),
        name="bottom",
    )(info, *field, *pre, gm, glo, ghi, gs, *wt, *last, *deps)


def three_parts(vec):
    high = lax.reduce_precision(vec, 8, 7)
    rest = vec - high
    mid = lax.reduce_precision(rest, 8, 7)
    low = lax.reduce_precision(rest - mid, 8, 7)
    return jnp.stack([high, mid, low], axis=-2)


def layer_weights(enc, mid, dec, vec):
    taps, chans, hid = enc.shape
    parts = jnp.concatenate([three_parts(vec[hid : 2 * hid]), three_parts(vec[:hid])], axis=0)
    parts = jnp.pad(parts, ((0, chans - 6), (0, 0)))
    w1 = jnp.concatenate([enc.reshape(taps * chans, hid), parts], axis=0).astype(BF16)
    pad = jnp.zeros((hid - chans,), F32)
    bias = jnp.stack([vec[2 * hid : 3 * hid], jnp.concatenate([vec[3 * hid :], pad])])
    return {
        "w1": w1,
        "mid": mid.astype(BF16),
        "dec": dec.astype(BF16),
        "bias": bias,
        "w1t": jnp.transpose(enc, (2, 0, 1)).reshape(hid, taps * chans).astype(BF16),
        "midt": mid.T.astype(BF16),
        "dect": dec.T.astype(BF16),
    }


def reduce_steps(part, order):
    lon_n = lax.axis_size("lon")
    me = lax.axis_index("lon")

    def over(stride):
        return "lon", (me // stride) % 2, [(i, i ^ stride) for i in range(lon_n)]

    links = {"core": over(1), "x": over(2), "y": ("lat", lax.axis_index("lat"), [(0, 1), (1, 0)]), "z": over(8)}
    stages = [links[name] for name in order]

    def after(x, hold):
        return x if hold is None else lax.optimization_barrier((x, hold))[0]

    hold = None
    for axis, bit, perm in stages:
        half = part.shape[0] // 2
        give = lax.dynamic_slice_in_dim(part, (1 - bit) * half, half)
        mine = lax.dynamic_slice_in_dim(part, bit * half, half)
        part = after(mine, hold) + lax.ppermute(give, axis, perm)
        hold = yield part
    axis, _, perm = over(4)
    part = after(part, hold) + lax.ppermute(part, axis, perm)
    hold = yield part
    for axis, bit, perm in reversed(stages):
        got = lax.ppermute(part, axis, perm)
        part = after(part, hold)
        part = jnp.concatenate([jnp.where(bit == 0, part, got), jnp.where(bit == 0, got, part)])
        hold = yield part


def fast_grads(states, targets, sea_temp, ocean, valid, w_enc, w_mid, w_dec, biases):
    pool, lon_t, lat_t, chans = states.shape
    lon_n, lat_n = lax.axis_size("lon"), lax.axis_size("lat")
    nlon, nlat = lon_t * lon_n, lat_t * lat_n
    zonal, forward, inverse, area_all = host_tables(nlon, nlat, 88)
    hemi = lax.axis_index("lat")
    info = hemi[None].astype(jnp.int32)
    flip = np.concatenate([np.arange(lat_t, nlat), np.arange(lat_t)])
    flip2 = np.concatenate([flip, nlat + flip])
    ends = (np.arange(0, nlon, lon_t)[None, :] + np.array([[-1], [lon_t]])).reshape(-1) % nlon
    zonal_in = jnp.asarray(np.concatenate([zonal, zonal[:, ends]], axis=1))
    zonal_out = jnp.asarray(
        np.concatenate([zonal[:nlon], zonal[:nlon][ends], zonal[nlon:], zonal[nlon:][ends]], axis=0)
    )
    forward = jnp.where(hemi == 0, jnp.asarray(forward), jnp.asarray(forward[:, flip]))
    inverse = jnp.where(hemi == 0, jnp.asarray(inverse), jnp.asarray(inverse[flip2]))
    side = jnp.stack([hemi == 1, hemi == 0]).astype(F32)
    masks = jnp.broadcast_to(side[:, None], (2, chans))
    area = lax.dynamic_slice_in_dim(jnp.asarray(area_all, F32), hemi * lat_t, lat_t)
    area_wide = jnp.broadcast_to(area[:, None], (lat_t, chans))
    up = [(i, (i + 1) % lon_n) for i in range(lon_n)]
    down = [(t, s) for s, t in up]
    swap = [(0, 1), (1, 0)]
    chunks = range(pool // CHUNK)

    first_traded = lax.ppermute(pick_call(info, states, 0, 1, []), "lat", swap)
    held = lax.optimization_barrier((first_traded, w_enc, w_mid, w_dec, biases))
    _, w_enc, w_mid, w_dec, biases = held
    layers = [layer_weights(w_enc[i], w_mid[i], w_dec[i], biases[i]) for i in range(2)]

    last = [forward]

    def then(result, pick=None):
        last[:] = [result if pick is None else result[pick]]
        return result

    def over_lon(spec):
        return lax.all_to_all(spec, "lon", split_axis=0, concat_axis=0, tiled=True)

    class Chunk:
        def __init__(self, c):
            self.c = c
            self.early = 0
            self.round = 0
            self.other = first_traded
            self.field0, self.pres = [None, None], [None, None]
            self.fresh, self.low, self.s_ext, self.gm = ([None, None] for _ in range(4))

        def legendre(self):
            half = self.early
            own, late = (states, states) if self.round == 0 else (self.low[half], self.low[1 - half])
            there = self.c if self.round == 0 else None
            wide = self.round == 2
            got = legendre_call(info, own, late, there, half, self.other, forward, last, wide)
            spec, to_up, to_down, sides = then(got, 0)
            self.spec = over_lon(spec)
            self.lo, self.hi = lax.ppermute(to_up, "lon", up), lax.ppermute(to_down, "lon", down)
            self.rows_of = (own, self.other) if wide else (sides,)

        def zonal(self):
            table = zonal_in if self.round == 2 else zonal_out
            self.spec = over_lon(then(zonal_call(self.spec, table, last, self.round == 2)))

        def synthesis(self):
            got = synthesis_call(
                info, self.spec, self.lo, self.hi, inverse, self.rows_of, HALF, self.round < 2, last
            )
            own, send = then(got, 0)
            self.s_ext[self.early] = own
            self.s_ext[1 - self.early] = lax.ppermute(send, "lat", swap)

        def forward(self, late):
            half = self.early ^ late
            field = (states, self.s_ext[half], self.lo, self.hi, extra, masks)
            self.field0[half] = field
            got = forward_call(info, self.c, half, late, field, layers[0], last)
            self.fresh[half], self.low[half], *pre = then(got, 1)
            self.pres[half] = pre
            self.send(half, late)

        def turn(self, late, before):
            half = self.early ^ late
            field = (self.fresh[half], self.s_ext[half], self.lo, self.hi, extra, masks)
            got = turn_call(
                info, self.c, half, late, field, layers[1], targets, area_wide, last, before
            )
            self.gm[half], self.low[half], before = then(got, 1)
            self.send(half, late)
            return before

        def send(self, half, late):
            if not late:
                self.other = lax.ppermute(self.low[half], "lat", swap)

        def flip(self):
            self.early = 1 - self.early
            self.round += 1

        def bottom(self, late, before):
            half = self.early ^ late
            got = bottom_call(
                info, self.c, half, late, self.field0[half], layers[0], self.pres[half],
                self.gm[half], self.lo, self.hi, late, self.s_ext[half], last, before,
            )
            return then(got)

    a, b = (Chunk(c) for c in chunks)
    top, low = None, None
    a.legendre()
    b.other = lax.ppermute(then(pick_call(info, states, 1, 1, last)), "lat", swap)
    a.zonal()
    _, ocean, sea_temp, valid = lax.optimization_barrier((last[0], ocean, sea_temp, valid))
    sea = ocean.astype(F32) * sea_temp.astype(F32)
    cells = lon_t * lat_t
    lane = jnp.arange(chans)
    wide_sea = sea.reshape(pool, cells, 1).astype(BF16)
    wide_valid = valid.reshape(pool, cells, 1).astype(BF16)
    extra = jnp.where(lane < 3, wide_sea, jnp.where(lane < 6, jnp.ones((), BF16), wide_valid))
    extra = jnp.where(lane < 7, extra, jnp.zeros((), BF16))
    b.legendre()
    for one, two in ((a, b), (b, a)):
        one.synthesis()
        one.forward(0)
        two.zonal()
        one.forward(1)
        one.flip()
        one.legendre()
    for one, two in ((a, b), (b, a)):
        one.synthesis()
        top = one.turn(0, top)
        two.zonal()
        top = one.turn(1, top)
        one.flip()
        one.legendre()
    a.synthesis()
    top, _ = lax.optimization_barrier((top, last[0]))
    upper = reduce_steps(top, ("core", "y", "x", "z"))
    low = a.bottom(0, low)
    b.zonal()
    last.append(next(upper))
    low = a.bottom(1, low)
    last.append(next(upper))
    b.synthesis()
    last.append(next(upper))
    low = b.bottom(0, low)
    last.append(next(upper))
    low = b.bottom(1, low)
    lower = reduce_steps(low, ("core", "x", "y", "z"))
    *_, high = upper
    *_, low = lower
    return low, high


def update_kernel(rate, taps_each, info, g0_ref, g1_ref, m0_ref, m1_ref, v0_ref, v1_ref, *refs):
    ins, outs = refs[:12], refs[12:]
    layer, part = pl.program_id(0), pl.program_id(1)
    chans, hid = ins[0].shape[2:]
    scale = 1.0 / v1_ref[4:5, 0:1]

    def apply(group, at, grad):
        w_ref, m_ref, a_ref = (ins[4 * i + group] for i in range(3))
        new_ref, mom_ref, avg_ref, copy_ref = (outs[4 * i + group] for i in range(4))
        scaled = grad * scale
        mom = MOMENTUM * m_ref[at] + scaled
        fresh = w_ref[at] - rate * (scaled + MOMENTUM * mom)
        new_ref[at] = fresh
        mom_ref[at] = mom
        avg_ref[at] = AVERAGE * a_ref[at] + (1.0 - AVERAGE) * fresh
        copy_ref[at] = fresh.astype(BF16)

    def layer_step(g_ref, m_ref):
        for tap in range(taps_each):
            apply(0, (0, tap), g_ref[tap * chans : (tap + 1) * chans])

        @pl.when(part == 0)
        def _():
            apply(1, (0,), m_ref[:hid])
            apply(2, (0,), m_ref[hid:].T)

    pl.when(layer == 0)(lambda: layer_step(g0_ref, m0_ref))
    pl.when(layer == 1)(lambda: layer_step(g1_ref, m1_ref))

    @pl.when((layer == 0) & (part == 0))
    def _():
        for i, v_ref in enumerate((v0_ref, v1_ref)):
            for r in range(4):
                wide = hid if r < 3 else chans
                at = (slice(i, i + 1), slice(r * hid, r * hid + wide))
                apply(3, at, v_ref[r : r + 1, :wide])


TAPS_EACH = 9


def update_call(rate, sums, arrays):
    w_enc, w_mid, w_dec, biases = arrays[:4]
    layers, taps, chans, hid = w_enc.shape
    one, _, three, _ = grad_layout(chans, hid)
    steps = taps // TAPS_EACH
    rows = TAPS_EACH * chans
    enc = pl.BlockSpec((1, TAPS_EACH, chans, hid), lambda i, p, info: (i, p, 0, 0))
    mid = pl.BlockSpec((1, hid, hid), lambda i, p, info: (i, 0, 0))
    dec = pl.BlockSpec((1, hid, chans), lambda i, p, info: (i, 0, 0))
    bias = whole(biases.shape)
    specs = [enc, mid, dec, bias]
    shapes = [w_enc.shape, w_mid.shape, w_dec.shape, biases.shape]
    grads = [
        pl.BlockSpec((rows, hid), lambda i, p, info: (jnp.where(i == 0, p, steps - 1), 0)),
        pl.BlockSpec((rows, hid), lambda i, p, info: (jnp.where(i == 0, 0, p), 0)),
        pl.BlockSpec((three - one, hid), lambda i, p, info: (one // (three - one), 0)),
        pl.BlockSpec((three - one, hid), lambda i, p, info: (one // (three - one), 0)),
        pl.BlockSpec((8, hid), lambda i, p, info: (three // 8, 0)),
        pl.BlockSpec((8, hid), lambda i, p, info: (three // 8, 0)),
    ]
    got = pl.pallas_call(
        functools.partial(update_kernel, rate, TAPS_EACH),
        grid_spec=pltpu.PrefetchScalarGridSpec(
            num_scalar_prefetch=1,
            grid=(layers, steps),
            in_specs=grads + specs * 3,
            out_specs=specs * 4,
        ),
        out_shape=[shape_of(s, F32) for s in shapes * 3] + [shape_of(s, BF16) for s in shapes],
        compiler_params=params(),
        cost_estimate=cost(8.0),
        name="update",
    )(jnp.zeros((1,), jnp.int32), sums[0], sums[1], sums[0], sums[1], sums[0], sums[1], *arrays)
    vecs = sums[1][three : three + 8]
    return (jnp.sum(vecs[3, chans:]), vecs[4, 0], *got)


def fits(states, w_mid, lon_n, lat_n):
    pool, lon_t, lat_t, chans = states.shape
    return (
        lat_n == 2
        and lon_n == 16
        and lon_t == 16
        and lat_t == 64
        and pool == 2 * CHUNK
        and chans == 128
        and w_mid.shape[1] == 2 * chans
        and w_mid.shape[0] == 2
    )


def with_halo(block, sides, width, periodic):
    for axis, dim in sides:
        count = lax.axis_size(axis)
        forward = [(i, i + 1) for i in range(count - 1)]
        if periodic:
            forward.append((count - 1, 0))
        backward = [(target, source) for source, target in forward]
        low = lax.ppermute(
            lax.slice_in_dim(block, block.shape[dim] - width, None, axis=dim), axis, forward
        )
        high = lax.ppermute(lax.slice_in_dim(block, 0, width, axis=dim), axis, backward)
        block = jnp.concatenate([low, block, high], axis=dim)
    return block


def tables(nlon, nlat, groups):
    coeffs = jnp.arange(2 * MW)
    wave = jnp.where(coeffs < MW, coeffs, coeffs - MW + 1).astype(jnp.float32)
    places = jnp.arange(nlon).astype(jnp.float32)
    angle = 2.0 * math.pi * wave[:, None] * places[None, :] / nlon
    fourier = jnp.where((coeffs < MW)[:, None], jnp.cos(angle), jnp.sin(angle)) * math.sqrt(
        2.0 / nlon
    )
    phase = ((jnp.arange(nlat).astype(jnp.float32) + 0.5) / nlat - 0.5) * math.pi
    sine = jnp.sin(phase)
    quad = jnp.cos(phase) * math.pi / nlat
    polys = [jnp.ones_like(sine), sine]
    for degree in range(1, NDEG - 1):
        polys.append(((2 * degree + 1) * sine * polys[-1] - degree * polys[-2]) / (degree + 1))
    stacked = jnp.stack(polys[:NDEG])
    degrees = jnp.arange(NDEG).astype(jnp.float32)
    legendre = jnp.sqrt((2 * degrees + 1) / 2)[:, None] * jnp.sqrt(quad)[None, :] * stacked
    damping = 1.5 * (1.0 - 2.0 * degrees * (degrees + 1) / (NDEG * (NDEG + 1)))
    filters = damping[None, :] * (1.0 - 0.5 * wave / MW)[:, None]
    kept = 2 * MW
    slots = (kept + groups - 1) // groups * groups
    fourier = jnp.pad(fourier, ((0, slots - kept), (0, 0)))
    filters = jnp.pad(filters, ((0, slots - kept), (0, 0)))
    return (fourier, legendre, filters)


def spectral(values, tabs):
    fourier, legendre, filters = tabs
    cycles = lax.all_to_all(
        values.astype(jnp.bfloat16), "lon", split_axis=3, concat_axis=1, tiled=True
    ).astype(values.dtype)
    coeff = jnp.einsum("kx,sxjc->skjc", fourier, cycles, precision=HIGH)
    block = fourier.shape[0] // lax.axis_size("lat")
    where = lax.axis_index("lat")
    block_filter = lax.dynamic_slice_in_dim(filters, where * block, block, 0)
    columns = lax.all_to_all(
        coeff.astype(jnp.bfloat16), "lat", split_axis=1, concat_axis=2, tiled=True
    ).astype(coeff.dtype)
    spec = (
        jnp.einsum("nj,skjc->sknc", legendre, columns, precision=HIGH)
        * block_filter[None, :, :, None]
    )
    back = jnp.einsum("nj,sknc->skjc", legendre, spec, precision=HIGH)
    coeff_back = lax.all_to_all(
        back.astype(jnp.bfloat16), "lat", split_axis=2, concat_axis=1, tiled=True
    ).astype(back.dtype)
    grid = jnp.einsum("kx,skjc->sxjc", fourier, coeff_back, precision=HIGH)
    return lax.all_to_all(
        grid.astype(jnp.bfloat16), "lon", split_axis=1, concat_axis=3, tiled=True
    ).astype(grid.dtype)


def extend(field):
    wider = with_halo(field, (("lon", 1),), 1, True)
    return with_halo(wider, (("lat", 2),), 1, False)


def neighbours(padded, flipped, lon_t, lat_t):
    parts = []
    for row_off in range(3):
        for col_off in range(3):
            first = 2 - row_off if flipped else row_off
            second = 2 - col_off if flipped else col_off
            parts.append(padded[:, first : first + lon_t, second : second + lat_t])
    stacked = jnp.stack(parts, axis=3)
    return stacked.reshape(-1, 9 * padded.shape[-1])


def gelu_fn(value):
    return jax.nn.gelu(value, approximate=True)


def gelu_back(value, grad):
    return jax.vjp(gelu_fn, value)[1](grad)[0]


def layer_forward(state, sea, enc, mid, dec, vec, tabs):
    hid = mid.shape[0]
    lon_t, lat_t = (state.shape[1], state.shape[2])
    moved = state + spectral(state, tabs)
    patches = neighbours(extend(moved.astype(jnp.bfloat16)), False, lon_t, lat_t)
    pre1 = jnp.dot(patches, enc, preferred_element_type=jnp.float32)
    pre1 = pre1 + sea.reshape(-1, 1) * vec[hid : 2 * hid] + vec[:hid]
    active1 = gelu_fn(pre1).astype(jnp.bfloat16)
    pre2 = jnp.dot(active1, mid, preferred_element_type=jnp.float32) + vec[2 * hid : 3 * hid]
    active2 = gelu_fn(pre2).astype(jnp.bfloat16)
    output = jnp.dot(active2, dec, preferred_element_type=jnp.float32) + vec[3 * hid :]
    return (moved + output.reshape(state.shape), (patches, pre1, active1, pre2, active2))


def layer_backward(grad_state, sea, enc, mid, dec, saved, tabs):
    patches, pre1, active1, pre2, active2 = saved
    hid = mid.shape[0]
    shape = grad_state.shape
    chans = shape[-1]
    g_out = grad_state.reshape(-1, chans).astype(jnp.bfloat16)
    g_dec = jnp.einsum("rh,rc->hc", active2, g_out, preferred_element_type=jnp.float32)
    g_act2 = jnp.einsum("rc,hc->rh", g_out, dec, preferred_element_type=jnp.float32)
    g_pre2 = gelu_back(pre2, g_act2).astype(jnp.bfloat16)
    g_mid = jnp.einsum("rh,rg->hg", active1, g_pre2, preferred_element_type=jnp.float32)
    g_act1 = jnp.einsum("rg,hg->rh", g_pre2, mid, preferred_element_type=jnp.float32)
    g_pre1 = gelu_back(pre1, g_act1).astype(jnp.bfloat16)
    g_enc = jnp.einsum("rk,rh->kh", patches, g_pre1, preferred_element_type=jnp.float32)
    wide1 = g_pre1.astype(jnp.float32)
    g_vec = jnp.concatenate(
        [
            jnp.sum(wide1, 0),
            jnp.sum(sea.reshape(-1, 1) * wide1, 0),
            jnp.sum(g_pre2.astype(jnp.float32), 0),
            jnp.sum(g_out.astype(jnp.float32), 0),
        ]
    )
    spread = extend(g_pre1.reshape(shape[0], shape[1], shape[2], hid))
    gathered = neighbours(spread, True, shape[1], shape[2]).reshape(-1, 9, hid)
    g_input = jnp.einsum(
        "rkh,kch->rc", gathered, enc.reshape(9, chans, hid), preferred_element_type=jnp.float32
    )
    grad_moved = grad_state + g_input.reshape(shape)
    return (grad_moved + spectral(grad_moved, tabs), (g_enc, g_mid, g_dec, g_vec))


def general_grads(states, targets, sea_temp, ocean, valid, order, w_enc, w_mid, w_dec, biases):
    pool, lon_t, lat_t, chans = states.shape
    layers, hid = (w_mid.shape[0], w_mid.shape[1])
    nlon = lon_t * lax.axis_size("lon")
    nlat = lat_t * lax.axis_size("lat")
    tabs = tables(nlon, nlat, lax.axis_size("lat"))
    lat_glob = (lax.axis_index("lat") * lat_t + jnp.arange(lat_t)).astype(jnp.float32)
    area = jnp.cos(((lat_glob + 0.5) / nlat - 0.5) * math.pi)
    enc_low = w_enc.astype(jnp.bfloat16).reshape(layers, 9 * chans, hid)
    mid_low = w_mid.astype(jnp.bfloat16)
    dec_low = w_dec.astype(jnp.bfloat16)
    snaps = pool // MB
    sums = [
        jnp.zeros((layers, 9 * chans, hid), jnp.float32),
        jnp.zeros_like(w_mid),
        jnp.zeros_like(w_dec),
        jnp.zeros_like(biases),
    ]
    loss = jnp.zeros((), jnp.float32)
    total = jnp.zeros((), jnp.float32)
    for batch_id in range(MB):
        picks = lax.dynamic_slice_in_dim(order, batch_id * snaps, snaps)
        state = jnp.take(states, picks, axis=0).astype(jnp.float32)
        target = jnp.take(targets, picks, axis=0).astype(jnp.float32)
        sea = jnp.take(ocean, picks, axis=0).astype(jnp.float32) * jnp.take(
            sea_temp, picks, axis=0
        ).astype(jnp.float32)
        weight = jnp.take(valid, picks, axis=0).astype(jnp.float32) * area[None, None, :]
        kept = []
        for layer_id in range(layers):
            state, saved = layer_forward(
                state,
                sea,
                enc_low[layer_id],
                mid_low[layer_id],
                dec_low[layer_id],
                biases[layer_id],
                tabs,
            )
            kept.append(saved)
        diff = state - target
        loss = loss + jnp.sum(weight[..., None] * diff * diff)
        total = total + jnp.sum(weight)
        grad_state = 2.0 * weight[..., None] * diff
        for layer_id in reversed(range(layers)):
            grad_state, found = layer_backward(
                grad_state,
                sea,
                enc_low[layer_id],
                mid_low[layer_id],
                dec_low[layer_id],
                kept[layer_id],
                tabs,
            )
            sums = [acc.at[layer_id].add(part) for acc, part in zip(sums, found)]
    g_enc, g_mid, g_dec, g_vec, loss, total = lax.psum(
        (sums[0], sums[1], sums[2], sums[3], loss, total), ("lon", "lat")
    )
    return g_enc.reshape(w_enc.shape), g_mid, g_dec, g_vec, loss, total


def body(
    states,
    targets,
    sea_temp,
    ocean,
    valid,
    order,
    w_enc,
    w_mid,
    w_dec,
    biases,
    mom_enc,
    mom_mid,
    mom_dec,
    mom_bias,
    avg_enc,
    avg_mid,
    avg_dec,
    avg_bias,
):
    pool, lon_t, lat_t = states.shape[:3]
    lon_n, lat_n = lax.axis_size("lon"), lax.axis_size("lat")
    rate = RATE_BASE * math.sqrt(pool * lon_t * lon_n * lat_t * lat_n)
    if fits(states, w_mid, lon_n, lat_n):
        sums = fast_grads(states, targets, sea_temp, ocean, valid, w_enc, w_mid, w_dec, biases)
        arrays = (w_enc, w_mid, w_dec, biases, mom_enc, mom_mid, mom_dec, mom_bias)
        arrays += (avg_enc, avg_mid, avg_dec, avg_bias)
        return update_call(rate, sums, arrays)
    found = general_grads(
        states, targets, sea_temp, ocean, valid, order, w_enc, w_mid, w_dec, biases
    )
    loss, total = found[4:]
    grads = (found[0].reshape(w_enc.shape),) + found[1:4]
    news, moms, avgs, copies = ([], [], [], [])
    for weight_now, grad, mom, avg in zip(
        (w_enc, w_mid, w_dec, biases),
        grads,
        (mom_enc, mom_mid, mom_dec, mom_bias),
        (avg_enc, avg_mid, avg_dec, avg_bias),
    ):
        scaled = grad / total
        mom_new = MOMENTUM * mom + scaled
        fresh = weight_now - rate * (scaled + MOMENTUM * mom_new)
        news.append(fresh)
        moms.append(mom_new)
        avgs.append(AVERAGE * avg + (1.0 - AVERAGE) * fresh)
        copies.append(fresh.astype(jnp.bfloat16))
    return (
        loss,
        total,
        news[0],
        news[1],
        news[2],
        news[3],
        moms[0],
        moms[1],
        moms[2],
        moms[3],
        avgs[0],
        avgs[1],
        avgs[2],
        avgs[3],
        copies[0],
        copies[1],
        copies[2],
        copies[3],
    )


def solution(mesh):
    placed = (
        P(None, "lon", "lat", None),
        P(None, "lon", "lat", None),
        P(None, "lon", "lat"),
        P(None, "lon", "lat"),
        P(None, "lon", "lat"),
        P(),
        P(),
        P(),
        P(),
        P(),
        P(),
        P(),
        P(),
        P(),
        P(),
        P(),
        P(),
        P(),
    )
    return jax.shard_map(
        body,
        mesh=mesh,
        in_specs=placed,
        out_specs=(
            P(),
            P(),
            P(),
            P(),
            P(),
            P(),
            P(),
            P(),
            P(),
            P(),
            P(),
            P(),
            P(),
            P(),
            P(),
            P(),
            P(),
            P(),
        ),
        check_vma=False,
    )
```

```python
import functools
import math

import jax
import jax.numpy as jnp
import numpy as np
from jax import lax
from jax.experimental import pallas as pl
from jax.experimental.pallas import tpu as pltpu
from jax.sharding import PartitionSpec as P

MW = 86
NDEG = 86
MB = 4


HIGH = lax.Precision.HIGHEST
MOMENTUM = 0.9
AVERAGE = 0.99
RATE_BASE = 0.0006

F32 = jnp.float32
BF16 = jnp.bfloat16
CHUNK = 4
VMEM = 56 * 1024 * 1024
GELU_A = math.sqrt(2.0 / math.pi)
GELU_B = 0.044715


def split_table(table):
    table = np.asarray(table, np.float32)
    high = table.astype(BF16)
    low = (table - high.astype(np.float32)).astype(BF16)
    return np.concatenate([high, low], axis=0)


def host_tables(nlon, nlat, deg):
    kept = np.arange(2 * MW)
    wave = np.where(kept < MW, kept, kept - MW + 1).astype(np.float64)
    angle = 2.0 * np.pi * wave[:, None] * np.arange(nlon)[None, :] / nlon
    fourier = np.where((kept < MW)[:, None], np.cos(angle), np.sin(angle)) * np.sqrt(2.0 / nlon)
    zonal = (fourier * (1.0 - 0.5 * wave / MW)[:, None]).T @ fourier
    phase = ((np.arange(nlat) + 0.5) / nlat - 0.5) * np.pi
    sine, area = np.sin(phase), np.cos(phase)
    polys = [np.ones_like(sine), sine]
    for n in range(1, NDEG - 1):
        polys.append(((2 * n + 1) * sine * polys[-1] - n * polys[-2]) / (n + 1))
    degrees = np.arange(NDEG)
    legendre = np.sqrt((2 * degrees + 1) / 2)[:, None] * np.sqrt(area * np.pi / nlat)[None, :]
    legendre = legendre * np.stack(polys)
    damping = 1.5 * (1.0 - 2.0 * degrees * (degrees + 1) / (NDEG * (NDEG + 1)))
    forward = np.zeros((deg, nlat))
    forward[:NDEG] = legendre
    inverse = np.zeros((nlat, -(-deg // 32) * 32))
    inverse[:, :NDEG] = (legendre * damping[:, None]).T
    return split_table(zonal), split_table(forward), split_table(inverse), area


def mm(a, b):
    return jnp.dot(a, b, preferred_element_type=F32)


def mm_rows(a, b):
    return lax.dot_general(a, b, (((0,), (0,)), ((), ())), preferred_element_type=F32)


def whole(shape):
    return pl.BlockSpec(shape, lambda *_: (0,) * len(shape))


def params():
    return pltpu.CompilerParams(vmem_limit_bytes=VMEM)


HALF = CHUNK // 2


def any_spec():
    return pl.BlockSpec(memory_space=pl.ANY)


def shape_of(dims, dtype):
    return jax.ShapeDtypeStruct(dims, dtype)


def grid_of(count, in_specs, out_specs, scratch):
    return pltpu.PrefetchScalarGridSpec(
        num_scalar_prefetch=1,
        grid=(count,),
        in_specs=in_specs,
        out_specs=out_specs,
        scratch_shapes=scratch,
    )


def first_of(chunk, half, info):
    if chunk is None:
        return 0
    return chunk * CHUNK + HALF * (info[0] if half == 0 else 1 - info[0])


def snap_spec(dims, chunk=None, half=0):
    return pl.BlockSpec(
        (1,) + dims, lambda g, info: (first_of(chunk, half, info) + g,) + (0,) * len(dims)
    )


def pick_kernel(info, x_ref, *refs):
    refs[-1][...] = x_ref[...]


def pick_call(info, fields, chunk, half, deps):
    dims = fields.shape[1:]
    return pl.pallas_call(
        pick_kernel,
        grid_spec=grid_of(
            HALF, [snap_spec(dims, chunk, half)] + [any_spec()] * len(deps), snap_spec(dims), []
        ),
        out_shape=shape_of((HALF,) + dims, fields.dtype),
        compiler_params=params(),
        cost_estimate=cost(1.0),
        name="pick",
    )(info, fields, *deps)


def legendre_kernel(
    wide, info, own_ref, other_ref, first_ref, last_ref, l_ref, *refs
):
    o_ref, up_ref, down_ref, rows_ref, tmp = refs[-5:]
    parts, rows, lon_t, chans = o_ref.shape
    lat_t = own_ref.shape[2]
    deg = l_ref.shape[0] // 2
    count = lon_t + 2 if wide else lon_t
    each = deg // parts
    place = lax.broadcasted_iota(jnp.int32, (lat_t, chans), 0)
    south = info[0] == 1
    inner = place == jnp.where(south, 0, lat_t - 1)
    other_inner = place == jnp.where(south, lat_t - 1, 0)

    def column(x):
        own, other = own_ref[0, x], other_ref[0, x]
        if wide:
            to_own = other_ref[0, count, x : x + 1].astype(F32)
            to_other = own_ref[0, count, x : x + 1].astype(F32)
            own = (own.astype(F32) + jnp.where(inner, to_own, 0.0)).astype(BF16)
            other = (other.astype(F32) + jnp.where(other_inner, to_other, 0.0)).astype(BF16)
        else:
            own_f, other_f = own.astype(F32), other.astype(F32)
            ends = [(own_f[:1], own_f[lat_t - 1 :]), (other_f[lat_t - 1 :], other_f[:1])]
            for i, (if_south, if_north) in enumerate(ends):
                rows_ref[0, i, x : x + 1] = jnp.where(south, if_south, if_north)
        return jnp.concatenate([own, other], axis=0)

    for base in range(0, count, 4):
        span = range(base, min(base + 4, count))
        r = mm(l_ref[...], jnp.concatenate([column(x) for x in span], axis=1))
        r = r[:deg] + r[deg:]
        for x in span:
            tmp[:deg, x, :] = r[:, (x - base) * chans : (x - base + 1) * chans]
    o_ref[:, :each] = tmp[:deg, :lon_t, :].astype(BF16).reshape(parts, each, lon_t, chans)
    if wide:
        rest = jnp.zeros((lon_t - each, chans), F32)
        for p in range(parts):
            for side in range(2):
                edge = tmp[p * each : (p + 1) * each, lon_t + side, :]
                o_ref[p, each + side] = jnp.concatenate([edge, rest], axis=0).astype(BF16)
        rows_ref[...] = jnp.zeros_like(rows_ref)
    for ref, late_ref, x in ((down_ref, first_ref, 0), (up_ref, last_ref, lon_t - 1)):
        if wide:
            at = lon_t if x == 0 else lon_t + 1
            corner, far = other_ref[0, count, at : at + 1], own_ref[0, count, at : at + 1]
            pieces = [jnp.broadcast_to(v.astype(F32), (8, chans)) for v in (corner, far)]
        else:
            at = x
            pieces = [jnp.broadcast_to(rows_ref[0, 1, x : x + 1], (16, chans))]
        ref[0, 0, :lat_t] = own_ref[0, at]
        ref[0, 0, lat_t:] = jnp.concatenate(pieces, axis=0).astype(BF16)
        ref[0, 1, :lat_t] = late_ref[0, 0]
        ref[0, 1, lat_t:] = jnp.zeros((16, chans), BF16)


def legendre_call(info, own, late, chunk, half, other, table, deps, wide):
    snaps, slabs, lat_t, chans = other.shape
    deg = table.shape[0] // 2
    parts = 8
    lon_t = slabs - 3 if wide else slabs
    rows = deg // parts + (2 if wide else 0)
    message = (2, lat_t + 16, chans)
    sides = (2, lon_t, chans)

    def late_column(x):
        return pl.BlockSpec(
            (1, 1, lat_t, chans), lambda g, info: (first_of(chunk, 1 - half, info) + g, x, 0, 0)
        )

    columns = (lon_t, lon_t + 1) if wide else (0, lon_t - 1)
    return pl.pallas_call(
        functools.partial(legendre_kernel, wide),
        grid_spec=grid_of(
            snaps,
            [
                snap_spec(own.shape[1:], chunk, half),
                snap_spec(other.shape[1:]),
                late_column(columns[0]),
                late_column(columns[1]),
                whole(table.shape),
            ]
            + [any_spec()] * len(deps),
            [
                pl.BlockSpec((parts, rows, lon_t, chans), lambda s, info: (s, 0, 0, 0)),
                snap_spec(message),
                snap_spec(message),
                snap_spec(sides),
            ],
            [pltpu.VMEM((-(-deg // 32) * 32, lon_t + 8 if wide else lon_t, chans), F32)],
        ),
        out_shape=[
            shape_of((snaps * parts, rows, lon_t, chans), BF16),
            shape_of((snaps,) + message, BF16),
            shape_of((snaps,) + message, BF16),
            shape_of((snaps,) + sides, F32),
        ],
        compiler_params=params(),
        cost_estimate=cost(3.4),
        name="legendre",
    )(info, own, other, late, late, table, *deps)


def zonal_kernel(wide_in, x_ref, a_ref, *refs):
    o_ref, tmp = refs[-2:]
    groups, _, lon_t, chans = x_ref.shape
    nlon = groups * lon_t
    rows = min(x_ref.shape[1], o_ref.shape[1])
    if wide_in:
        for side in range(2):
            tmp[side * groups : (side + 1) * groups] = x_ref[:, rows + side].astype(F32)
    else:
        tmp[...] = jnp.zeros_like(tmp)
    for base in range(0, rows, 4):
        span = range(base, min(base + 4, rows))
        fields = jnp.concatenate([x_ref[:, n].reshape(nlon, chans) for n in span], axis=1)
        if wide_in:
            edges = jnp.concatenate([tmp[:, n, :] for n in span], axis=1).astype(BF16)
            r = mm(a_ref[:, :nlon], fields) + mm(a_ref[:, nlon:], edges)
            r = r[:nlon] + r[nlon:]
        else:
            r = mm(a_ref[...], fields)
            size = r.shape[0] // 2
            r = r[:size] + r[size:]
        low = r[:nlon].astype(BF16)
        for n in span:
            lanes = slice((n - base) * chans, (n - base + 1) * chans)
            o_ref[:, n] = low[:, lanes].reshape(groups, lon_t, chans)
            if not wide_in:
                tmp[:, n, :] = r[nlon:, lanes]
    if not wide_in:
        for side in range(2):
            o_ref[:, rows + side] = tmp[side * groups : (side + 1) * groups].astype(BF16)


def zonal_call(fields, table, deps, wide_in):
    groups, rows, lon_t, chans = fields.shape
    out = (groups, rows - 2 if wide_in else rows + 2, lon_t, chans)
    return pl.pallas_call(
        functools.partial(zonal_kernel, wide_in),
        in_specs=[pl.BlockSpec(memory_space=pltpu.VMEM)] * 2 + [any_spec()] * len(deps),
        out_specs=pl.BlockSpec(memory_space=pltpu.VMEM),
        out_shape=shape_of(out, BF16),
        scratch_shapes=[pltpu.VMEM((2 * groups, lon_t, chans), F32)],
        compiler_params=params(),
        cost_estimate=cost(2.8),
        name="zonal",
    )(fields, table, *deps)


def synthesis_kernel(wide, info, x_ref, lo_ref, hi_ref, l_ref, *refs):
    rows_refs = refs[: 1 if wide else 2]
    own_ref, send_ref, tmp, side = refs[-4:]
    parts, rows, lon_t, chans = x_ref.shape
    each = rows - 2 if wide else rows
    deg = parts * each
    count = lon_t + 2 if wide else lon_t
    nlat = l_ref.shape[0] // 2
    half = nlat // 2
    south = info[0] == 1
    tmp[:deg, :lon_t, :] = x_ref[:, :each].reshape(deg, lon_t, chans).astype(F32)
    if wide:
        for p in range(parts):
            for e in range(2):
                tmp[p * each : (p + 1) * each, lon_t + e, :] = x_ref[p, each + e, :each].astype(F32)
    tmp[deg:] = jnp.zeros((tmp.shape[0] - deg,) + tmp.shape[1:], F32)
    side[...] = jnp.zeros_like(side)
    low, high = lo_ref[0, 0].astype(F32), hi_ref[0, 0].astype(F32)
    if wide:
        sides_ref = rows_refs[0]
        for i in range(2):
            side[i, :lon_t] = sides_ref[0, 1 - i]
        for at, edge in ((lon_t, low), (lon_t + 1, high)):
            side[0, at : at + 1] = edge[half : half + 1]
            side[1, at : at + 1] = jnp.where(south, edge[:1], edge[half - 1 : half])
    else:
        for i, ref in enumerate(rows_refs[::-1]):
            side[i, :lon_t] = ref[0, 0, :lon_t].astype(F32)
            for at, edge in ((0, low), (lon_t - 1, high)):
                side[i, at : at + 1] += edge[half + 8 * i : half + 8 * i + 1]
    for base in range(0, count, 4):
        span = range(base, min(base + 4, count))
        cols = jnp.concatenate([tmp[:, x, :] for x in span], axis=1).astype(BF16)
        r = mm(l_ref[...], cols)
        r = r[:nlat] + r[nlat:]
        for x in span:
            one = r[:, (x - base) * chans : (x - base + 1) * chans]
            own_ref[0, x] = one[:half].astype(BF16)
            send_ref[0, x] = one[half:].astype(BF16)
            if wide:
                side[0, x : x + 1] += jnp.where(south, one[2 * half - 1 :], one[half : half + 1])
                side[1, x : x + 1] += jnp.where(south, one[:1], one[half - 1 : half])
    rest = jnp.zeros((half - side.shape[1], chans), F32)
    for i, ref in enumerate((own_ref, send_ref)):
        ref[0, count] = jnp.concatenate([side[i], rest], axis=0).astype(BF16)


def synthesis_call(info, coeffs, lo, hi, table, rows_of, snaps, wide, deps):
    total, rows, lon_t, chans = coeffs.shape
    parts = total // snaps
    nlat = table.shape[0] // 2
    slabs = lon_t + 3 if wide else lon_t + 1
    out = snap_spec((slabs, nlat // 2, chans))
    message = pl.BlockSpec((1, 1) + lo.shape[2:], lambda s, info: (s, 0, 0, 0))
    if wide:
        row_specs = [snap_spec(r.shape[1:]) for r in rows_of]
    else:
        last = pl.BlockSpec((1, 1) + rows_of[0].shape[2:], lambda s, info: (s, lon_t + 2, 0, 0))
        row_specs = [last for _ in rows_of]
    return pl.pallas_call(
        functools.partial(synthesis_kernel, wide),
        grid_spec=grid_of(
            snaps,
            [
                pl.BlockSpec((parts, rows, lon_t, chans), lambda s, info: (s, 0, 0, 0)),
                message,
                message,
                whole(table.shape),
            ]
            + row_specs
            + [any_spec()] * len(deps),
            [out, out],
            [
                pltpu.VMEM((table.shape[1], lon_t + 8 if wide else lon_t, chans), F32),
                pltpu.VMEM((2, lon_t + 8, chans), F32),
            ],
        ),
        out_shape=[shape_of((snaps, slabs, nlat // 2, chans), BF16)] * 2,
        compiler_params=params(),
        cost_estimate=cost(3.6),
        name="synthesis",
    )(info, coeffs, lo, hi, table, *rows_of, *deps)


def gelu_of(x):
    t = jnp.tanh(x * (GELU_A + (GELU_A * GELU_B) * (x * x)))
    return 0.5 * x * (1.0 + t)


def gelu_and_slope(x):
    sq = x * x
    t = jnp.tanh(x * (GELU_A + (GELU_A * GELU_B) * sq))
    cdf = 0.5 + 0.5 * t
    slope = cdf + (0.5 * x) * (1.0 - t * t) * (GELU_A + (3.0 * GELU_A * GELU_B) * sq)
    return x * cdf, slope


def fill_patches(patches, slabs, ends, masks):
    lat_t, chans = slabs[0].shape
    lon_t = len(slabs) - 2
    place = lax.broadcasted_iota(jnp.int32, (lat_t, chans), 0)
    for i in range(lon_t + 2):
        low_row, high_row = ends[i] * masks[0:1], ends[i] * masks[1:2]
        down = jnp.where(place == 0, low_row, pltpu.roll(slabs[i], 1, 0)).astype(BF16)
        up = jnp.where(place == lat_t - 1, high_row, pltpu.roll(slabs[i], lat_t - 1, 0)).astype(BF16)
        mid = slabs[i].astype(BF16)
        for a in range(3):
            x = i - a
            if 0 <= x < lon_t:
                for b, piece in enumerate((down, mid, up)):
                    k = 3 * a + b
                    patches[x * lat_t : (x + 1) * lat_t, k * chans : (k + 1) * chans] = piece


def assemble(patches, field_refs, moved):
    state_ref, s_ref, lo_ref, hi_ref, extra_ref, masks_ref = field_refs
    lon_t, lat_t, chans = moved.shape
    moved[...] = state_ref[0].astype(F32) + s_ref[0, :lon_t].astype(F32)
    rows = s_ref[0, lon_t + 2].astype(F32)
    slabs = [lo_ref[0, 0, :lat_t].astype(F32) + s_ref[0, lon_t].astype(F32)]
    slabs += [moved[i] for i in range(lon_t)]
    slabs += [hi_ref[0, 0, :lat_t].astype(F32) + s_ref[0, lon_t + 1].astype(F32)]
    ends = [rows[i : i + 1] for i in [lon_t] + list(range(lon_t)) + [lon_t + 1]]
    fill_patches(patches, slabs, ends, masks_ref[...])
    patches[:, 9 * chans :] = extra_ref[0]


def forward_kernel(info, *refs):
    field_refs, (w1_ref, mid_ref, dec_ref, bias_ref) = refs[:6], refs[6:10]
    state_out, low_out, pre1_out, pre2_out, patches, moved = refs[-6:]
    lon_t, lat_t, chans = moved.shape
    hid = mid_ref.shape[0]
    assemble(patches, field_refs, moved)
    pre1 = mm(patches[...], w1_ref[...])
    pre1_out[0] = pre1
    active1 = gelu_of(pre1).astype(BF16)
    pre2 = mm(active1, mid_ref[...]) + bias_ref[0:1, :hid]
    pre2_out[0] = pre2
    active2 = gelu_of(pre2).astype(BF16)
    out = mm(active2, dec_ref[...]) + bias_ref[1:2, :chans]
    state_out[0] = moved[...] + out.reshape(lon_t, lat_t, chans)
    low_out[0] = state_out[0].astype(BF16)


GRAD_PAD = 128


def grad_layout(chans, hid):
    one, two, three = 9 * chans, 9 * chans + hid, 9 * chans + hid + chans
    return (one, two, three, -(-(three + 8) // GRAD_PAD) * GRAD_PAD)


def add_grads(first, out, before, patches, active1, active2, g_out, g_pre2, g_pre1, ends):
    chans, hid = g_out.shape[1], g_pre1.shape[1]
    one, two, three, _ = grad_layout(chans, hid)
    enc = mm_rows(patches[...], g_pre1[...])
    pieces = [
        (0, one, enc[:one]),
        (one, two, mm_rows(active1[...], g_pre2[...])),
        (two, three, mm_rows(g_out[...], active2[...])),
    ]

    @pl.when(first)
    def _():
        ends[...] = enc[one : one + 8]
        for start, stop, piece in pieces:
            out[start:stop] = piece if before is None else before[start:stop] + piece

    @pl.when(jnp.logical_not(first))
    def _():
        ends[...] += enc[one : one + 8]
        for start, stop, piece in pieces:
            out[start:stop] += piece


def pack_grads(out, before, chans, hid, ends, vecs):
    _, _, three, rows = grad_layout(chans, hid)
    tail = jnp.concatenate([vecs[2:3, :chans], vecs[1:2, :chans]], axis=1)
    out[three:] = jnp.zeros((rows - three, hid), F32)
    for row, piece in enumerate((ends[3:4], ends[0:1], vecs[0:1], tail, vecs[3:4])):
        at = slice(three + row, three + row + 1)
        out[at] = piece if before is None else before[at] + piece


def turn_kernel(more, info, *refs):
    field_refs, (w1_ref, mid_ref, dec_ref, bias_ref) = refs[:6], refs[6:10]
    extra_ref, masks_ref = field_refs[4:]
    target_ref, area_ref, w1t_ref, midt_ref, dect_ref = refs[10:15]
    before = refs[15] if more else None
    (
        gm_out, low_out, grads_out,
        patches, moved, active1, active2, slope1, slope2, g_out, g_pre2, g_pre1, spread,
        ends, vecs, side,
    ) = refs[-16:]
    lon_t, lat_t, chans = moved.shape
    hid = mid_ref.shape[0]
    first = pl.program_id(0) == 0
    assemble(patches, field_refs, moved)
    spread[...] = jnp.zeros_like(spread)

    @pl.when(first)
    def _():
        vecs[...] = jnp.zeros_like(vecs)
        side[...] = jnp.zeros_like(side)

    step = 16
    for x in range(0, lon_t, step):
        rows = slice(x * lat_t, (x + step) * lat_t)
        pre1 = mm(patches[rows], w1_ref[...])
        a1, d1 = gelu_and_slope(pre1)
        active1[rows] = a1.astype(BF16)
        slope1[rows] = d1
        pre2 = mm(active1[rows], mid_ref[...]) + bias_ref[0:1, :hid]
        a2, d2 = gelu_and_slope(pre2)
        active2[rows] = a2.astype(BF16)
        slope2[rows] = d2
        out = mm(active2[rows], dec_ref[...]) + bias_ref[1:2, :chans]
        fresh = moved[x : x + step] + out.reshape(step, lat_t, chans)
        diff = fresh - target_ref[0, x : x + step].astype(F32)
        valid = jnp.broadcast_to(extra_ref[0, rows, 6:7].astype(F32), (step * lat_t, chans))
        weight = valid.reshape(step, lat_t, chans) * area_ref[...][None]
        vecs[3:4, :chans] += jnp.sum(weight.reshape(step * lat_t, chans), 0, keepdims=True)
        weighted = weight * diff
        vecs[1:2, :chans] += jnp.sum((weighted * diff).reshape(step * lat_t, chans), 0, keepdims=True)
        grad = 2.0 * weighted
        moved[x : x + step] = grad
        low = grad.reshape(step * lat_t, chans).astype(BF16)
        g_out[rows] = low
        vecs[2:3, :chans] += jnp.sum(low.astype(F32), 0, keepdims=True)
        gp2 = (mm(low, dect_ref[...]) * slope2[rows]).astype(BF16)
        g_pre2[rows] = gp2
        vecs[0:1] += jnp.sum(gp2.astype(F32), 0, keepdims=True)
        gp1 = (mm(gp2, midt_ref[...]) * slope1[rows]).astype(BF16)
        g_pre1[rows] = gp1
        taps = mm(gp1, w1t_ref[...])
        for a in range(3):
            for b in range(3):
                k = 3 * a + b
                spread[b, x + a : x + a + step] += taps[:, k * chans : (k + 1) * chans].reshape(
                    step, lat_t, chans
                )
    place = lax.broadcasted_iota(jnp.int32, (lat_t, chans), 0)
    masks = masks_ref[...]
    for i in range(lon_t + 2):
        down, here, up = spread[0, i], spread[1, i], spread[2, i]
        got = here + jnp.where(place == lat_t - 1, 0.0, pltpu.roll(down, lat_t - 1, 0))
        got = got + jnp.where(place == 0, 0.0, pltpu.roll(up, 1, 0))
        beyond = down[0:1] * masks[0:1] + up[lat_t - 1 : lat_t] * masks[1:2]
        if i in (0, lon_t + 1):
            at = lon_t if i == 0 else lon_t + 1
            low_out[0, at] = got.astype(BF16)
        else:
            at = i - 1
            total = got + moved[at]
            gm_out[0, at] = total
            low_out[0, at] = total.astype(BF16)
        side[at : at + 1] = beyond
    rest = jnp.zeros((lat_t - side.shape[0], chans), F32)
    low_out[0, lon_t + 2] = jnp.concatenate([side[...], rest], axis=0).astype(BF16)
    add_grads(first, grads_out, before, patches, active1, active2, g_out, g_pre2, g_pre1, ends)

    @pl.when(pl.program_id(0) == pl.num_programs(0) - 1)
    def _():
        pack_grads(grads_out, before, chans, hid, ends, vecs)


def bottom_kernel(more, info, *refs):
    field_refs = refs[:6]
    pre1_ref, pre2_ref, gm_ref, glo_ref, ghi_ref, gs_ref, midt_ref, dect_ref = refs[6:14]
    before = refs[14] if more else None
    (
        grads_out, patches, moved, active1, active2, g_out, g_pre2, g_pre1, ends, vecs,
    ) = refs[-10:]
    lon_t, lat_t, chans = moved.shape
    hid = midt_ref.shape[0]
    first = pl.program_id(0) == 0
    assemble(patches, field_refs, moved)

    moved[...] = gm_ref[0] + gs_ref[0, :lon_t].astype(F32)
    moved[0] += glo_ref[0, 0, :lat_t].astype(F32)
    moved[lon_t - 1] += ghi_ref[0, 0, :lat_t].astype(F32)
    place = lax.broadcasted_iota(jnp.int32, (lat_t, chans), 0)
    inner = place == jnp.where(info[0] == 1, 0, lat_t - 1)
    for x in range(lon_t):
        moved[x] += jnp.where(inner, gs_ref[0, lon_t, x : x + 1].astype(F32), 0.0)

    @pl.when(first)
    def _():
        vecs[...] = jnp.zeros_like(vecs)

    step = 8
    for x in range(0, lon_t, step):
        rows = slice(x * lat_t, (x + step) * lat_t)
        a1, d1 = gelu_and_slope(pre1_ref[0, rows])
        active1[rows] = a1.astype(BF16)
        a2, d2 = gelu_and_slope(pre2_ref[0, rows])
        active2[rows] = a2.astype(BF16)
        low = moved[x : x + step].reshape(step * lat_t, chans).astype(BF16)
        g_out[rows] = low
        vecs[2:3, :chans] += jnp.sum(low.astype(F32), 0, keepdims=True)
        gp2 = (mm(low, dect_ref[...]) * d2).astype(BF16)
        g_pre2[rows] = gp2
        vecs[0:1] += jnp.sum(gp2.astype(F32), 0, keepdims=True)
        g_pre1[rows] = (mm(gp2, midt_ref[...]) * d1).astype(BF16)
    add_grads(first, grads_out, before, patches, active1, active2, g_out, g_pre2, g_pre1, ends)

    @pl.when(pl.program_id(0) == pl.num_programs(0) - 1)
    def _():
        pack_grads(grads_out, before, chans, hid, ends, vecs)


def message_spec(dims, late):
    return pl.BlockSpec((1, 1) + dims, lambda g, info: (g, late, 0, 0))


def field_specs(field, chunk, half, late, pool_state):
    state, s_ext, lo, hi, extra, masks = field
    return [
        snap_spec(state.shape[1:], chunk if pool_state else None, half),
        snap_spec(s_ext.shape[1:]),
        message_spec(lo.shape[2:], late),
        message_spec(hi.shape[2:], late),
        snap_spec(extra.shape[1:], chunk, half),
        whole(masks.shape),
    ]


def cost(micros):
    return pl.CostEstimate(flops=int(micros * 3e10), bytes_accessed=int(micros * 1e8), transcendentals=0)


def forward_call(info, chunk, half, late, field, weights, deps):
    dims = field[0].shape[1:]
    lon_t, lat_t, chans = dims
    cells = lon_t * lat_t
    hid = weights["mid"].shape[0]
    ws = [weights[k] for k in ("w1", "mid", "dec", "bias")]
    outs = [(dims, F32), (dims, BF16), ((cells, hid), F32), ((cells, hid), F32)]
    return pl.pallas_call(
        forward_kernel,
        grid_spec=grid_of(
            HALF,
            field_specs(field, chunk, half, late, True) + [whole(w.shape) for w in ws] + [any_spec()] * len(deps),
            [snap_spec(d) for d, _ in outs],
            [pltpu.VMEM((cells, 10 * chans), BF16), pltpu.VMEM(dims, F32)],
        ),
        out_shape=[shape_of((HALF,) + d, t) for d, t in outs],
        compiler_params=params(),
        cost_estimate=cost(6.5),
        name="forward",
    )(info, *field, *ws, *deps)


def back_scratch(dims, hid):
    lon_t, lat_t, chans = dims
    cells = lon_t * lat_t
    return [
        pltpu.VMEM((cells, chans), BF16),
        pltpu.VMEM((cells, hid), BF16),
        pltpu.VMEM((cells, hid), BF16),
    ], [
        pltpu.VMEM((8, hid), F32),
        pltpu.VMEM((8, hid), F32),
    ]


def turn_call(info, chunk, half, late, field, weights, targets, area, deps, before):
    dims = field[0].shape[1:]
    lon_t, lat_t, chans = dims
    cells = lon_t * lat_t
    hid = weights["mid"].shape[0]
    ws = [weights[k] for k in ("w1", "mid", "dec", "bias")]
    wt = [weights[k] for k in ("w1t", "midt", "dect")]
    grad_rows = grad_layout(chans, hid)[-1]
    more = before is not None
    last = [before] if more else []
    outs = [(dims, F32), ((lon_t + 3, lat_t, chans), BF16)]
    grads, sums = back_scratch(dims, hid)
    return pl.pallas_call(
        functools.partial(turn_kernel, more),
        grid_spec=grid_of(
            HALF,
            field_specs(field, chunk, half, late, False)
            + [whole(w.shape) for w in ws]
            + [snap_spec(dims, chunk, half), whole(area.shape)]
            + [whole(w.shape) for w in wt + last]
            + [any_spec()] * len(deps),
            [snap_spec(d) for d, _ in outs] + [whole((grad_rows, hid))],
            [
                pltpu.VMEM((cells, 10 * chans), BF16),
                pltpu.VMEM(dims, F32),
                pltpu.VMEM((cells, hid), BF16),
                pltpu.VMEM((cells, hid), BF16),
                pltpu.VMEM((cells, hid), F32),
                pltpu.VMEM((cells, hid), F32),
            ]
            + grads
            + [pltpu.VMEM((3, lon_t + 2, lat_t, chans), F32)]
            + sums
            + [pltpu.VMEM((lon_t + 8, chans), F32)],
        ),
        out_shape=[shape_of((HALF,) + d, t) for d, t in outs] + [shape_of((grad_rows, hid), F32)],
        compiler_params=params(),
        cost_estimate=cost(13.0),
        name="turn",
    )(info, *field, *ws, targets, area, *wt, *last, *deps)


def bottom_call(info, chunk, half, late, field, weights, pre, gm, glo, ghi, glate, gs, deps, before):
    dims = field[0].shape[1:]
    lon_t, lat_t, chans = dims
    cells = lon_t * lat_t
    hid = weights["mid"].shape[0]
    wt = [weights[k] for k in ("midt", "dect")]
    grad_rows = grad_layout(chans, hid)[-1]
    more = before is not None
    last = [before] if more else []
    grads, sums = back_scratch(dims, hid)
    return pl.pallas_call(
        functools.partial(bottom_kernel, more),
        grid_spec=grid_of(
            HALF,
            field_specs(field, chunk, half, late, True)
            + [snap_spec(v.shape[1:]) for v in (*pre, gm)]
            + [message_spec(glo.shape[2:], glate)] * 2
            + [snap_spec(gs.shape[1:])]
            + [whole(w.shape) for w in wt + last]
            + [any_spec()] * len(deps),
            whole((grad_rows, hid)),
            [
                pltpu.VMEM((cells, 10 * chans), BF16),
                pltpu.VMEM(dims, F32),
                pltpu.VMEM((cells, hid), BF16),
                pltpu.VMEM((cells, hid), BF16),
            ]
            + grads
            + sums,
        ),
        out_shape=shape_of((grad_rows, hid), F32),
        compiler_params=params(),
        cost_estimate=cost(8.0),
        name="bottom",
    )(info, *field, *pre, gm, glo, ghi, gs, *wt, *last, *deps)


def three_parts(vec):
    high = lax.reduce_precision(vec, 8, 7)
    rest = vec - high
    mid = lax.reduce_precision(rest, 8, 7)
    low = lax.reduce_precision(rest - mid, 8, 7)
    return jnp.stack([high, mid, low], axis=-2)


def layer_weights(enc, mid, dec, vec):
    taps, chans, hid = enc.shape
    parts = jnp.concatenate([three_parts(vec[hid : 2 * hid]), three_parts(vec[:hid])], axis=0)
    parts = jnp.pad(parts, ((0, chans - 6), (0, 0)))
    w1 = jnp.concatenate([enc.reshape(taps * chans, hid), parts], axis=0).astype(BF16)
    pad = jnp.zeros((hid - chans,), F32)
    bias = jnp.stack([vec[2 * hid : 3 * hid], jnp.concatenate([vec[3 * hid :], pad])])
    return {
        "w1": w1,
        "mid": mid.astype(BF16),
        "dec": dec.astype(BF16),
        "bias": bias,
        "w1t": jnp.transpose(enc, (2, 0, 1)).reshape(hid, taps * chans).astype(BF16),
        "midt": mid.T.astype(BF16),
        "dect": dec.T.astype(BF16),
    }


def reduce_steps(part, order):
    lon_n = lax.axis_size("lon")
    me = lax.axis_index("lon")

    def over(stride):
        return "lon", (me // stride) % 2, [(i, i ^ stride) for i in range(lon_n)]

    links = {"core": over(1), "x": over(2), "y": ("lat", lax.axis_index("lat"), [(0, 1), (1, 0)]), "z": over(8)}
    stages = [links[name] for name in order]

    def after(x, hold):
        return x if hold is None else lax.optimization_barrier((x, hold))[0]

    hold = None
    for axis, bit, perm in stages:
        half = part.shape[0] // 2
        give = lax.dynamic_slice_in_dim(part, (1 - bit) * half, half)
        mine = lax.dynamic_slice_in_dim(part, bit * half, half)
        part = after(mine, hold) + lax.ppermute(give, axis, perm)
        hold = yield part
    axis, _, perm = over(4)
    part = after(part, hold) + lax.ppermute(part, axis, perm)
    hold = yield part
    for axis, bit, perm in reversed(stages):
        got = lax.ppermute(part, axis, perm)
        part = after(part, hold)
        part = jnp.concatenate([jnp.where(bit == 0, part, got), jnp.where(bit == 0, got, part)])
        hold = yield part


def fast_grads(states, targets, sea_temp, ocean, valid, w_enc, w_mid, w_dec, biases):
    pool, lon_t, lat_t, chans = states.shape
    lon_n, lat_n = lax.axis_size("lon"), lax.axis_size("lat")
    nlon, nlat = lon_t * lon_n, lat_t * lat_n
    zonal, forward, inverse, area_all = host_tables(nlon, nlat, 88)
    hemi = lax.axis_index("lat")
    info = hemi[None].astype(jnp.int32)
    flip = np.concatenate([np.arange(lat_t, nlat), np.arange(lat_t)])
    flip2 = np.concatenate([flip, nlat + flip])
    ends = (np.arange(0, nlon, lon_t)[None, :] + np.array([[-1], [lon_t]])).reshape(-1) % nlon
    zonal_in = jnp.asarray(np.concatenate([zonal, zonal[:, ends]], axis=1))
    zonal_out = jnp.asarray(
        np.concatenate([zonal[:nlon], zonal[:nlon][ends], zonal[nlon:], zonal[nlon:][ends]], axis=0)
    )
    forward = jnp.where(hemi == 0, jnp.asarray(forward), jnp.asarray(forward[:, flip]))
    inverse = jnp.where(hemi == 0, jnp.asarray(inverse), jnp.asarray(inverse[flip2]))
    side = jnp.stack([hemi == 1, hemi == 0]).astype(F32)
    masks = jnp.broadcast_to(side[:, None], (2, chans))
    area = lax.dynamic_slice_in_dim(jnp.asarray(area_all, F32), hemi * lat_t, lat_t)
    area_wide = jnp.broadcast_to(area[:, None], (lat_t, chans))
    up = [(i, (i + 1) % lon_n) for i in range(lon_n)]
    down = [(t, s) for s, t in up]
    swap = [(0, 1), (1, 0)]
    chunks = range(pool // CHUNK)

    first_traded = lax.ppermute(pick_call(info, states, 0, 1, []), "lat", swap)
    held = lax.optimization_barrier((first_traded, w_enc, w_mid, w_dec, biases))
    _, w_enc, w_mid, w_dec, biases = held
    layers = [layer_weights(w_enc[i], w_mid[i], w_dec[i], biases[i]) for i in range(2)]

    last = [forward]

    def then(result, pick=None):
        last[:] = [result if pick is None else result[pick]]
        return result

    def over_lon(spec):
        return lax.all_to_all(spec, "lon", split_axis=0, concat_axis=0, tiled=True)

    class Chunk:
        def __init__(self, c):
            self.c = c
            self.early = 0
            self.round = 0
            self.other = first_traded
            self.field0, self.pres = [None, None], [None, None]
            self.fresh, self.low, self.s_ext, self.gm = ([None, None] for _ in range(4))

        def legendre(self):
            half = self.early
            own, late = (states, states) if self.round == 0 else (self.low[half], self.low[1 - half])
            there = self.c if self.round == 0 else None
            wide = self.round == 2
            got = legendre_call(info, own, late, there, half, self.other, forward, last, wide)
            spec, to_up, to_down, sides = then(got, 0)
            self.spec = over_lon(spec)
            self.lo, self.hi = lax.ppermute(to_up, "lon", up), lax.ppermute(to_down, "lon", down)
            self.rows_of = (own, self.other) if wide else (sides,)

        def zonal(self):
            table = zonal_in if self.round == 2 else zonal_out
            self.spec = over_lon(then(zonal_call(self.spec, table, last, self.round == 2)))

        def synthesis(self):
            got = synthesis_call(
                info, self.spec, self.lo, self.hi, inverse, self.rows_of, HALF, self.round < 2, last
            )
            own, send = then(got, 0)
            self.s_ext[self.early] = own
            self.s_ext[1 - self.early] = lax.ppermute(send, "lat", swap)

        def forward(self, late):
            half = self.early ^ late
            field = (states, self.s_ext[half], self.lo, self.hi, extra, masks)
            self.field0[half] = field
            got = forward_call(info, self.c, half, late, field, layers[0], last)
            self.fresh[half], self.low[half], *pre = then(got, 1)
            self.pres[half] = pre
            self.send(half, late)

        def turn(self, late, before):
            half = self.early ^ late
            field = (self.fresh[half], self.s_ext[half], self.lo, self.hi, extra, masks)
            got = turn_call(
                info, self.c, half, late, field, layers[1], targets, area_wide, last, before
            )
            self.gm[half], self.low[half], before = then(got, 1)
            self.send(half, late)
            return before

        def send(self, half, late):
            if not late:
                self.other = lax.ppermute(self.low[half], "lat", swap)

        def flip(self):
            self.early = 1 - self.early
            self.round += 1

        def bottom(self, late, before):
            half = self.early ^ late
            got = bottom_call(
                info, self.c, half, late, self.field0[half], layers[0], self.pres[half],
                self.gm[half], self.lo, self.hi, late, self.s_ext[half], last, before,
            )
            return then(got)

    a, b = (Chunk(c) for c in chunks)
    top, low = None, None
    a.legendre()
    b.other = lax.ppermute(then(pick_call(info, states, 1, 1, last)), "lat", swap)
    a.zonal()
    _, ocean, sea_temp, valid = lax.optimization_barrier((last[0], ocean, sea_temp, valid))
    sea = ocean.astype(F32) * sea_temp.astype(F32)
    cells = lon_t * lat_t
    lane = jnp.arange(chans)
    wide_sea = sea.reshape(pool, cells, 1).astype(BF16)
    wide_valid = valid.reshape(pool, cells, 1).astype(BF16)
    extra = jnp.where(lane < 3, wide_sea, jnp.where(lane < 6, jnp.ones((), BF16), wide_valid))
    extra = jnp.where(lane < 7, extra, jnp.zeros((), BF16))
    b.legendre()
    for one, two in ((a, b), (b, a)):
        one.synthesis()
        one.forward(0)
        two.zonal()
        one.forward(1)
        one.flip()
        one.legendre()
    for one, two in ((a, b), (b, a)):
        one.synthesis()
        top = one.turn(0, top)
        two.zonal()
        top = one.turn(1, top)
        one.flip()
        one.legendre()
    a.synthesis()
    top, _ = lax.optimization_barrier((top, last[0]))
    upper = reduce_steps(top, ("core", "y", "x", "z"))
    low = a.bottom(0, low)
    b.zonal()
    last.append(next(upper))
    low = a.bottom(1, low)
    last.append(next(upper))
    b.synthesis()
    last.append(next(upper))
    low = b.bottom(0, low)
    last.append(next(upper))
    low = b.bottom(1, low)
    lower = reduce_steps(low, ("core", "x", "y", "z"))
    *_, high = upper
    *_, low = lower
    return low, high


def update_kernel(rate, taps_each, info, g0_ref, g1_ref, m0_ref, m1_ref, v0_ref, v1_ref, *refs):
    ins, outs = refs[:12], refs[12:]
    layer, part = pl.program_id(0), pl.program_id(1)
    chans, hid = ins[0].shape[2:]
    scale = 1.0 / v1_ref[4:5, 0:1]

    def apply(group, at, grad):
        w_ref, m_ref, a_ref = (ins[4 * i + group] for i in range(3))
        new_ref, mom_ref, avg_ref, copy_ref = (outs[4 * i + group] for i in range(4))
        scaled = grad * scale
        mom = MOMENTUM * m_ref[at] + scaled
        fresh = w_ref[at] - rate * (scaled + MOMENTUM * mom)
        new_ref[at] = fresh
        mom_ref[at] = mom
        avg_ref[at] = AVERAGE * a_ref[at] + (1.0 - AVERAGE) * fresh
        copy_ref[at] = fresh.astype(BF16)

    def layer_step(g_ref, m_ref):
        for tap in range(taps_each):
            apply(0, (0, tap), g_ref[tap * chans : (tap + 1) * chans])

        @pl.when(part == 0)
        def _():
            apply(1, (0,), m_ref[:hid])
            apply(2, (0,), m_ref[hid:].T)

    pl.when(layer == 0)(lambda: layer_step(g0_ref, m0_ref))
    pl.when(layer == 1)(lambda: layer_step(g1_ref, m1_ref))

    @pl.when((layer == 0) & (part == 0))
    def _():
        for i, v_ref in enumerate((v0_ref, v1_ref)):
            for r in range(4):
                wide = hid if r < 3 else chans
                at = (slice(i, i + 1), slice(r * hid, r * hid + wide))
                apply(3, at, v_ref[r : r + 1, :wide])


TAPS_EACH = 9


def update_call(rate, sums, arrays):
    w_enc, w_mid, w_dec, biases = arrays[:4]
    layers, taps, chans, hid = w_enc.shape
    one, _, three, _ = grad_layout(chans, hid)
    steps = taps // TAPS_EACH
    rows = TAPS_EACH * chans
    enc = pl.BlockSpec((1, TAPS_EACH, chans, hid), lambda i, p, info: (i, p, 0, 0))
    mid = pl.BlockSpec((1, hid, hid), lambda i, p, info: (i, 0, 0))
    dec = pl.BlockSpec((1, hid, chans), lambda i, p, info: (i, 0, 0))
    bias = whole(biases.shape)
    specs = [enc, mid, dec, bias]
    shapes = [w_enc.shape, w_mid.shape, w_dec.shape, biases.shape]
    grads = [
        pl.BlockSpec((rows, hid), lambda i, p, info: (jnp.where(i == 0, p, steps - 1), 0)),
        pl.BlockSpec((rows, hid), lambda i, p, info: (jnp.where(i == 0, 0, p), 0)),
        pl.BlockSpec((three - one, hid), lambda i, p, info: (one // (three - one), 0)),
        pl.BlockSpec((three - one, hid), lambda i, p, info: (one // (three - one), 0)),
        pl.BlockSpec((8, hid), lambda i, p, info: (three // 8, 0)),
        pl.BlockSpec((8, hid), lambda i, p, info: (three // 8, 0)),
    ]
    got = pl.pallas_call(
        functools.partial(update_kernel, rate, TAPS_EACH),
        grid_spec=pltpu.PrefetchScalarGridSpec(
            num_scalar_prefetch=1,
            grid=(layers, steps),
            in_specs=grads + specs * 3,
            out_specs=specs * 4,
        ),
        out_shape=[shape_of(s, F32) for s in shapes * 3] + [shape_of(s, BF16) for s in shapes],
        compiler_params=params(),
        cost_estimate=cost(8.0),
        name="update",
    )(jnp.zeros((1,), jnp.int32), sums[0], sums[1], sums[0], sums[1], sums[0], sums[1], *arrays)
    vecs = sums[1][three : three + 8]
    return (jnp.sum(vecs[3, chans:]), vecs[4, 0], *got)


def fits(states, w_mid, lon_n, lat_n):
    pool, lon_t, lat_t, chans = states.shape
    return (
        lat_n == 2
        and lon_n == 16
        and lon_t == 16
        and lat_t == 64
        and pool == 2 * CHUNK
        and chans == 128
        and w_mid.shape[1] == 2 * chans
        and w_mid.shape[0] == 2
    )


def with_halo(block, sides, width, periodic):
    for axis, dim in sides:
        count = lax.axis_size(axis)
        forward = [(i, i + 1) for i in range(count - 1)]
        if periodic:
            forward.append((count - 1, 0))
        backward = [(target, source) for source, target in forward]
        low = lax.ppermute(
            lax.slice_in_dim(block, block.shape[dim] - width, None, axis=dim), axis, forward
        )
        high = lax.ppermute(lax.slice_in_dim(block, 0, width, axis=dim), axis, backward)
        block = jnp.concatenate([low, block, high], axis=dim)
    return block


def tables(nlon, nlat, groups):
    coeffs = jnp.arange(2 * MW)
    wave = jnp.where(coeffs < MW, coeffs, coeffs - MW + 1).astype(jnp.float32)
    places = jnp.arange(nlon).astype(jnp.float32)
    angle = 2.0 * math.pi * wave[:, None] * places[None, :] / nlon
    fourier = jnp.where((coeffs < MW)[:, None], jnp.cos(angle), jnp.sin(angle)) * math.sqrt(
        2.0 / nlon
    )
    phase = ((jnp.arange(nlat).astype(jnp.float32) + 0.5) / nlat - 0.5) * math.pi
    sine = jnp.sin(phase)
    quad = jnp.cos(phase) * math.pi / nlat
    polys = [jnp.ones_like(sine), sine]
    for degree in range(1, NDEG - 1):
        polys.append(((2 * degree + 1) * sine * polys[-1] - degree * polys[-2]) / (degree + 1))
    stacked = jnp.stack(polys[:NDEG])
    degrees = jnp.arange(NDEG).astype(jnp.float32)
    legendre = jnp.sqrt((2 * degrees + 1) / 2)[:, None] * jnp.sqrt(quad)[None, :] * stacked
    damping = 1.5 * (1.0 - 2.0 * degrees * (degrees + 1) / (NDEG * (NDEG + 1)))
    filters = damping[None, :] * (1.0 - 0.5 * wave / MW)[:, None]
    kept = 2 * MW
    slots = (kept + groups - 1) // groups * groups
    fourier = jnp.pad(fourier, ((0, slots - kept), (0, 0)))
    filters = jnp.pad(filters, ((0, slots - kept), (0, 0)))
    return (fourier, legendre, filters)


def spectral(values, tabs):
    fourier, legendre, filters = tabs
    cycles = lax.all_to_all(
        values.astype(jnp.bfloat16), "lon", split_axis=3, concat_axis=1, tiled=True
    ).astype(values.dtype)
    coeff = jnp.einsum("kx,sxjc->skjc", fourier, cycles, precision=HIGH)
    block = fourier.shape[0] // lax.axis_size("lat")
    where = lax.axis_index("lat")
    block_filter = lax.dynamic_slice_in_dim(filters, where * block, block, 0)
    columns = lax.all_to_all(
        coeff.astype(jnp.bfloat16), "lat", split_axis=1, concat_axis=2, tiled=True
    ).astype(coeff.dtype)
    spec = (
        jnp.einsum("nj,skjc->sknc", legendre, columns, precision=HIGH)
        * block_filter[None, :, :, None]
    )
    back = jnp.einsum("nj,sknc->skjc", legendre, spec, precision=HIGH)
    coeff_back = lax.all_to_all(
        back.astype(jnp.bfloat16), "lat", split_axis=2, concat_axis=1, tiled=True
    ).astype(back.dtype)
    grid = jnp.einsum("kx,skjc->sxjc", fourier, coeff_back, precision=HIGH)
    return lax.all_to_all(
        grid.astype(jnp.bfloat16), "lon", split_axis=1, concat_axis=3, tiled=True
    ).astype(grid.dtype)


def extend(field):
    wider = with_halo(field, (("lon", 1),), 1, True)
    return with_halo(wider, (("lat", 2),), 1, False)


def neighbours(padded, flipped, lon_t, lat_t):
    parts = []
    for row_off in range(3):
        for col_off in range(3):
            first = 2 - row_off if flipped else row_off
            second = 2 - col_off if flipped else col_off
            parts.append(padded[:, first : first + lon_t, second : second + lat_t])
    stacked = jnp.stack(parts, axis=3)
    return stacked.reshape(-1, 9 * padded.shape[-1])


def gelu_fn(value):
    return jax.nn.gelu(value, approximate=True)


def gelu_back(value, grad):
    return jax.vjp(gelu_fn, value)[1](grad)[0]


def layer_forward(state, sea, enc, mid, dec, vec, tabs):
    hid = mid.shape[0]
    lon_t, lat_t = (state.shape[1], state.shape[2])
    moved = state + spectral(state, tabs)
    patches = neighbours(extend(moved.astype(jnp.bfloat16)), False, lon_t, lat_t)
    pre1 = jnp.dot(patches, enc, preferred_element_type=jnp.float32)
    pre1 = pre1 + sea.reshape(-1, 1) * vec[hid : 2 * hid] + vec[:hid]
    active1 = gelu_fn(pre1).astype(jnp.bfloat16)
    pre2 = jnp.dot(active1, mid, preferred_element_type=jnp.float32) + vec[2 * hid : 3 * hid]
    active2 = gelu_fn(pre2).astype(jnp.bfloat16)
    output = jnp.dot(active2, dec, preferred_element_type=jnp.float32) + vec[3 * hid :]
    return (moved + output.reshape(state.shape), (patches, pre1, active1, pre2, active2))


def layer_backward(grad_state, sea, enc, mid, dec, saved, tabs):
    patches, pre1, active1, pre2, active2 = saved
    hid = mid.shape[0]
    shape = grad_state.shape
    chans = shape[-1]
    g_out = grad_state.reshape(-1, chans).astype(jnp.bfloat16)
    g_dec = jnp.einsum("rh,rc->hc", active2, g_out, preferred_element_type=jnp.float32)
    g_act2 = jnp.einsum("rc,hc->rh", g_out, dec, preferred_element_type=jnp.float32)
    g_pre2 = gelu_back(pre2, g_act2).astype(jnp.bfloat16)
    g_mid = jnp.einsum("rh,rg->hg", active1, g_pre2, preferred_element_type=jnp.float32)
    g_act1 = jnp.einsum("rg,hg->rh", g_pre2, mid, preferred_element_type=jnp.float32)
    g_pre1 = gelu_back(pre1, g_act1).astype(jnp.bfloat16)
    g_enc = jnp.einsum("rk,rh->kh", patches, g_pre1, preferred_element_type=jnp.float32)
    wide1 = g_pre1.astype(jnp.float32)
    g_vec = jnp.concatenate(
        [
            jnp.sum(wide1, 0),
            jnp.sum(sea.reshape(-1, 1) * wide1, 0),
            jnp.sum(g_pre2.astype(jnp.float32), 0),
            jnp.sum(g_out.astype(jnp.float32), 0),
        ]
    )
    spread = extend(g_pre1.reshape(shape[0], shape[1], shape[2], hid))
    gathered = neighbours(spread, True, shape[1], shape[2]).reshape(-1, 9, hid)
    g_input = jnp.einsum(
        "rkh,kch->rc", gathered, enc.reshape(9, chans, hid), preferred_element_type=jnp.float32
    )
    grad_moved = grad_state + g_input.reshape(shape)
    return (grad_moved + spectral(grad_moved, tabs), (g_enc, g_mid, g_dec, g_vec))


def general_grads(states, targets, sea_temp, ocean, valid, order, w_enc, w_mid, w_dec, biases):
    pool, lon_t, lat_t, chans = states.shape
    layers, hid = (w_mid.shape[0], w_mid.shape[1])
    nlon = lon_t * lax.axis_size("lon")
    nlat = lat_t * lax.axis_size("lat")
    tabs = tables(nlon, nlat, lax.axis_size("lat"))
    lat_glob = (lax.axis_index("lat") * lat_t + jnp.arange(lat_t)).astype(jnp.float32)
    area = jnp.cos(((lat_glob + 0.5) / nlat - 0.5) * math.pi)
    enc_low = w_enc.astype(jnp.bfloat16).reshape(layers, 9 * chans, hid)
    mid_low = w_mid.astype(jnp.bfloat16)
    dec_low = w_dec.astype(jnp.bfloat16)
    snaps = pool // MB
    sums = [
        jnp.zeros((layers, 9 * chans, hid), jnp.float32),
        jnp.zeros_like(w_mid),
        jnp.zeros_like(w_dec),
        jnp.zeros_like(biases),
    ]
    loss = jnp.zeros((), jnp.float32)
    total = jnp.zeros((), jnp.float32)
    for batch_id in range(MB):
        picks = lax.dynamic_slice_in_dim(order, batch_id * snaps, snaps)
        state = jnp.take(states, picks, axis=0).astype(jnp.float32)
        target = jnp.take(targets, picks, axis=0).astype(jnp.float32)
        sea = jnp.take(ocean, picks, axis=0).astype(jnp.float32) * jnp.take(
            sea_temp, picks, axis=0
        ).astype(jnp.float32)
        weight = jnp.take(valid, picks, axis=0).astype(jnp.float32) * area[None, None, :]
        kept = []
        for layer_id in range(layers):
            state, saved = layer_forward(
                state,
                sea,
                enc_low[layer_id],
                mid_low[layer_id],
                dec_low[layer_id],
                biases[layer_id],
                tabs,
            )
            kept.append(saved)
        diff = state - target
        loss = loss + jnp.sum(weight[..., None] * diff * diff)
        total = total + jnp.sum(weight)
        grad_state = 2.0 * weight[..., None] * diff
        for layer_id in reversed(range(layers)):
            grad_state, found = layer_backward(
                grad_state,
                sea,
                enc_low[layer_id],
                mid_low[layer_id],
                dec_low[layer_id],
                kept[layer_id],
                tabs,
            )
            sums = [acc.at[layer_id].add(part) for acc, part in zip(sums, found)]
    g_enc, g_mid, g_dec, g_vec, loss, total = lax.psum(
        (sums[0], sums[1], sums[2], sums[3], loss, total), ("lon", "lat")
    )
    return g_enc.reshape(w_enc.shape), g_mid, g_dec, g_vec, loss, total


def body(
    states,
    targets,
    sea_temp,
    ocean,
    valid,
    order,
    w_enc,
    w_mid,
    w_dec,
    biases,
    mom_enc,
    mom_mid,
    mom_dec,
    mom_bias,
    avg_enc,
    avg_mid,
    avg_dec,
    avg_bias,
):
    pool, lon_t, lat_t = states.shape[:3]
    lon_n, lat_n = lax.axis_size("lon"), lax.axis_size("lat")
    rate = RATE_BASE * math.sqrt(pool * lon_t * lon_n * lat_t * lat_n)
    if fits(states, w_mid, lon_n, lat_n):
        sums = fast_grads(states, targets, sea_temp, ocean, valid, w_enc, w_mid, w_dec, biases)
        arrays = (w_enc, w_mid, w_dec, biases, mom_enc, mom_mid, mom_dec, mom_bias)
        arrays += (avg_enc, avg_mid, avg_dec, avg_bias)
        return update_call(rate, sums, arrays)
    found = general_grads(
        states, targets, sea_temp, ocean, valid, order, w_enc, w_mid, w_dec, biases
    )
    loss, total = found[4:]
    grads = (found[0].reshape(w_enc.shape),) + found[1:4]
    news, moms, avgs, copies = ([], [], [], [])
    for weight_now, grad, mom, avg in zip(
        (w_enc, w_mid, w_dec, biases),
        grads,
        (mom_enc, mom_mid, mom_dec, mom_bias),
        (avg_enc, avg_mid, avg_dec, avg_bias),
    ):
        scaled = grad / total
        mom_new = MOMENTUM * mom + scaled
        fresh = weight_now - rate * (scaled + MOMENTUM * mom_new)
        news.append(fresh)
        moms.append(mom_new)
        avgs.append(AVERAGE * avg + (1.0 - AVERAGE) * fresh)
        copies.append(fresh.astype(jnp.bfloat16))
    return (
        loss,
        total,
        news[0],
        news[1],
        news[2],
        news[3],
        moms[0],
        moms[1],
        moms[2],
        moms[3],
        avgs[0],
        avgs[1],
        avgs[2],
        avgs[3],
        copies[0],
        copies[1],
        copies[2],
        copies[3],
    )


def solution(mesh):
    placed = (
        P(None, "lon", "lat", None),
        P(None, "lon", "lat", None),
        P(None, "lon", "lat"),
        P(None, "lon", "lat"),
        P(None, "lon", "lat"),
        P(),
        P(),
        P(),
        P(),
        P(),
        P(),
        P(),
        P(),
        P(),
        P(),
        P(),
        P(),
        P(),
    )
    return jax.shard_map(
        body,
        mesh=mesh,
        in_specs=placed,
        out_specs=(
            P(),
            P(),
            P(),
            P(),
            P(),
            P(),
            P(),
            P(),
            P(),
            P(),
            P(),
            P(),
            P(),
            P(),
            P(),
            P(),
            P(),
            P(),
        ),
        check_vma=False,
    )
```
